32 devices in a mesh: dp: 8 (over y, x, core), tensor: 4 (over z).
Axes of the slice: x: 2, y: 2, z: 4, core: 2. Of those that a mesh axis runs over, the one named last changes fastest.
Arguments:
- inputs: bfloat16 [16, 544, 1536], P('dp', 'tensor'), may hold values from -6 to 6
- context: bfloat16 [16, 130, 768], P('dp'), may hold values from -6 to 6
- lengths: int32 [16], P('dp'), may hold values from 257 to 513, as said below
- cotangent: bfloat16 [16, 544, 1536], P('dp', 'tensor'), may hold values from -6 to 6
- self_qkv: float32 [3, 1536, 1536], P(None, 'dp', 'tensor'), may hold values from -0.15625 to 0.15625
- self_out: float32 [1536, 1536], P('tensor', 'dp'), may hold values from -1 to 1
- cross_query: float32 [1536, 1536], P('dp', 'tensor'), may hold values from -0.15625 to 0.15625
- cross_context: float32 [2, 768, 1536], P(None, 'dp', 'tensor'), may hold values from -0.21875 to 0.21875
- cross_out: float32 [1536, 1536], P('tensor', 'dp'), may hold values from -1 to 1
- gate_up: float32 [2, 1536, 6144], P(None, 'dp', 'tensor'), may hold values from -0.15625 to 0.15625
- down_proj: float32 [6144, 1536], P('tensor', 'dp'), may hold values from -0.078125 to 0.078125
- norm_gains: float32 [3, 1536], replicated, may hold values from 0.5 to 1.5
Outputs:
- output: bfloat16 [16, 544, 1536], P('dp', 'tensor')
- grad_inputs: float32 [16, 544, 1536], P('dp', 'tensor')
- grad_context: float32 [16, 130, 768], P('dp')
- grad_self_qkv: float32 [3, 1536, 1536], P(None, 'dp', 'tensor')
- grad_self_out: float32 [1536, 1536], P('tensor', 'dp')
- grad_cross_query: float32 [1536, 1536], P('dp', 'tensor')
- grad_cross_context: float32 [2, 768, 1536], P(None, 'dp', 'tensor')
- grad_cross_out: float32 [1536, 1536], P('tensor', 'dp')
- grad_gate_up: float32 [2, 1536, 6144], P(None, 'dp', 'tensor')
- grad_down_proj: float32 [6144, 1536], P('tensor', 'dp')
- grad_norm_gains: float32 [3, 1536], P(None, 'dp')
The draws below stay inside these ranges and needn't reach their ends.
Inputs may be any that keep to these rules, and one draw needn't show every extreme that they name: `lengths`: each sequence has more than half of 513 valid positions, and some sequence has exactly 513.
All inputs are finite; a program needn't handle non-finite values.
Results may differ from the reference program's by a relative error of at most 0.025.
Values may be sent and summed in bfloat16 or wider, within the bound.
A program may use at most 256 MiB of HBM per device.

```python
import jax
import jax.numpy as jnp
from jax import lax

D = 1536
HEADS = 24
HD = 64
FF = 6144
CD = 768
CTOK = 130
MAXLEN = 513
PADLEN = 544
SEQS = 16


def draw_lengths(key, part):
    drawn = jax.random.randint(jax.random.fold_in(key, 11), (SEQS,), MAXLEN // 2 + 1, MAXLEN + 1, dtype=jnp.int32)
    longest = jax.random.randint(jax.random.fold_in(key, 12), (), 0, SEQS, dtype=jnp.int32)
    return jnp.where(jnp.arange(SEQS, dtype=jnp.int32) == longest, MAXLEN, drawn).astype(jnp.int32)


def level_of(key, shape, split, least, top_value):
    factor_of = 1.0
    for position, blocks in split:
        draws = jax.random.uniform(jax.random.fold_in(jax.random.fold_in(key, 6), position), (blocks,), jnp.float32, least / len(split), top_value / len(split))
        factor_of = factor_of * jnp.repeat(jnp.exp(draws), shape[position] // blocks).reshape((-1,) + (1,) * (len(shape) - 1 - position))
    return factor_of


def noise(key, shape, spread, reach, cuts=(), held_as=jnp.bfloat16):
    level = level_of(key, shape, cuts, -0.22, 0.18) if cuts else 1.0
    entries = jax.random.normal(key, shape, jnp.float32) * spread * level
    return jnp.minimum(jnp.maximum(entries, -reach), reach).astype(held_as)


def setup_inputs(seed: int = 0) -> dict:
    keys = jax.random.split(jax.random.key(seed), 13)
    return {
        "inputs": noise(keys[0], (SEQS, PADLEN, D), 1.0, 6.0, ((0, 8), (1, 4))),
        "context": noise(keys[1], (SEQS, CTOK, CD), 1.0, 6.0, ((0, 8),)),
        "lengths": draw_lengths(jax.random.fold_in(keys[12], 71), 0),
        "cotangent": noise(keys[3], (SEQS, PADLEN, D), 1.0, 6.0, ((0, 8), (1, 4))),
        "self_qkv": noise(keys[4], (3, D, D), D ** -0.5, 0.15625, ((1, 8), (2, 4)), jnp.float32),
        "self_out": noise(keys[5], (D, D), 32 ** -0.5, 1.0, ((0, 4), (1, 8)), jnp.float32),
        "cross_query": noise(keys[6], (D, D), D ** -0.5, 0.15625, ((0, 8), (1, 4)), jnp.float32),
        "cross_context": noise(keys[7], (2, CD, D), CD ** -0.5, 0.21875, ((1, 8), (2, 4)), jnp.float32),
        "cross_out": noise(keys[8], (D, D), 32 ** -0.5, 1.0, ((0, 4), (1, 8)), jnp.float32),
        "gate_up": noise(keys[9], (2, D, FF), D ** -0.5, 0.15625, ((1, 8), (2, 4)), jnp.float32),
        "down_proj": noise(keys[10], (FF, D), FF ** -0.5, 0.078125, ((0, 4), (1, 8)), jnp.float32),
        "norm_gains": jnp.clip(1.0 + 0.1 * jax.random.normal(keys[11], (3, D), jnp.float32), 0.5, 1.5),
    }


@jax.custom_vjp
def low(v):
    return lax.optimization_barrier(v.astype(jnp.bfloat16)).astype(jnp.float32)

@jax.custom_vjp
def low_back(v):
    return v

def low_keep(v):
    return (low(v), None)

def low_pass(kept, grad):
    return (grad,)

def back_keep(v):
    return (v, None)

def back_low(kept, grad):
    return (low(grad),)
low.defvjp(low_keep, low_pass)
low_back.defvjp(back_keep, back_low)

def layer_norm(stream, gain):
    centred = stream - lax.optimization_barrier(jnp.mean(stream, axis=-1, keepdims=True))
    inverse = lax.rsqrt(lax.optimization_barrier(jnp.mean(centred * centred, axis=-1, keepdims=True)) + 1e-05)
    return centred * inverse * gain

def matmul(left, right):
    return jnp.dot(left, right, precision=lax.Precision.HIGHEST)

def attend(queries, keys_in, values, key_valid):
    query_heads = queries.reshape(queries.shape[0], HEADS, HD)
    key_heads = keys_in.reshape(keys_in.shape[0], HEADS, HD)
    value_heads = values.reshape(values.shape[0], HEADS, HD)
    scores = jnp.einsum('qhd,khd->hqk', query_heads, key_heads, precision=lax.Precision.HIGHEST) * HD ** (-0.5)
    scores = low_back(jnp.where(key_valid[None, None, :], scores, -1000000000.0))
    probs = low(jax.nn.softmax(scores, axis=-1))
    mixed = jnp.einsum('hqk,khd->qhd', probs, value_heads, precision=lax.Precision.HIGHEST)
    return low_back(low(mixed.reshape(queries.shape[0], D)))

def block(stream, context, weights, norm_gains, key_valid):
    rounded = [low(matrix) for matrix in weights]
    self_qkv, self_out, cross_query, cross_context, cross_out, gate_up, down_proj = rounded
    row_keep = key_valid.astype(jnp.float32)[:, None]
    normed = low(layer_norm(stream, norm_gains[0]))
    parts = [low_back(low(matmul(normed, self_qkv[index]))) for index in range(3)]
    branch = low_back(matmul(attend(parts[0], parts[1], parts[2], key_valid), self_out))
    stream = stream + row_keep * branch
    normed = low(layer_norm(stream, norm_gains[1]))
    queries = low_back(low(matmul(normed, cross_query)))
    keys_in = low_back(low(matmul(context, cross_context[0])))
    values = low_back(low(matmul(context, cross_context[1])))
    every_key = jnp.ones((context.shape[0],), dtype=jnp.bool_)
    branch = low_back(matmul(attend(queries, keys_in, values, every_key), cross_out))
    stream = stream + row_keep * branch
    normed = low(layer_norm(stream, norm_gains[2]))
    gate = low_back(matmul(normed, gate_up[0]))
    upper = low_back(matmul(normed, gate_up[1]))
    hidden = low(jax.nn.silu(gate) * upper)
    branch = low_back(matmul(hidden, down_proj))
    stream = stream + row_keep * branch
    return row_keep * stream

def reference(inputs, context, lengths, cotangent, self_qkv, self_out, cross_query, cross_context, cross_out, gate_up, down_proj, norm_gains):
    weights = (self_qkv, self_out, cross_query, cross_context, cross_out, gate_up, down_proj)
    positions = jnp.arange(PADLEN, dtype=jnp.int32)

    def one_sequence(totals, item):
        stream, cond_rows, length, grad_out = item
        key_valid = positions < length

        def forward(stream_in, context_in, weight_set, gain_set):
            return block(stream_in, context_in, weight_set, gain_set, key_valid)
        result, pullback = jax.vjp(forward, stream.astype(jnp.float32), cond_rows.astype(jnp.float32), weights, norm_gains)
        grad_stream, grad_cond, grad_weights, grad_gains = pullback(grad_out.astype(jnp.float32))
        totals = jax.tree.map(lambda left, right: left + right, totals, (grad_weights, grad_gains))
        return (totals, (result.astype(jnp.bfloat16), grad_stream, grad_cond))
    zeros = jax.tree.map(jnp.zeros_like, (weights, norm_gains))
    totals, stacked = lax.scan(one_sequence, zeros, (inputs, context, lengths, cotangent))
    output, grad_inputs, grad_context = stacked
    grad_weights, grad_gains = totals
    return (output, grad_inputs, grad_context, grad_weights[0], grad_weights[1], grad_weights[2], grad_weights[3], grad_weights[4], grad_weights[5], grad_weights[6], grad_gains)
```

```python
import functools

import jax
import jax.numpy as jnp
from jax import lax
from jax.experimental import pallas as pl
from jax.experimental.pallas import tpu as pltpu
from jax.sharding import PartitionSpec as P

HD = 64


EPSILON = 1e-05
NEGATIVE = -1000000000.0


def norm_rows(stream, gain):
    centred = stream - jnp.mean(stream, axis=-1, keepdims=True)
    inverse = lax.rsqrt(jnp.mean(centred * centred, axis=-1, keepdims=True) + EPSILON)
    scaled = centred * inverse
    return (scaled * gain, scaled, inverse)


def norm_back(grad_out, scaled, inverse, gain):
    grad_scaled = grad_out * gain
    centre_part = jnp.mean(grad_scaled, axis=-1, keepdims=True)
    slope_part = jnp.mean(grad_scaled * scaled, axis=-1, keepdims=True)
    grad_in = inverse * (grad_scaled - centre_part - scaled * slope_part)
    return (grad_in, grad_out * scaled)


def split_heads(flat):
    return flat.reshape(flat.shape[0], flat.shape[1] // HD, HD)


def masked_scores(queries, keys_in, key_valid):
    scores = jnp.einsum(
        "qhd,khd->hqk", queries, keys_in, preferred_element_type=jnp.float32
    ) * HD ** (-0.5)
    return jnp.where(key_valid[None, None, :], scores, NEGATIVE)


def attend_forward(item):
    query_rows, key_rows, value_rows, key_valid = item
    scores = masked_scores(split_heads(query_rows), split_heads(key_rows), key_valid)
    peak_score = jnp.max(scores, axis=-1, keepdims=True)
    exponent = jnp.exp(scores - peak_score)
    denominator = jnp.sum(exponent, axis=-1, keepdims=True)
    probs = (exponent / denominator).astype(jnp.bfloat16)
    mixed = jnp.einsum(
        "hqk,khd->qhd", probs, split_heads(value_rows), preferred_element_type=jnp.float32
    )
    return (
        mixed.reshape(query_rows.shape).astype(jnp.bfloat16),
        (peak_score + jnp.log(denominator))[..., 0],
    )


def attend_backward(item):
    query_rows, key_rows, value_rows, logsum, grad_mixed, key_valid = item
    queries = split_heads(query_rows)
    keys_in = split_heads(key_rows)
    values = split_heads(value_rows)
    grads = split_heads(grad_mixed)
    probs = jnp.exp(masked_scores(queries, keys_in, key_valid) - logsum[..., None])
    grad_probs = jnp.einsum("qhd,khd->hqk", grads, values, preferred_element_type=jnp.float32)
    inner_sum = jnp.sum(probs * grad_probs, axis=-1, keepdims=True)
    grad_scores = (probs * (grad_probs - inner_sum)).astype(jnp.bfloat16)
    grad_values = jnp.einsum(
        "hqk,qhd->khd", probs.astype(jnp.bfloat16), grads, preferred_element_type=jnp.float32
    )
    grad_queries = jnp.einsum(
        "hqk,khd->qhd", grad_scores, keys_in, preferred_element_type=jnp.float32
    ) * HD ** (-0.5)
    grad_keys = jnp.einsum(
        "hqk,qhd->khd", grad_scores, queries, preferred_element_type=jnp.float32
    ) * HD ** (-0.5)
    return (
        grad_queries.reshape(query_rows.shape).astype(jnp.bfloat16),
        grad_keys.reshape(key_rows.shape).astype(jnp.bfloat16),
        grad_values.reshape(value_rows.shape).astype(jnp.bfloat16),
    )


def rows_whole(local_rows):
    return lax.all_gather(local_rows, "tensor", axis=1, tiled=True)


def rows_share(partial_value):
    return lax.psum_scatter(partial_value, "tensor", scatter_dimension=1, tiled=True)


def grad_whole(local_rows):
    return lax.all_gather(local_rows, "tensor", axis=1, tiled=True)


def grad_share(partial_value):
    return lax.psum_scatter(
        partial_value.astype(jnp.bfloat16), "tensor", scatter_dimension=1, tiled=True
    ).astype(jnp.float32)


def shards(
    inputs,
    context,
    lengths,
    cotangent,
    self_qkv,
    self_out,
    cross_query,
    cross_context,
    cross_out,
    gate_up,
    down_proj,
    norm_gains,
):
    seq_count, row_count, model_width = inputs.shape
    padded = row_count * lax.axis_size("tensor")
    tokens = seq_count * padded
    local_pos = lax.axis_index("tensor") * row_count + jnp.arange(row_count, dtype=jnp.int32)
    key_valid = jnp.arange(padded, dtype=jnp.int32)[None, :] < lengths[:, None]
    context_valid = jnp.ones((seq_count, context.shape[1]), dtype=jnp.bool_)
    row_keep = (local_pos[None, :] < lengths[:, None]).astype(jnp.float32)[:, :, None]
    (
        full_self_qkv,
        full_self_out,
        full_cross_query,
        full_cross_context,
        full_cross_out,
        full_gate_up,
        full_down,
    ) = (
        lax.all_gather(self_qkv.astype(jnp.bfloat16), "dp", axis=1, tiled=True),
        lax.all_gather(self_out.astype(jnp.bfloat16), "dp", axis=1, tiled=True),
        lax.all_gather(cross_query.astype(jnp.bfloat16), "dp", axis=0, tiled=True),
        lax.all_gather(cross_context.astype(jnp.bfloat16), "dp", axis=1, tiled=True),
        lax.all_gather(cross_out.astype(jnp.bfloat16), "dp", axis=1, tiled=True),
        lax.all_gather(gate_up.astype(jnp.bfloat16), "dp", axis=1, tiled=True),
        lax.all_gather(down_proj.astype(jnp.bfloat16), "dp", axis=1, tiled=True),
    )
    stream = inputs.astype(jnp.float32)
    normed, scaled_one, inverse_one = norm_rows(stream, norm_gains[0])
    whole_one = rows_whole(normed.astype(jnp.bfloat16)).reshape(tokens, model_width)
    qkv_rows = jnp.einsum(
        "td,cde->cte", whole_one, full_self_qkv, preferred_element_type=jnp.float32
    )
    qkv_rows = qkv_rows.astype(jnp.bfloat16).reshape(3, seq_count, padded, -1)
    mixed_one, logsum_one = lax.map(
        attend_forward, (qkv_rows[0], qkv_rows[1], qkv_rows[2], key_valid)
    )
    branch = jnp.dot(
        mixed_one.reshape(tokens, -1), full_self_out, preferred_element_type=jnp.float32
    )
    stream = stream + row_keep * rows_share(branch.reshape(seq_count, padded, model_width))
    normed, scaled_two, inverse_two = norm_rows(stream, norm_gains[1])
    whole_two = rows_whole(normed.astype(jnp.bfloat16)).reshape(tokens, model_width)
    cross_rows = jnp.dot(whole_two, full_cross_query, preferred_element_type=jnp.float32)
    cross_rows = cross_rows.astype(jnp.bfloat16).reshape(seq_count, padded, -1)
    context_rows = jnp.einsum(
        "scd,kde->ksce", context, full_cross_context, preferred_element_type=jnp.float32
    ).astype(jnp.bfloat16)
    mixed_two, logsum_two = lax.map(
        attend_forward, (cross_rows, context_rows[0], context_rows[1], context_valid)
    )
    branch = jnp.dot(
        mixed_two.reshape(tokens, -1), full_cross_out, preferred_element_type=jnp.float32
    )
    stream = stream + row_keep * rows_share(branch.reshape(seq_count, padded, model_width))
    normed, scaled_three, inverse_three = norm_rows(stream, norm_gains[2])
    whole_three = rows_whole(normed.astype(jnp.bfloat16)).reshape(tokens, model_width)
    gate_rows = jnp.einsum(
        "td,kdf->ktf", whole_three, full_gate_up, preferred_element_type=jnp.float32
    )
    sigmoid_gate = jax.nn.sigmoid(gate_rows[0])
    hidden = (gate_rows[0] * sigmoid_gate * gate_rows[1]).astype(jnp.bfloat16)
    branch = jnp.dot(hidden, full_down, preferred_element_type=jnp.float32)
    stream = stream + row_keep * rows_share(branch.reshape(seq_count, padded, model_width))
    output = (row_keep * stream).astype(jnp.bfloat16)
    (
        full_self_qkv,
        full_self_out,
        full_cross_query,
        full_cross_context,
        full_cross_out,
        full_gate_up,
        full_down,
    ) = (
        lax.all_gather(self_qkv.astype(jnp.bfloat16), "dp", axis=1, tiled=True),
        lax.all_gather(self_out.astype(jnp.bfloat16), "dp", axis=1, tiled=True),
        lax.all_gather(cross_query.astype(jnp.bfloat16), "dp", axis=0, tiled=True),
        lax.all_gather(cross_context.astype(jnp.bfloat16), "dp", axis=1, tiled=True),
        lax.all_gather(cross_out.astype(jnp.bfloat16), "dp", axis=1, tiled=True),
        lax.all_gather(gate_up.astype(jnp.bfloat16), "dp", axis=1, tiled=True),
        lax.all_gather(down_proj.astype(jnp.bfloat16), "dp", axis=1, tiled=True),
    )
    grad_stream = row_keep * cotangent.astype(jnp.float32)
    grad_branch = grad_whole((row_keep * grad_stream).astype(jnp.bfloat16)).reshape(
        tokens, model_width
    )
    grad_down = jnp.einsum("tf,td->fd", hidden, grad_branch, preferred_element_type=jnp.float32)
    grad_hidden = jnp.einsum(
        "td,fd->tf", grad_branch, full_down, preferred_element_type=jnp.float32
    )
    grad_gate = (
        grad_hidden * gate_rows[1] * sigmoid_gate * (1.0 + gate_rows[0] * (1.0 - sigmoid_gate))
    )
    grad_upper = grad_hidden * gate_rows[0] * sigmoid_gate
    grad_expand = jnp.stack([grad_gate, grad_upper]).astype(jnp.bfloat16)
    grad_gates = jnp.einsum(
        "td,ktf->kdf", whole_three, grad_expand, preferred_element_type=jnp.float32
    )
    partial_value = jnp.einsum(
        "ktf,kdf->td", grad_expand, full_gate_up, preferred_element_type=jnp.float32
    )
    grad_norm, gain_rows = norm_back(
        grad_share(partial_value.reshape(seq_count, padded, model_width)),
        scaled_three,
        inverse_three,
        norm_gains[2],
    )
    gain_three = jnp.sum(gain_rows, axis=(0, 1))
    grad_stream = grad_stream + grad_norm
    grad_branch = grad_whole((row_keep * grad_stream).astype(jnp.bfloat16)).reshape(
        tokens, model_width
    )
    grad_merge = jnp.einsum(
        "te,td->ed", mixed_two.reshape(tokens, -1), grad_branch, preferred_element_type=jnp.float32
    )
    grad_mixed = jnp.einsum(
        "td,ed->te", grad_branch, full_cross_out, preferred_element_type=jnp.float32
    )
    grad_mixed = grad_mixed.astype(jnp.bfloat16).reshape(seq_count, padded, -1)
    grad_query, grad_key, grad_value = lax.map(
        attend_backward,
        (cross_rows, context_rows[0], context_rows[1], logsum_two, grad_mixed, context_valid),
    )
    grad_cross = jnp.einsum(
        "td,te->de", whole_two, grad_query.reshape(tokens, -1), preferred_element_type=jnp.float32
    )
    grad_pairs = jnp.stack([grad_key, grad_value])
    grad_context_proj = jnp.einsum(
        "scd,ksce->kde", context, grad_pairs, preferred_element_type=jnp.float32
    )
    context_part = jnp.einsum(
        "ksce,kde->scd", grad_pairs, full_cross_context, preferred_element_type=jnp.float32
    )
    partial_value = jnp.einsum(
        "te,de->td",
        grad_query.reshape(tokens, -1),
        full_cross_query,
        preferred_element_type=jnp.float32,
    )
    grad_norm, gain_rows = norm_back(
        grad_share(partial_value.reshape(seq_count, padded, model_width)),
        scaled_two,
        inverse_two,
        norm_gains[1],
    )
    gain_two = jnp.sum(gain_rows, axis=(0, 1))
    grad_stream = grad_stream + grad_norm
    grad_branch = grad_whole((row_keep * grad_stream).astype(jnp.bfloat16)).reshape(
        tokens, model_width
    )
    grad_after = jnp.einsum(
        "te,td->ed", mixed_one.reshape(tokens, -1), grad_branch, preferred_element_type=jnp.float32
    )
    grad_mixed = jnp.einsum(
        "td,ed->te", grad_branch, full_self_out, preferred_element_type=jnp.float32
    )
    grad_mixed = grad_mixed.astype(jnp.bfloat16).reshape(seq_count, padded, -1)
    grad_query, grad_key, grad_value = lax.map(
        attend_backward, (qkv_rows[0], qkv_rows[1], qkv_rows[2], logsum_one, grad_mixed, key_valid)
    )
    grad_triple = jnp.stack([grad_query, grad_key, grad_value]).reshape(3, tokens, -1)
    grad_self = jnp.einsum(
        "td,cte->cde", whole_one, grad_triple, preferred_element_type=jnp.float32
    )
    partial_value = jnp.einsum(
        "cte,cde->td", grad_triple, full_self_qkv, preferred_element_type=jnp.float32
    )
    grad_norm, gain_rows = norm_back(
        grad_share(partial_value.reshape(seq_count, padded, model_width)),
        scaled_one,
        inverse_one,
        norm_gains[0],
    )
    gain_one = jnp.sum(gain_rows, axis=(0, 1))
    grad_inputs = grad_stream + grad_norm
    gain_partial = jnp.stack([gain_one, gain_two, gain_three])
    gain_total, grad_context = (
        lax.psum(gain_partial.astype(jnp.bfloat16), "tensor").astype(jnp.float32),
        lax.psum(context_part.astype(jnp.bfloat16), "tensor").astype(jnp.float32),
    )
    result_grads = (
        lax.psum_scatter(
            grad_self.astype(jnp.bfloat16), "dp", scatter_dimension=1, tiled=True
        ).astype(jnp.float32),
        lax.psum_scatter(
            grad_after.astype(jnp.bfloat16), "dp", scatter_dimension=1, tiled=True
        ).astype(jnp.float32),
        lax.psum_scatter(
            grad_cross.astype(jnp.bfloat16), "dp", scatter_dimension=0, tiled=True
        ).astype(jnp.float32),
        lax.psum_scatter(
            grad_context_proj.astype(jnp.bfloat16), "dp", scatter_dimension=1, tiled=True
        ).astype(jnp.float32),
        lax.psum_scatter(
            grad_merge.astype(jnp.bfloat16), "dp", scatter_dimension=1, tiled=True
        ).astype(jnp.float32),
        lax.psum_scatter(
            grad_gates.astype(jnp.bfloat16), "dp", scatter_dimension=1, tiled=True
        ).astype(jnp.float32),
        lax.psum_scatter(
            grad_down.astype(jnp.bfloat16), "dp", scatter_dimension=1, tiled=True
        ).astype(jnp.float32),
        lax.psum_scatter(
            gain_total.astype(jnp.bfloat16), "dp", scatter_dimension=1, tiled=True
        ).astype(jnp.float32),
    )
    return (
        output,
        grad_inputs,
        grad_context,
        result_grads[0],
        result_grads[1],
        result_grads[2],
        result_grads[3],
        result_grads[4],
        result_grads[5],
        result_grads[6],
        result_grads[7],
    )


CORE, XBIT, YBIT = 1, 2, 4
BF = jnp.bfloat16
F32 = jnp.float32


def swap(value, bit):
    count = lax.axis_size("dp")
    return lax.ppermute(value, "dp", [(i, i ^ bit) for i in range(count)])


def take(value, index, axis):
    return lax.dynamic_index_in_dim(value, index, axis, keepdims=False)


def ordered(place, mine, theirs, axis):
    low = jnp.where(place == 0, mine, theirs)
    high = jnp.where(place == 0, theirs, mine)
    return jnp.stack([low, high], axis)


def added(mine, theirs):
    return mine.astype(F32) + theirs.astype(F32)


def z_routes(turn):
    pairs = []
    for plane in range(4):
        for core in range(2):
            for z in range(4):
                picked = (z + turn) % 2
                source = (plane * 2 + core) * 4 + z
                target = (plane * 2 + z // 2) * 4 + 2 * core + picked
                pairs.append((source, target))
    return pairs


def rows_in(value, z):
    first = lax.ppermute(take(value, z % 2, 0), ("dp", "tensor"), z_routes(0))
    second = lax.ppermute(take(value, 1 - z % 2, 0), ("dp", "tensor"), z_routes(1))
    return ordered(z % 2, first, second, 0).reshape(-1, value.shape[-1])


def rows_out(half, z):
    blocks = half.reshape(2, -1, half.shape[-1])
    back = [[(b, a) for a, b in z_routes(turn)] for turn in range(2)]
    first = lax.ppermute(take(blocks, z % 2, 0), ("dp", "tensor"), back[0])
    second = lax.ppermute(take(blocks, 1 - z % 2, 0), ("dp", "tensor"), back[1])
    return ordered(z % 2, first, second, 0)


def plane_rows(half):
    cut = half.shape[0] // 2
    upper, lower = half[:cut], half[cut:]
    upper_x = swap(upper, XBIT)
    lower_y = swap(lower, YBIT)
    upper_two = swap(jnp.stack([upper, upper_x]), YBIT)
    lower_two = swap(jnp.stack([lower, lower_y]), XBIT)
    return jnp.concatenate(
        [upper, lower, upper_x, lower_two[0], upper_two[0], lower_y, upper_two[1], lower_two[1]]
    )


def plane_sums(partial_value):
    blocks = partial_value.astype(BF).reshape(4, 2, -1, partial_value.shape[-1])
    upper, lower = blocks[:, 0], blocks[:, 1]
    got = swap(jnp.stack([upper[1], upper[3]]), XBIT)
    upper_near, upper_far = added(upper[0], got[0]), added(upper[2], got[1])
    got = swap(jnp.stack([lower[2], lower[3]]), YBIT)
    lower_near, lower_far = added(lower[0], got[0]), added(lower[1], got[1])
    upper_sum = added(upper_near, swap(upper_far.astype(BF), YBIT))
    lower_sum = added(lower_near, swap(lower_far.astype(BF), XBIT))
    return jnp.concatenate([upper_sum, lower_sum])


def narrow_share(grads, place):
    core, xbit, ybit, z = place
    count, depth, width = grads.shape[0], grads.shape[1] // 8, grads.shape[2] // 2
    grid = grads.astype(BF).reshape(count, 2, 2, 2 * depth, 2 * width)
    left, right = grid[..., :width], grid[..., width:]
    left = added(take(left, xbit, 2), swap(take(left, 1 - xbit, 2), XBIT)).astype(BF)
    right = added(take(right, ybit, 1), swap(take(right, 1 - ybit, 1), YBIT)).astype(BF)
    left = added(take(left, ybit, 1), swap(take(left, 1 - ybit, 1), YBIT)).astype(BF)
    right = added(take(right, xbit, 1), swap(take(right, 1 - xbit, 1), XBIT)).astype(BF)
    both = jnp.stack([left, right]).reshape(2, count, 2, depth, width)
    mine = take(both, core, 2)
    theirs = swap(take(both, 1 - core, 2), CORE)
    parts = ordered(core, mine, theirs, 0).reshape(4, count, depth, width)
    return lax.psum_scatter(parts, "tensor", scatter_dimension=0, tiled=False)


def wide_share(grads, place):
    core, xbit, ybit, z = place
    count, depth, width = grads.shape[0], grads.shape[1] // 8, grads.shape[2]
    grid = grads.astype(BF).reshape(count, 2, 2, 2, depth, 4, width // 4)
    grid = added(take(grid, core, 3), swap(take(grid, 1 - core, 3), CORE)).astype(BF)
    grid = jnp.moveaxis(grid, 4, 0)
    grid = lax.psum_scatter(grid, "tensor", scatter_dimension=0, tiled=False)
    grid = ordered(ybit, take(grid, ybit, 1), swap(take(grid, 1 - ybit, 1), YBIT), 3)
    grid = ordered(xbit, take(grid, xbit, 1), swap(take(grid, 1 - xbit, 1), XBIT), 3)
    return grid.reshape(count, depth, width)


MESH = pl.DeviceIdType.MESH


def spot():
    dp, z = lax.axis_index("dp"), lax.axis_index("tensor")
    return dp, dp // 2, dp % 2, z


def greet(devices):
    barrier = pltpu.get_barrier_semaphore()
    for dp, z in devices:
        pl.semaphore_signal(
            barrier, inc=1, device_id={"dp": dp, "tensor": z}, device_id_type=MESH
        )
    pl.semaphore_wait(barrier, len(devices))


def flip(dp, bit):
    bits = {1: dp % 2, 2: dp // 2 % 2, 4: dp // 4 % 2}
    return dp + bit * (1 - 2 * bits[bit])


def plane_mates(dp, z):
    return [(flip(dp, 2), z), (flip(dp, 4), z), (flip(flip(dp, 2), 4), z)]


def column_mates(dp, z):
    mates = [(flip(dp, 1), z)]
    for step in range(1, 4):
        far = lax.rem(z + step, 4)
        mates += [(dp, far), (flip(dp, 1), far)]
    return mates


def push(source, target, send, recv, device):
    dp, z = device
    return pltpu.make_async_remote_copy(
        src_ref=source,
        dst_ref=target,
        send_sem=send,
        recv_sem=recv,
        device_id={"dp": dp, "tensor": z},
        device_id_type=MESH,
    )


def first_kernel(
    rows_ref, wide_ref, seq_ref, block_ref, send_a, recv_a, send_b, recv_b, send_c, recv_c, local
):
    dp, plane, core, z = spot()
    sibling = (flip(dp, 1), z)
    greet(plane_mates(dp, z) + column_mates(dp, z))
    home = z // 2 == core
    for s in range(2):
        stays = jnp.logical_and(home, z % 2 == s)

        @pl.when(jnp.logical_not(stays))
        def _(s=s):
            target = (plane * 2 + z // 2, 2 * core + s)
            push(rows_ref.at[s], seq_ref.at[z], send_a.at[s], recv_a.at[z % 2], target).start()

        @pl.when(stays)
        def _(s=s):
            pltpu.make_async_copy(rows_ref.at[s], seq_ref.at[z], local.at[0]).start()

    wide = []
    for slot, mate in enumerate(plane_mates(dp, z)):
        copy = push(
            wide_ref.at[:, mate[0] // 2],
            block_ref.at[:, plane],
            send_b.at[slot],
            recv_b.at[slot],
            mate,
        )
        copy.start()
        wide.append(copy)
    own = pltpu.make_async_copy(wide_ref.at[:, plane], block_ref.at[:, plane], local.at[1])
    own.start()
    for j in range(2):
        block = 2 * core + j
        stays = jnp.logical_and(home, block == z)

        @pl.when(stays)
        def _(block=block):
            pltpu.make_async_copy(rows_ref.at[0], seq_ref.at[block], local.at[0]).wait()

        @pl.when(jnp.logical_not(stays))
        def _(block=block, j=j):
            push(rows_ref.at[0], seq_ref.at[block], send_a.at[0], recv_a.at[j], sibling).wait_recv()

        push(seq_ref.at[block], seq_ref.at[block], send_c.at[j], recv_c.at[j], sibling).start()
    for j in range(2):
        mine, other = 2 * core + j, 2 * (1 - core) + j
        push(seq_ref.at[mine], seq_ref.at[mine], send_c.at[j], recv_c.at[j], sibling).wait_send()
        push(seq_ref.at[other], seq_ref.at[other], send_c.at[j], recv_c.at[j], sibling).wait_recv()
    for s in range(2):
        stays = jnp.logical_and(home, z % 2 == s)

        @pl.when(jnp.logical_not(stays))
        def _(s=s):
            push(rows_ref.at[s], seq_ref.at[z], send_a.at[s], recv_a.at[0], sibling).wait_send()

    for copy in wide:
        copy.wait()
    own.wait()


def any_specs(count):
    return [pl.BlockSpec(memory_space=pl.ANY)] * count


def near_specs(count):
    return [pl.BlockSpec(memory_space=pltpu.VMEM)] * count


ROOM = 56 << 20


def dma(*shape):
    return pltpu.SemaphoreType.DMA(shape)


def first_moves(rows, wide):
    _, height, width = rows.shape
    return pl.pallas_call(
        first_kernel,
        out_shape=[
            jax.ShapeDtypeStruct((4, height, width), BF),
            jax.ShapeDtypeStruct(wide.shape, BF),
        ],
        in_specs=near_specs(2),
        out_specs=any_specs(2),
        scratch_shapes=[dma(2), dma(2), dma(3), dma(3), dma(2), dma(2), dma(2)],
        compiler_params=pltpu.CompilerParams(
            collective_id=1, has_side_effects=True, vmem_limit_bytes=ROOM
        ),
        name="first_moves",
    )(rows, wide)


def narrow_kernel(shard_ref, whole_ref, send_s, recv_s, send_z, recv_z, send_p, recv_p, local, *, groups):
    dp, plane, core, z = spot()
    width = shard_ref.shape[2]
    sibling = (flip(dp, 1), z)
    xmate, ymate, far = plane_mates(dp, z)
    lines = [(dp, lax.rem(z + step, 4)) for step in range(1, 4)]
    greet([sibling, xmate, ymate] + lines)
    home = z // 2 == core
    above, below = (dp, z + 1), (dp, z - 1)

    def columns(which):
        return pl.ds(pl.multiple_of(which * width, width), width)

    for g, (low, count) in enumerate(groups):
        piece = shard_ref.at[pl.ds(low, count)]

        @pl.when(home)
        def _(g=g, low=low, count=count, piece=piece):
            spot_ref = whole_ref.at[pl.ds(low, count), plane, core, :, columns(z % 2)]
            pltpu.make_async_copy(piece, spot_ref, local.at[g]).start()

        @pl.when(jnp.logical_not(home))
        def _(g=g, low=low, count=count, piece=piece):
            spot_ref = whole_ref.at[pl.ds(low, count), plane, core, :, columns(z % 2)]
            push(piece, spot_ref, send_s.at[g], recv_s.at[g], sibling).start()

    near = jnp.where(core == 0, jnp.where(z >= 1, 1, 0), jnp.where(z <= 2, 0, 1))

    def area(g, which, chip):
        low, count = groups[g]
        return whole_ref.at[pl.ds(low, count), chip, :, :, columns(which)]

    def order(turn):
        return near if turn == 0 else 1 - near

    def on_z(g, turn, act):
        which = order(turn)
        source_z = 2 * core + which
        spot_ref = area(g, which, plane)
        for way, (wanted, target) in enumerate(
            [
                (jnp.logical_and(z >= source_z, z < 3), above),
                (jnp.logical_and(z <= source_z, z > 0), below),
            ]
        ):

            @pl.when(wanted)
            def _(way=way, target=target):
                act(push(spot_ref, spot_ref, send_z.at[g, which, way], recv_z.at[g, which], target))

    def arrive(g, turn):
        which = order(turn)
        source_z = 2 * core + which
        low, count = groups[g]

        @pl.when(z == source_z)
        def _():
            mine = whole_ref.at[pl.ds(low, count), plane, core, :, columns(which)]
            other = whole_ref.at[pl.ds(low, count), plane, 1 - core, :, columns(which)]
            pltpu.make_async_copy(shard_ref.at[pl.ds(low, count)], mine, local.at[g]).wait()
            push(mine, other, send_s.at[g], recv_s.at[g], sibling).wait_recv()

        @pl.when(z != source_z)
        def _():
            spot_ref = area(g, which, plane)
            push(spot_ref, spot_ref, send_z.at[g, which, 0], recv_z.at[g, which], sibling).wait_recv()

    def hop(g, turn, chip, slot, mate):
        spot_ref = area(g, order(turn), chip)
        return push(spot_ref, spot_ref, send_p.at[g, turn, slot], recv_p.at[g, turn, slot], mate)

    mates = (xmate, ymate)

    def spread(g, turn):
        arrive(g, turn)
        on_z(g, turn, lambda copy: copy.start())
        hop(g, turn, plane, turn, mates[turn]).start()
        hop(g, turn, plane, 1 - turn, mates[1 - turn]).start()

    def relay(g, turn):
        chip = mates[turn][0] // 2
        hop(g, turn, chip, turn, mates[turn]).wait_recv()
        hop(g, turn, chip, 2, mates[1 - turn]).start()

    count = len(groups)
    spread(0, 0)
    spread(0, 1)
    for g in range(count):
        relay(g, 0)
        if g + 1 < count:
            spread(g + 1, 0)
        relay(g, 1)
        if g + 1 < count:
            spread(g + 1, 1)
    for g in range(count):
        for turn in range(2):
            hop(g, turn, mates[1 - turn][0] // 2, 1 - turn, mates[1 - turn]).wait_recv()
            hop(g, turn, far[0] // 2, 2, mates[1 - turn]).wait_recv()
            for slot in range(3):
                hop(g, turn, plane, slot, xmate).wait_send()
            on_z(g, turn, lambda copy: copy.wait_send())
        low, size = groups[g]

        @pl.when(jnp.logical_not(home))
        def _(g=g, low=low, size=size):
            piece = shard_ref.at[pl.ds(low, size)]
            push(piece, piece, send_s.at[g], recv_s.at[g], sibling).wait_send()


def narrow_moves(shard, groups):
    count, depth, width = shard.shape
    parts = len(groups)
    whole = pl.pallas_call(
        functools.partial(narrow_kernel, groups=groups),
        out_shape=jax.ShapeDtypeStruct((count, 4, 2, depth, 2 * width), BF),
        in_specs=near_specs(1),
        out_specs=pl.BlockSpec(memory_space=pl.ANY),
        scratch_shapes=[
            dma(parts),
            dma(parts),
            dma(parts, 2, 2),
            dma(parts, 2),
            dma(parts, 2, 3),
            dma(parts, 2, 3),
            dma(parts),
        ],
        compiler_params=pltpu.CompilerParams(
            collective_id=2, has_side_effects=True, vmem_limit_bytes=ROOM
        ),
        name="narrow_moves",
    )(shard)
    return whole.reshape(count, 8 * depth, 2 * width)


def second_kernel(
    rows_ref, quarter_ref, all_ref, wide_ref, send_r, recv_r, send_w, recv_w, local, held, held_sem
):
    dp, plane, core, z = spot()
    sibling = (flip(dp, 1), z)
    xmate, ymate, far = plane_mates(dp, z)
    greet([sibling, xmate, ymate])
    width = quarter_ref.shape[4]

    def rows(source, chip, part, slot, mate):
        return push(source, all_ref.at[chip, part], send_r.at[slot], recv_r.at[slot], mate)

    own = [
        rows(rows_ref.at[0], 1, 0, 0, xmate),
        rows(rows_ref.at[1], 2, 1, 1, ymate),
        rows(rows_ref.at[0], 2, 0, 2, ymate),
        rows(rows_ref.at[1], 1, 1, 3, xmate),
    ]
    for copy in own:
        copy.start()
    wide, loads = [], []
    for block in range(4):
        columns = pl.ds(block * width, width)
        target = wide_ref.at[:, :, core, :, columns]
        loads.append(pltpu.make_async_copy(quarter_ref.at[block], held.at[block], held_sem.at[block]))
        wide.append(pltpu.make_async_copy(held.at[block], target, local.at[block]))
        wide.append(push(held.at[block], target, send_w.at[block], recv_w.at[block], sibling))
    for copy in loads:
        copy.start()
    keep = pltpu.make_async_copy(rows_ref, all_ref.at[0], local.at[4])
    keep.start()
    for block in range(4):
        loads[block].wait()
        wide[2 * block].start()
        wide[2 * block + 1].start()
    own[0].wait_recv()
    upper = rows(all_ref.at[1, 0], 3, 0, 4, ymate)
    upper.start()
    own[1].wait_recv()
    lower = rows(all_ref.at[2, 1], 3, 1, 5, xmate)
    lower.start()
    own[2].wait_recv()
    own[3].wait_recv()
    for copy in own:
        copy.wait_send()
    upper.wait()
    lower.wait()
    keep.wait()
    for block in range(4):
        columns = pl.ds(block * width, width)
        wide[2 * block].wait()
        wide[2 * block + 1].wait_send()
        theirs = wide_ref.at[:, :, 1 - core, :, columns]
        push(theirs, theirs, send_w.at[block], recv_w.at[block], sibling).wait_recv()


def second_moves(rows, quarter):
    blocks, count, chips, depth, width = quarter.shape
    return pl.pallas_call(
        second_kernel,
        out_shape=[
            jax.ShapeDtypeStruct((4, *rows.shape), BF),
            jax.ShapeDtypeStruct((count, chips, 2, depth, blocks * width), BF),
        ],
        in_specs=near_specs(1) + any_specs(1),
        out_specs=any_specs(2),
        scratch_shapes=[
            dma(6),
            dma(6),
            dma(4),
            dma(4),
            dma(5),
            pltpu.VMEM(quarter.shape, BF),
            dma(4),
        ],
        compiler_params=pltpu.CompilerParams(
            collective_id=3, has_side_effects=True, vmem_limit_bytes=ROOM
        ),
        name="second_moves",
    )(rows, quarter)


def chip_shards(
    inputs,
    context,
    lengths,
    cotangent,
    self_qkv,
    self_out,
    cross_query,
    cross_context,
    cross_out,
    gate_up,
    down_proj,
    norm_gains,
):
    dp, z = lax.axis_index("dp"), lax.axis_index("tensor")
    core, xbit, ybit = dp & 1, (dp >> 1) & 1, (dp >> 2) & 1
    place = (core, xbit, ybit, z)
    model_width = inputs.shape[-1]
    padded = inputs.shape[1] * 4
    half_rows = padded // 2

    def sibling_owned(value):
        mine = take(value, z % 2, 0)
        return jnp.where(core == z // 2, mine, swap(mine, CORE))

    def own_half(value):
        return take(value.reshape(2, half_rows, -1), core, 0)

    def both_halves(mine, theirs):
        return ordered(core, mine, theirs, 0).reshape(padded, -1)

    pair_sum = lambda value: value + swap(value.astype(BF), CORE).astype(F32)

    cc_depth = cross_context.shape[1]
    narrow = jnp.concatenate(
        [
            self_qkv,
            self_out.T[None],
            cross_query[None],
            cross_context.reshape(1, 2 * cc_depth, -1),
            cross_out.T[None],
        ]
    ).astype(BF)
    depth, units = gate_up.shape[1], gate_up.shape[2]
    wide = jnp.concatenate([gate_up, down_proj.T[None]]).astype(BF)
    wide = jnp.moveaxis(wide.reshape(3, depth, 4, units // 4), 2, 1)
    sequence, wide = first_moves(inputs, wide)
    quarter = lax.all_gather(wide, "tensor", axis=0)
    stream = sequence.reshape(padded, model_width).astype(F32)
    length = sibling_owned(lengths[:, None])[0]
    cond = sibling_owned(context)
    narrow_all = narrow_moves(narrow, ((0, 3), (3, 4)))
    qkv_whole, so_whole, cq_whole, co_whole = narrow_all[:3], narrow_all[3], narrow_all[4], narrow_all[6]
    cc_whole = narrow_all[5].reshape(8, 2, cc_depth, -1)
    cc_whole = jnp.moveaxis(cc_whole, 1, 0).reshape(2, 8 * cc_depth, -1)
    cot_half = rows_in(cotangent, z)
    cot = both_halves(cot_half, swap(cot_half, CORE)).astype(F32)

    positions = jnp.arange(padded, dtype=jnp.int32)
    key_valid = positions < length
    row_keep = key_valid.astype(F32)[:, None]
    keep_half = own_half(row_keep)
    context_valid = jnp.ones((cond.shape[0],), dtype=jnp.bool_)

    normed_one, scaled_one, inverse_one = norm_rows(stream, norm_gains[0])
    normed_one = normed_one.astype(BF)
    qkv = jnp.einsum("td,kde->kte", normed_one, qkv_whole, preferred_element_type=F32).astype(BF)
    mixed_one, logsum_one = attend_forward((qkv[0], qkv[1], qkv[2], key_valid))
    branch = jnp.einsum("te,de->td", mixed_one, so_whole, preferred_element_type=F32)
    stream = stream + row_keep * pair_sum(branch)
    normed_two, scaled_two, inverse_two = norm_rows(stream, norm_gains[1])
    normed_two = normed_two.astype(BF)
    cross_rows = jnp.einsum("td,de->te", normed_two, cq_whole, preferred_element_type=F32).astype(BF)
    cond_rows = jnp.einsum("sd,kde->kse", cond, cc_whole, preferred_element_type=F32).astype(BF)
    mixed_two, logsum_two = attend_forward((cross_rows, cond_rows[0], cond_rows[1], context_valid))
    branch = jnp.einsum("te,de->td", mixed_two, co_whole, preferred_element_type=F32)
    stream = stream + row_keep * pair_sum(branch)
    stream_half = own_half(stream)
    normed_three, scaled_three, inverse_three = norm_rows(stream_half, norm_gains[2])
    rows_three, wide_all = second_moves(
        normed_three.astype(BF).reshape(2, -1, model_width), quarter
    )
    rows_three = rows_three.reshape(-1, model_width)
    wide_all = wide_all.reshape(3, model_width, units)
    gu_whole, down_whole = wide_all[:2], wide_all[2]
    gate_rows = jnp.einsum("td,kde->kte", rows_three, gu_whole, preferred_element_type=F32)
    sigmoid_gate = jax.nn.sigmoid(gate_rows[0])
    hidden = (gate_rows[0] * sigmoid_gate * gate_rows[1]).astype(BF)

    grad_stream = row_keep * cot
    grad_branch = plane_rows((keep_half * own_half(grad_stream)).astype(BF))
    grad_hidden = jnp.einsum("td,df->tf", grad_branch, down_whole, preferred_element_type=F32)
    grad_gate = (
        grad_hidden * gate_rows[1] * sigmoid_gate * (1.0 + gate_rows[0] * (1.0 - sigmoid_gate))
    )
    grad_upper = grad_hidden * gate_rows[0] * sigmoid_gate
    grad_expand = jnp.stack([grad_gate, grad_upper]).astype(BF)
    partial_value = jnp.einsum("ktf,kdf->td", grad_expand, gu_whole, preferred_element_type=F32)
    grad_norm, gain_rows = norm_back(
        plane_sums(partial_value), scaled_three, inverse_three, norm_gains[2]
    )
    gain_three = jnp.sum(gain_rows, axis=0)
    branch = jnp.einsum("tf,df->td", hidden, down_whole, preferred_element_type=F32)
    stream_half = stream_half + keep_half * plane_sums(branch)
    output = rows_out((keep_half * stream_half).astype(BF), z)
    grad_down = jnp.einsum("td,tf->df", grad_branch, hidden, preferred_element_type=F32)
    grad_gates = jnp.einsum("td,ktf->kdf", rows_three, grad_expand, preferred_element_type=F32)
    grad_gates = wide_share(grad_gates, place)
    grad_down = wide_share(grad_down[None], place)[0]

    grad_stream = grad_stream + both_halves(grad_norm, swap(grad_norm.astype(BF), CORE).astype(F32))
    grad_branch = (row_keep * grad_stream).astype(BF)
    grad_mixed = jnp.einsum("td,de->te", grad_branch, co_whole, preferred_element_type=F32).astype(BF)
    grad_query, grad_key, grad_value = attend_backward(
        (cross_rows, cond_rows[0], cond_rows[1], logsum_two, grad_mixed, context_valid)
    )
    partial_value = jnp.einsum("te,de->td", grad_query, cq_whole, preferred_element_type=F32)
    grad_norm, gain_rows = norm_back(
        pair_sum(partial_value), scaled_two, inverse_two, norm_gains[1]
    )
    gain_two = 0.5 * jnp.sum(gain_rows, axis=0)
    grad_merge = jnp.einsum("td,te->de", grad_branch, mixed_two, preferred_element_type=F32)
    grad_cross = jnp.einsum("td,te->de", normed_two, grad_query, preferred_element_type=F32)
    grad_pairs = jnp.stack([grad_key, grad_value])
    grad_cc = jnp.einsum("sd,kse->kde", cond, grad_pairs, preferred_element_type=F32)
    grad_cc = jnp.moveaxis(grad_cc.reshape(2, 8, cc_depth, -1), 0, 1).reshape(model_width, -1)
    crossed = narrow_share(
        jnp.stack([grad_merge.astype(BF), grad_cross.astype(BF), grad_cc.astype(BF)]), place
    )
    context_part = jnp.einsum("kse,kde->sd", grad_pairs, cc_whole, preferred_element_type=F32)
    context_all = lax.all_gather(pair_sum(context_part).astype(BF), "tensor", axis=0)
    grad_context = take(context_all.reshape(2, 2, *context_part.shape), core, 0).astype(F32)

    grad_stream = grad_stream + grad_norm
    grad_branch = (row_keep * grad_stream).astype(BF)
    grad_mixed = jnp.einsum("td,de->te", grad_branch, so_whole, preferred_element_type=F32).astype(BF)
    grad_after = jnp.einsum("td,te->de", grad_branch, mixed_one, preferred_element_type=F32)
    after = narrow_share(grad_after.astype(BF)[None], place)[0]
    grad_triple = jnp.stack(
        attend_backward((qkv[0], qkv[1], qkv[2], logsum_one, grad_mixed, key_valid))
    )
    grad_self = jnp.einsum("td,kte->kde", normed_one, grad_triple, preferred_element_type=F32)
    selfed = narrow_share(grad_self, place)
    partial_value = jnp.einsum("kte,kde->td", grad_triple, qkv_whole, preferred_element_type=F32)
    grad_norm, gain_rows = norm_back(
        pair_sum(partial_value), scaled_one, inverse_one, norm_gains[0]
    )
    gain_one = 0.5 * jnp.sum(gain_rows, axis=0)
    grad_inputs = rows_out(own_half(grad_stream + grad_norm).astype(BF), z).astype(F32)
    gains = lax.psum(jnp.stack([gain_one, gain_two, gain_three]), ("dp", "tensor"))
    gains = lax.dynamic_slice_in_dim(gains, dp * (model_width // 8), model_width // 8, 1)
    return (
        output,
        grad_inputs,
        grad_context,
        selfed.astype(F32),
        after.T.astype(F32),
        crossed[1].astype(F32),
        crossed[2].reshape(2, cc_depth, -1).astype(F32),
        crossed[0].T.astype(F32),
        grad_gates.astype(F32),
        grad_down.T.astype(F32),
        gains,
    )


def solution(mesh):
    sizes = (mesh.shape["dp"], mesh.shape["tensor"])
    body = chip_shards if sizes == (8, 4) else shards
    placed = (
        P("dp", "tensor", None),
        P("dp", None, None),
        P("dp"),
        P("dp", "tensor", None),
        P(None, "dp", "tensor"),
        P("tensor", "dp"),
        P("dp", "tensor"),
        P(None, "dp", "tensor"),
        P("tensor", "dp"),
        P(None, "dp", "tensor"),
        P("tensor", "dp"),
        P(),
    )
    return jax.shard_map(
        body,
        mesh=mesh,
        in_specs=placed,
        out_specs=(
            P("dp", "tensor", None),
            P("dp", "tensor", None),
            P("dp", None, None),
            P(None, "dp", "tensor"),
            P("tensor", "dp"),
            P("dp", "tensor"),
            P(None, "dp", "tensor"),
            P("tensor", "dp"),
            P(None, "dp", "tensor"),
            P("tensor", "dp"),
            P(None, "dp"),
        ),
        check_vma=False,
    )
```

```python
import functools

import jax
import jax.numpy as jnp
from jax import lax
from jax.experimental import pallas as pl
from jax.experimental.pallas import tpu as pltpu
from jax.sharding import PartitionSpec as P

HD = 64


EPSILON = 1e-05
NEGATIVE = -1000000000.0


def norm_rows(stream, gain):
    centred = stream - jnp.mean(stream, axis=-1, keepdims=True)
    inverse = lax.rsqrt(jnp.mean(centred * centred, axis=-1, keepdims=True) + EPSILON)
    scaled = centred * inverse
    return (scaled * gain, scaled, inverse)


def norm_back(grad_out, scaled, inverse, gain):
    grad_scaled = grad_out * gain
    centre_part = jnp.mean(grad_scaled, axis=-1, keepdims=True)
    slope_part = jnp.mean(grad_scaled * scaled, axis=-1, keepdims=True)
    grad_in = inverse * (grad_scaled - centre_part - scaled * slope_part)
    return (grad_in, grad_out * scaled)


def split_heads(flat):
    return flat.reshape(flat.shape[0], flat.shape[1] // HD, HD)


def masked_scores(queries, keys_in, key_valid):
    scores = jnp.einsum(
        "qhd,khd->hqk", queries, keys_in, preferred_element_type=jnp.float32
    ) * HD ** (-0.5)
    return jnp.where(key_valid[None, None, :], scores, NEGATIVE)


def attend_forward(item):
    query_rows, key_rows, value_rows, key_valid = item
    scores = masked_scores(split_heads(query_rows), split_heads(key_rows), key_valid)
    peak_score = jnp.max(scores, axis=-1, keepdims=True)
    exponent = jnp.exp(scores - peak_score)
    denominator = jnp.sum(exponent, axis=-1, keepdims=True)
    probs = (exponent / denominator).astype(jnp.bfloat16)
    mixed = jnp.einsum(
        "hqk,khd->qhd", probs, split_heads(value_rows), preferred_element_type=jnp.float32
    )
    return (
        mixed.reshape(query_rows.shape).astype(jnp.bfloat16),
        (peak_score + jnp.log(denominator))[..., 0],
    )


def attend_backward(item):
    query_rows, key_rows, value_rows, logsum, grad_mixed, key_valid = item
    queries = split_heads(query_rows)
    keys_in = split_heads(key_rows)
    values = split_heads(value_rows)
    grads = split_heads(grad_mixed)
    probs = jnp.exp(masked_scores(queries, keys_in, key_valid) - logsum[..., None])
    grad_probs = jnp.einsum("qhd,khd->hqk", grads, values, preferred_element_type=jnp.float32)
    inner_sum = jnp.sum(probs * grad_probs, axis=-1, keepdims=True)
    grad_scores = (probs * (grad_probs - inner_sum)).astype(jnp.bfloat16)
    grad_values = jnp.einsum(
        "hqk,qhd->khd", probs.astype(jnp.bfloat16), grads, preferred_element_type=jnp.float32
    )
    grad_queries = jnp.einsum(
        "hqk,khd->qhd", grad_scores, keys_in, preferred_element_type=jnp.float32
    ) * HD ** (-0.5)
    grad_keys = jnp.einsum(
        "hqk,qhd->khd", grad_scores, queries, preferred_element_type=jnp.float32
    ) * HD ** (-0.5)
    return (
        grad_queries.reshape(query_rows.shape).astype(jnp.bfloat16),
        grad_keys.reshape(key_rows.shape).astype(jnp.bfloat16),
        grad_values.reshape(value_rows.shape).astype(jnp.bfloat16),
    )


def rows_whole(local_rows):
    return lax.all_gather(local_rows, "tensor", axis=1, tiled=True)


def rows_share(partial_value):
    return lax.psum_scatter(partial_value, "tensor", scatter_dimension=1, tiled=True)


def grad_whole(local_rows):
    return lax.all_gather(local_rows, "tensor", axis=1, tiled=True)


def grad_share(partial_value):
    return lax.psum_scatter(
        partial_value.astype(jnp.bfloat16), "tensor", scatter_dimension=1, tiled=True
    ).astype(jnp.float32)


def shards(
    inputs,
    context,
    lengths,
    cotangent,
    self_qkv,
    self_out,
    cross_query,
    cross_context,
    cross_out,
    gate_up,
    down_proj,
    norm_gains,
):
    seq_count, row_count, model_width = inputs.shape
    padded = row_count * lax.axis_size("tensor")
    tokens = seq_count * padded
    local_pos = lax.axis_index("tensor") * row_count + jnp.arange(row_count, dtype=jnp.int32)
    key_valid = jnp.arange(padded, dtype=jnp.int32)[None, :] < lengths[:, None]
    context_valid = jnp.ones((seq_count, context.shape[1]), dtype=jnp.bool_)
    row_keep = (local_pos[None, :] < lengths[:, None]).astype(jnp.float32)[:, :, None]
    (
        full_self_qkv,
        full_self_out,
        full_cross_query,
        full_cross_context,
        full_cross_out,
        full_gate_up,
        full_down,
    ) = (
        lax.all_gather(self_qkv.astype(jnp.bfloat16), "dp", axis=1, tiled=True),
        lax.all_gather(self_out.astype(jnp.bfloat16), "dp", axis=1, tiled=True),
        lax.all_gather(cross_query.astype(jnp.bfloat16), "dp", axis=0, tiled=True),
        lax.all_gather(cross_context.astype(jnp.bfloat16), "dp", axis=1, tiled=True),
        lax.all_gather(cross_out.astype(jnp.bfloat16), "dp", axis=1, tiled=True),
        lax.all_gather(gate_up.astype(jnp.bfloat16), "dp", axis=1, tiled=True),
        lax.all_gather(down_proj.astype(jnp.bfloat16), "dp", axis=1, tiled=True),
    )
    stream = inputs.astype(jnp.float32)
    normed, scaled_one, inverse_one = norm_rows(stream, norm_gains[0])
    whole_one = rows_whole(normed.astype(jnp.bfloat16)).reshape(tokens, model_width)
    qkv_rows = jnp.einsum(
        "td,cde->cte", whole_one, full_self_qkv, preferred_element_type=jnp.float32
    )
    qkv_rows = qkv_rows.astype(jnp.bfloat16).reshape(3, seq_count, padded, -1)
    mixed_one, logsum_one = lax.map(
        attend_forward, (qkv_rows[0], qkv_rows[1], qkv_rows[2], key_valid)
    )
    branch = jnp.dot(
        mixed_one.reshape(tokens, -1), full_self_out, preferred_element_type=jnp.float32
    )
    stream = stream + row_keep * rows_share(branch.reshape(seq_count, padded, model_width))
    normed, scaled_two, inverse_two = norm_rows(stream, norm_gains[1])
    whole_two = rows_whole(normed.astype(jnp.bfloat16)).reshape(tokens, model_width)
    cross_rows = jnp.dot(whole_two, full_cross_query, preferred_element_type=jnp.float32)
    cross_rows = cross_rows.astype(jnp.bfloat16).reshape(seq_count, padded, -1)
    context_rows = jnp.einsum(
        "scd,kde->ksce", context, full_cross_context, preferred_element_type=jnp.float32
    ).astype(jnp.bfloat16)
    mixed_two, logsum_two = lax.map(
        attend_forward, (cross_rows, context_rows[0], context_rows[1], context_valid)
    )
    branch = jnp.dot(
        mixed_two.reshape(tokens, -1), full_cross_out, preferred_element_type=jnp.float32
    )
    stream = stream + row_keep * rows_share(branch.reshape(seq_count, padded, model_width))
    normed, scaled_three, inverse_three = norm_rows(stream, norm_gains[2])
    whole_three = rows_whole(normed.astype(jnp.bfloat16)).reshape(tokens, model_width)
    gate_rows = jnp.einsum(
        "td,kdf->ktf", whole_three, full_gate_up, preferred_element_type=jnp.float32
    )
    sigmoid_gate = jax.nn.sigmoid(gate_rows[0])
    hidden = (gate_rows[0] * sigmoid_gate * gate_rows[1]).astype(jnp.bfloat16)
    branch = jnp.dot(hidden, full_down, preferred_element_type=jnp.float32)
    stream = stream + row_keep * rows_share(branch.reshape(seq_count, padded, model_width))
    output = (row_keep * stream).astype(jnp.bfloat16)
    (
        full_self_qkv,
        full_self_out,
        full_cross_query,
        full_cross_context,
        full_cross_out,
        full_gate_up,
        full_down,
    ) = (
        lax.all_gather(self_qkv.astype(jnp.bfloat16), "dp", axis=1, tiled=True),
        lax.all_gather(self_out.astype(jnp.bfloat16), "dp", axis=1, tiled=True),
        lax.all_gather(cross_query.astype(jnp.bfloat16), "dp", axis=0, tiled=True),
        lax.all_gather(cross_context.astype(jnp.bfloat16), "dp", axis=1, tiled=True),
        lax.all_gather(cross_out.astype(jnp.bfloat16), "dp", axis=1, tiled=True),
        lax.all_gather(gate_up.astype(jnp.bfloat16), "dp", axis=1, tiled=True),
        lax.all_gather(down_proj.astype(jnp.bfloat16), "dp", axis=1, tiled=True),
    )
    grad_stream = row_keep * cotangent.astype(jnp.float32)
    grad_branch = grad_whole((row_keep * grad_stream).astype(jnp.bfloat16)).reshape(
        tokens, model_width
    )
    grad_down = jnp.einsum("tf,td->fd", hidden, grad_branch, preferred_element_type=jnp.float32)
    grad_hidden = jnp.einsum(
        "td,fd->tf", grad_branch, full_down, preferred_element_type=jnp.float32
    )
    grad_gate = (
        grad_hidden * gate_rows[1] * sigmoid_gate * (1.0 + gate_rows[0] * (1.0 - sigmoid_gate))
    )
    grad_upper = grad_hidden * gate_rows[0] * sigmoid_gate
    grad_expand = jnp.stack([grad_gate, grad_upper]).astype(jnp.bfloat16)
    grad_gates = jnp.einsum(
        "td,ktf->kdf", whole_three, grad_expand, preferred_element_type=jnp.float32
    )
    partial_value = jnp.einsum(
        "ktf,kdf->td", grad_expand, full_gate_up, preferred_element_type=jnp.float32
    )
    grad_norm, gain_rows = norm_back(
        grad_share(partial_value.reshape(seq_count, padded, model_width)),
        scaled_three,
        inverse_three,
        norm_gains[2],
    )
    gain_three = jnp.sum(gain_rows, axis=(0, 1))
    grad_stream = grad_stream + grad_norm
    grad_branch = grad_whole((row_keep * grad_stream).astype(jnp.bfloat16)).reshape(
        tokens, model_width
    )
    grad_merge = jnp.einsum(
        "te,td->ed", mixed_two.reshape(tokens, -1), grad_branch, preferred_element_type=jnp.float32
    )
    grad_mixed = jnp.einsum(
        "td,ed->te", grad_branch, full_cross_out, preferred_element_type=jnp.float32
    )
    grad_mixed = grad_mixed.astype(jnp.bfloat16).reshape(seq_count, padded, -1)
    grad_query, grad_key, grad_value = lax.map(
        attend_backward,
        (cross_rows, context_rows[0], context_rows[1], logsum_two, grad_mixed, context_valid),
    )
    grad_cross = jnp.einsum(
        "td,te->de", whole_two, grad_query.reshape(tokens, -1), preferred_element_type=jnp.float32
    )
    grad_pairs = jnp.stack([grad_key, grad_value])
    grad_context_proj = jnp.einsum(
        "scd,ksce->kde", context, grad_pairs, preferred_element_type=jnp.float32
    )
    context_part = jnp.einsum(
        "ksce,kde->scd", grad_pairs, full_cross_context, preferred_element_type=jnp.float32
    )
    partial_value = jnp.einsum(
        "te,de->td",
        grad_query.reshape(tokens, -1),
        full_cross_query,
        preferred_element_type=jnp.float32,
    )
    grad_norm, gain_rows = norm_back(
        grad_share(partial_value.reshape(seq_count, padded, model_width)),
        scaled_two,
        inverse_two,
        norm_gains[1],
    )
    gain_two = jnp.sum(gain_rows, axis=(0, 1))
    grad_stream = grad_stream + grad_norm
    grad_branch = grad_whole((row_keep * grad_stream).astype(jnp.bfloat16)).reshape(
        tokens, model_width
    )
    grad_after = jnp.einsum(
        "te,td->ed", mixed_one.reshape(tokens, -1), grad_branch, preferred_element_type=jnp.float32
    )
    grad_mixed = jnp.einsum(
        "td,ed->te", grad_branch, full_self_out, preferred_element_type=jnp.float32
    )
    grad_mixed = grad_mixed.astype(jnp.bfloat16).reshape(seq_count, padded, -1)
    grad_query, grad_key, grad_value = lax.map(
        attend_backward, (qkv_rows[0], qkv_rows[1], qkv_rows[2], logsum_one, grad_mixed, key_valid)
    )
    grad_triple = jnp.stack([grad_query, grad_key, grad_value]).reshape(3, tokens, -1)
    grad_self = jnp.einsum(
        "td,cte->cde", whole_one, grad_triple, preferred_element_type=jnp.float32
    )
    partial_value = jnp.einsum(
        "cte,cde->td", grad_triple, full_self_qkv, preferred_element_type=jnp.float32
    )
    grad_norm, gain_rows = norm_back(
        grad_share(partial_value.reshape(seq_count, padded, model_width)),
        scaled_one,
        inverse_one,
        norm_gains[0],
    )
    gain_one = jnp.sum(gain_rows, axis=(0, 1))
    grad_inputs = grad_stream + grad_norm
    gain_partial = jnp.stack([gain_one, gain_two, gain_three])
    gain_total, grad_context = (
        lax.psum(gain_partial.astype(jnp.bfloat16), "tensor").astype(jnp.float32),
        lax.psum(context_part.astype(jnp.bfloat16), "tensor").astype(jnp.float32),
    )
    result_grads = (
        lax.psum_scatter(
            grad_self.astype(jnp.bfloat16), "dp", scatter_dimension=1, tiled=True
        ).astype(jnp.float32),
        lax.psum_scatter(
            grad_after.astype(jnp.bfloat16), "dp", scatter_dimension=1, tiled=True
        ).astype(jnp.float32),
        lax.psum_scatter(
            grad_cross.astype(jnp.bfloat16), "dp", scatter_dimension=0, tiled=True
        ).astype(jnp.float32),
        lax.psum_scatter(
            grad_context_proj.astype(jnp.bfloat16), "dp", scatter_dimension=1, tiled=True
        ).astype(jnp.float32),
        lax.psum_scatter(
            grad_merge.astype(jnp.bfloat16), "dp", scatter_dimension=1, tiled=True
        ).astype(jnp.float32),
        lax.psum_scatter(
            grad_gates.astype(jnp.bfloat16), "dp", scatter_dimension=1, tiled=True
        ).astype(jnp.float32),
        lax.psum_scatter(
            grad_down.astype(jnp.bfloat16), "dp", scatter_dimension=1, tiled=True
        ).astype(jnp.float32),
        lax.psum_scatter(
            gain_total.astype(jnp.bfloat16), "dp", scatter_dimension=1, tiled=True
        ).astype(jnp.float32),
    )
    return (
        output,
        grad_inputs,
        grad_context,
        result_grads[0],
        result_grads[1],
        result_grads[2],
        result_grads[3],
        result_grads[4],
        result_grads[5],
        result_grads[6],
        result_grads[7],
    )


CORE, XBIT, YBIT = 1, 2, 4
BF = jnp.bfloat16
F32 = jnp.float32


def swap(value, bit):
    count = lax.axis_size("dp")
    return lax.ppermute(value, "dp", [(i, i ^ bit) for i in range(count)])


def take(value, index, axis):
    return lax.dynamic_index_in_dim(value, index, axis, keepdims=False)


def ordered(place, mine, theirs, axis):
    low = jnp.where(place == 0, mine, theirs)
    high = jnp.where(place == 0, theirs, mine)
    return jnp.stack([low, high], axis)


def added(mine, theirs):
    return mine.astype(F32) + theirs.astype(F32)


def z_routes(turn):
    pairs = []
    for plane in range(4):
        for core in range(2):
            for z in range(4):
                picked = (z + turn) % 2
                source = (plane * 2 + core) * 4 + z
                target = (plane * 2 + z // 2) * 4 + 2 * core + picked
                pairs.append((source, target))
    return pairs


def rows_in(value, z):
    first = lax.ppermute(take(value, z % 2, 0), ("dp", "tensor"), z_routes(0))
    second = lax.ppermute(take(value, 1 - z % 2, 0), ("dp", "tensor"), z_routes(1))
    return ordered(z % 2, first, second, 0).reshape(-1, value.shape[-1])


def plane_rows(half):
    cut = half.shape[0] // 2
    upper, lower = half[:cut], half[cut:]
    upper_x = swap(upper, XBIT)
    lower_y = swap(lower, YBIT)
    upper_two = swap(jnp.stack([upper, upper_x]), YBIT)
    lower_two = swap(jnp.stack([lower, lower_y]), XBIT)
    return jnp.concatenate(
        [upper, lower, upper_x, lower_two[0], upper_two[0], lower_y, upper_two[1], lower_two[1]]
    )


def plane_sums(partial_value):
    blocks = partial_value.astype(BF).reshape(4, 2, -1, partial_value.shape[-1])
    upper, lower = blocks[:, 0], blocks[:, 1]
    got = swap(jnp.stack([upper[1], upper[3]]), XBIT)
    upper_near, upper_far = added(upper[0], got[0]), added(upper[2], got[1])
    got = swap(jnp.stack([lower[2], lower[3]]), YBIT)
    lower_near, lower_far = added(lower[0], got[0]), added(lower[1], got[1])
    upper_sum = added(upper_near, swap(upper_far.astype(BF), YBIT))
    lower_sum = added(lower_near, swap(lower_far.astype(BF), XBIT))
    return jnp.concatenate([upper_sum, lower_sum])


MESH = pl.DeviceIdType.MESH


def spot():
    dp, z = lax.axis_index("dp"), lax.axis_index("tensor")
    return dp, dp // 2, dp % 2, z


def greet(devices):
    barrier = pltpu.get_barrier_semaphore()
    for dp, z in devices:
        pl.semaphore_signal(
            barrier, inc=1, device_id={"dp": dp, "tensor": z}, device_id_type=MESH
        )
    pl.semaphore_wait(barrier, len(devices))


def flip(dp, bit):
    bits = {1: dp % 2, 2: dp // 2 % 2, 4: dp // 4 % 2}
    return dp + bit * (1 - 2 * bits[bit])


def plane_mates(dp, z):
    return [(flip(dp, 2), z), (flip(dp, 4), z), (flip(flip(dp, 2), 4), z)]


def column_mates(dp, z):
    mates = [(flip(dp, 1), z)]
    for step in range(1, 4):
        far = lax.rem(z + step, 4)
        mates += [(dp, far), (flip(dp, 1), far)]
    return mates


def push(source, target, send, recv, device):
    dp, z = device
    return pltpu.make_async_remote_copy(
        src_ref=source,
        dst_ref=target,
        send_sem=send,
        recv_sem=recv,
        device_id={"dp": dp, "tensor": z},
        device_id_type=MESH,
    )


def first_kernel(
    rows_ref,
    wide_ref,
    cond_ref,
    size_ref,
    seq_ref,
    block_ref,
    cond_both,
    size_both,
    send_a,
    recv_a,
    send_b,
    recv_b,
    send_c,
    recv_c,
    send_d,
    recv_d,
    local,
):
    dp, plane, core, z = spot()
    sibling = (flip(dp, 1), z)
    greet(plane_mates(dp, z) + column_mates(dp, z))
    home = z // 2 == core
    for s in range(2):
        stays = jnp.logical_and(home, z % 2 == s)

        @pl.when(jnp.logical_not(stays))
        def _(s=s):
            target = (plane * 2 + z // 2, 2 * core + s)
            push(rows_ref.at[s], seq_ref.at[z], send_a.at[s], recv_a.at[z % 2], target).start()

        @pl.when(stays)
        def _(s=s):
            pltpu.make_async_copy(rows_ref.at[s], seq_ref.at[z], local.at[0]).start()

    wide = []
    for slot, mate in enumerate(plane_mates(dp, z)):
        copy = push(
            wide_ref.at[:, mate[0] // 2],
            block_ref.at[:, plane],
            send_b.at[slot],
            recv_b.at[slot],
            mate,
        )
        copy.start()
        wide.append(copy)
    own = pltpu.make_async_copy(wide_ref.at[:, plane], block_ref.at[:, plane], local.at[1])
    own.start()
    small = []
    for slot, (source, target) in enumerate([(cond_ref, cond_both), (size_ref, size_both)]):
        copy = push(source, target.at[core], send_d.at[slot], recv_d.at[slot], sibling)
        copy.start()
        keep = pltpu.make_async_copy(source, target.at[core], local.at[2 + slot])
        keep.start()
        small.append((copy, keep, slot, target))
    for j in range(2):
        block = 2 * core + j
        stays = jnp.logical_and(home, block == z)

        @pl.when(stays)
        def _(block=block):
            pltpu.make_async_copy(rows_ref.at[0], seq_ref.at[block], local.at[0]).wait()

        @pl.when(jnp.logical_not(stays))
        def _(block=block, j=j):
            push(rows_ref.at[0], seq_ref.at[block], send_a.at[0], recv_a.at[j], sibling).wait_recv()

        push(seq_ref.at[block], seq_ref.at[block], send_c.at[j], recv_c.at[j], sibling).start()
    for j in range(2):
        mine, other = 2 * core + j, 2 * (1 - core) + j
        push(seq_ref.at[mine], seq_ref.at[mine], send_c.at[j], recv_c.at[j], sibling).wait_send()
        push(seq_ref.at[other], seq_ref.at[other], send_c.at[j], recv_c.at[j], sibling).wait_recv()
    for s in range(2):
        stays = jnp.logical_and(home, z % 2 == s)

        @pl.when(jnp.logical_not(stays))
        def _(s=s):
            push(rows_ref.at[s], seq_ref.at[z], send_a.at[s], recv_a.at[0], sibling).wait_send()

    for copy in wide:
        copy.wait()
    own.wait()
    for copy, keep, slot, target in small:
        keep.wait()
        copy.wait_send()
        theirs = target.at[1 - core]
        push(theirs, theirs, send_d.at[slot], recv_d.at[slot], sibling).wait_recv()


def any_specs(count):
    return [pl.BlockSpec(memory_space=pl.ANY)] * count


def near_specs(count):
    return [pl.BlockSpec(memory_space=pltpu.VMEM)] * count


ROOM = 56 << 20


def dma(*shape):
    return pltpu.SemaphoreType.DMA(shape)


def first_moves(rows, wide, cond, size):
    _, height, width = rows.shape
    return pl.pallas_call(
        first_kernel,
        out_shape=[
            jax.ShapeDtypeStruct((4, height, width), BF),
            jax.ShapeDtypeStruct(wide.shape, BF),
            jax.ShapeDtypeStruct((2, *cond.shape), BF),
            jax.ShapeDtypeStruct((2, *size.shape), size.dtype),
        ],
        in_specs=near_specs(4),
        out_specs=any_specs(4),
        scratch_shapes=[dma(2), dma(2), dma(3), dma(3), dma(2), dma(2), dma(2), dma(2), dma(4)],
        compiler_params=pltpu.CompilerParams(
            collective_id=1, has_side_effects=True, vmem_limit_bytes=ROOM
        ),
        name="first_moves",
    )(rows, wide, cond, size)


def weights_kernel(
    shard_ref, block_ref, *refs, groups, wides
):
    count = len(groups)
    arrays = max(which for which, _ in groups) + 1
    whole_refs, wide_ref = refs[:arrays], refs[arrays]
    send_s, recv_s, send_z, recv_z, send_p, recv_p, local = refs[arrays + 1 : arrays + 8]
    send_w, recv_w, send_v, recv_v, local_w = refs[arrays + 8 :]
    dp, plane, core, z = spot()
    width = shard_ref.shape[2]
    sibling = (flip(dp, 1), z)
    xmate, ymate, far = plane_mates(dp, z)
    lines = [(dp, lax.rem(z + step, 4)) for step in range(1, 4)]
    greet([sibling, xmate, ymate] + lines)
    home = z // 2 == core
    above, below = (dp, z + 1), (dp, z - 1)

    def columns(which):
        return pl.ds(pl.multiple_of(which * width, width), width)

    def slab(g):
        array, index = groups[g]
        return whole_refs[array].at[index]

    for g in range(count):
        target = slab(g).at[plane, core, :, columns(z % 2)]

        @pl.when(home)
        def _(g=g, target=target):
            pltpu.make_async_copy(shard_ref.at[g], target, local.at[g]).start()

        @pl.when(jnp.logical_not(home))
        def _(g=g, target=target):
            push(shard_ref.at[g], target, send_s.at[g], recv_s.at[g], sibling).start()

    near = jnp.where(core == 0, jnp.where(z >= 1, 1, 0), jnp.where(z <= 2, 0, 1))

    def order(turn):
        return near if turn == 0 else 1 - near

    def area(g, which, chip):
        return slab(g).at[chip, :, :, columns(which)]

    def on_z(g, turn, act):
        which = order(turn)
        source_z = 2 * core + which
        place = area(g, which, plane)
        for way, (wanted, target) in enumerate(
            [
                (jnp.logical_and(z >= source_z, z < 3), above),
                (jnp.logical_and(z <= source_z, z > 0), below),
            ]
        ):

            @pl.when(wanted)
            def _(way=way, target=target):
                act(push(place, place, send_z.at[g, turn, way], recv_z.at[g, which], target))

    def arrive(g, turn):
        which = order(turn)
        source_z = 2 * core + which

        @pl.when(z == source_z)
        def _():
            mine = slab(g).at[plane, core, :, columns(which)]
            other = slab(g).at[plane, 1 - core, :, columns(which)]
            pltpu.make_async_copy(shard_ref.at[g], mine, local.at[g]).wait()
            push(mine, other, send_s.at[g], recv_s.at[g], sibling).wait_recv()

        @pl.when(z != source_z)
        def _():
            place = area(g, which, plane)
            push(place, place, send_z.at[g, turn, 0], recv_z.at[g, which], sibling).wait_recv()

    def hop(g, turn, chip, slot, mate):
        place = area(g, order(turn), chip)
        return push(place, place, send_p.at[g, turn, slot], recv_p.at[g, turn, slot], mate)

    mates = (xmate, ymate)

    def spread(g, turn):
        arrive(g, turn)
        on_z(g, turn, lambda copy: copy.start())
        hop(g, turn, plane, turn, mates[turn]).start()
        hop(g, turn, plane, 1 - turn, mates[1 - turn]).start()

    def relay(g, turn):
        chip = mates[turn][0] // 2
        hop(g, turn, chip, turn, mates[turn]).wait_recv()
        hop(g, turn, chip, 2, mates[1 - turn]).start()

    wide_width = block_ref.shape[3]

    def quarter(k, block, side):
        return wide_ref.at[k, :, side, :, pl.ds(pl.multiple_of(block * wide_width, wide_width), wide_width)]

    def wide_copy(k, block, way, target):
        place = quarter(k, block, core)
        return push(place, place, send_w.at[k, block, way], recv_w.at[k, block], target)

    def to_sibling(k, block, side):
        place = quarter(k, block, side)
        return push(place, place, send_v.at[k, block], recv_v.at[k, block], sibling)

    def wide_own(k):
        pltpu.make_async_copy(block_ref.at[k], quarter(k, z, core), local_w.at[k]).start()
        pltpu.make_async_copy(block_ref.at[k], quarter(k, z, core), local_w.at[k]).wait()
        for way, (wanted, target) in enumerate([(z < 3, above), (z > 0, below)]):

            @pl.when(wanted)
            def _(way=way, target=target):
                wide_copy(k, z, way, target).start()

        to_sibling(k, z, core).start()

    def wide_step(k, step):
        for way, (block, wanted, further, target) in enumerate(
            [
                (z - step, z - step >= 0, z < 3, above),
                (z + step, z + step <= 3, z > 0, below),
            ]
        ):

            @pl.when(wanted)
            def _(block=block, way=way, target=target):
                wide_copy(k, block, way, target).wait_recv()
                to_sibling(k, block, core).start()

            @pl.when(jnp.logical_and(wanted, further))
            def _(block=block, way=way, target=target):
                wide_copy(k, block, way, target).start()

    script = (
        "S0 S1 R0 S2 R1 S3 R2 S4 R3 S5 S6 W0 R4 W1 R5 V01 R6 V11 V02 V12 V03 V13"
    )
    for word in script.split():
        kind = word[0]
        if kind == "S":
            spread(int(word[1]), 0)
            spread(int(word[1]), 1)
        elif kind == "R":
            relay(int(word[1]), 0)
            relay(int(word[1]), 1)
        elif kind == "W" and int(word[1]) < wides:
            wide_own(int(word[1]))
        elif kind == "V" and int(word[1]) < wides:
            wide_step(int(word[1]), int(word[2]))
    for g in range(count):
        for turn in range(2):
            hop(g, turn, mates[1 - turn][0] // 2, 1 - turn, mates[1 - turn]).wait_recv()
            hop(g, turn, far[0] // 2, 2, mates[1 - turn]).wait_recv()
            for slot in range(3):
                hop(g, turn, plane, slot, xmate).wait_send()
            on_z(g, turn, lambda copy: copy.wait_send())

        @pl.when(jnp.logical_not(home))
        def _(g=g):
            push(shard_ref.at[g], shard_ref.at[g], send_s.at[g], recv_s.at[g], sibling).wait_send()

    for k in range(wides):
        for block in range(4):
            to_sibling(k, block, core).wait_send()
            to_sibling(k, block, 1 - core).wait_recv()

            @pl.when(jnp.logical_and(block <= z, z < 3))
            def _(k=k, block=block):
                wide_copy(k, block, 0, above).wait_send()

            @pl.when(jnp.logical_and(block >= z, z > 0))
            def _(k=k, block=block):
                wide_copy(k, block, 1, below).wait_send()


def weights_moves(shard, block, groups, wides):
    count, depth, width = shard.shape
    sizes = [0] * (max(which for which, _ in groups) + 1)
    for which, _ in groups:
        sizes[which] += 1
    _, chips, _, unit = block.shape
    out = pl.pallas_call(
        functools.partial(weights_kernel, groups=groups, wides=wides),
        out_shape=[jax.ShapeDtypeStruct((size, 4, 2, depth, 2 * width), BF) for size in sizes]
        + [jax.ShapeDtypeStruct((wides, chips, 2, depth, 4 * unit), BF)],
        in_specs=near_specs(2),
        out_specs=any_specs(len(sizes) + 1),
        scratch_shapes=[
            dma(count),
            dma(count),
            dma(count, 2, 2),
            dma(count, 2),
            dma(count, 2, 3),
            dma(count, 2, 3),
            dma(count),
            dma(wides, 4, 2),
            dma(wides, 4),
            dma(wides, 4),
            dma(wides, 4),
            dma(wides),
        ],
        compiler_params=pltpu.CompilerParams(
            collective_id=2, has_side_effects=True, vmem_limit_bytes=ROOM
        ),
        name="weights_moves",
    )(shard, block)
    return [whole.reshape(whole.shape[0], 8 * depth, whole.shape[-1]) for whole in out]


def second_kernel(
    rows_ref, quarter_ref, all_ref, wide_ref, send_r, recv_r, send_w, recv_w, local, held, held_sem
):
    dp, plane, core, z = spot()
    sibling = (flip(dp, 1), z)
    xmate, ymate, far = plane_mates(dp, z)
    greet([sibling, xmate, ymate])
    width = quarter_ref.shape[4]

    def rows(source, chip, part, slot, mate):
        return push(source, all_ref.at[chip, part], send_r.at[slot], recv_r.at[slot], mate)

    own = [
        rows(rows_ref.at[0], 1, 0, 0, xmate),
        rows(rows_ref.at[1], 2, 1, 1, ymate),
        rows(rows_ref.at[0], 2, 0, 2, ymate),
        rows(rows_ref.at[1], 1, 1, 3, xmate),
    ]
    for copy in own:
        copy.start()
    wide, loads = [], []
    for block in range(4):
        columns = pl.ds(block * width, width)
        target = wide_ref.at[:, :, core, :, columns]
        loads.append(pltpu.make_async_copy(quarter_ref.at[block], held.at[block], held_sem.at[block]))
        wide.append(pltpu.make_async_copy(held.at[block], target, local.at[block]))
        wide.append(push(held.at[block], target, send_w.at[block], recv_w.at[block], sibling))
    for copy in loads:
        copy.start()
    keep = pltpu.make_async_copy(rows_ref, all_ref.at[0], local.at[4])
    keep.start()
    for block in range(4):
        loads[block].wait()
        wide[2 * block].start()
        wide[2 * block + 1].start()
    own[0].wait_recv()
    upper = rows(all_ref.at[1, 0], 3, 0, 4, ymate)
    upper.start()
    own[1].wait_recv()
    lower = rows(all_ref.at[2, 1], 3, 1, 5, xmate)
    lower.start()
    own[2].wait_recv()
    own[3].wait_recv()
    for copy in own:
        copy.wait_send()
    upper.wait()
    lower.wait()
    keep.wait()
    for block in range(4):
        columns = pl.ds(block * width, width)
        wide[2 * block].wait()
        wide[2 * block + 1].wait_send()
        theirs = wide_ref.at[:, :, 1 - core, :, columns]
        push(theirs, theirs, send_w.at[block], recv_w.at[block], sibling).wait_recv()


def second_moves(rows, quarter):
    blocks, count, chips, depth, width = quarter.shape
    return pl.pallas_call(
        second_kernel,
        out_shape=[
            jax.ShapeDtypeStruct((4, *rows.shape), BF),
            jax.ShapeDtypeStruct((count, chips, 2, depth, blocks * width), BF),
        ],
        in_specs=near_specs(1) + any_specs(1),
        out_specs=any_specs(2),
        scratch_shapes=[
            dma(6),
            dma(6),
            dma(4),
            dma(4),
            dma(5),
            pltpu.VMEM(quarter.shape, BF),
            dma(4),
        ],
        compiler_params=pltpu.CompilerParams(
            collective_id=3, has_side_effects=True, vmem_limit_bytes=ROOM
        ),
        name="second_moves",
    )(rows, quarter)


def third_kernel(
    part_ref, *refs, counts
):
    many = len(counts)
    grad_refs = refs[:many]
    sum_ref, quarter_ref = refs[many : many + 2]
    got, far_x, far_y, own, theirs = refs[many + 2 : many + 7]
    send_r, recv_r, send_w, recv_w, load, store = refs[many + 7 :]
    dp, plane, core, z = spot()
    sibling = (flip(dp, 1), z)
    xmate, ymate, _ = plane_mates(dp, z)
    greet([sibling, xmate, ymate])

    def rows(source, slot, mate):
        return push(source, got.at[slot], send_r.at[slot], recv_r.at[slot], mate)

    first = [
        rows(part_ref.at[3, 0], 0, xmate),
        rows(part_ref.at[3, 1], 1, ymate),
        rows(part_ref.at[1, 0], 2, xmate),
        rows(part_ref.at[2, 1], 3, ymate),
    ]
    for copy in first:
        copy.start()
    wide, loads, base = [], [], 0
    for grad, count in zip(grad_refs, counts, strict=True):
        for k in range(count):
            slot = base + k
            wide.append(
                push(grad.at[k, :, 1 - core], theirs.at[slot], send_w.at[slot], recv_w.at[slot], sibling)
            )
            loads.append(pltpu.make_async_copy(grad.at[k, :, core], own.at[slot], load.at[slot]))
        base += count
    for copy in wide + loads:
        copy.start()
    slabs = base
    chips, depth, width = own.shape[1:]
    unit = width // 4

    def core_sums(slot):
        loads[slot].wait()
        wide[slot].wait_recv()

        def body(chip, carry):
            own[slot, chip] = own[slot, chip] + theirs[slot, chip]
            return carry

        lax.fori_loop(0, chips, body, 0)
        for block in range(4):
            pltpu.make_async_copy(
                own.at[slot, :, :, pl.ds(block * unit, unit)],
                quarter_ref.at[block, slot],
                store.at[slot, block],
            ).start()

    core_sums(0)
    first[0].wait_recv()
    far_x[...] = (part_ref[2, 0].astype(F32) + got[0].astype(F32)).astype(BF)
    upper = rows(far_x, 4, ymate)
    upper.start()
    first[1].wait_recv()
    far_y[...] = (part_ref[1, 1].astype(F32) + got[1].astype(F32)).astype(BF)
    lower = rows(far_y, 5, xmate)
    lower.start()
    for slot in range(1, slabs):
        core_sums(slot)
    first[2].wait_recv()
    first[3].wait_recv()
    upper.wait_recv()
    sum_ref[0] = part_ref[0, 0].astype(F32) + got[2].astype(F32) + got[4].astype(F32)
    lower.wait_recv()
    sum_ref[1] = part_ref[0, 1].astype(F32) + got[3].astype(F32) + got[5].astype(F32)
    for copy in first + wide + [upper, lower]:
        copy.wait_send()
    for slot in range(slabs):
        for block in range(4):
            pltpu.make_async_copy(
                own.at[slot, :, :, pl.ds(block * unit, unit)],
                quarter_ref.at[block, slot],
                store.at[slot, block],
            ).wait()


def third_moves(part, grads):
    _, _, height, width = part.shape
    counts = tuple(grad.shape[0] for grad in grads)
    slabs = sum(counts)
    depth, units = grads[0].shape[1] // 8, grads[0].shape[2]
    return pl.pallas_call(
        functools.partial(third_kernel, counts=counts),
        out_shape=[
            jax.ShapeDtypeStruct((2, height, width), F32),
            jax.ShapeDtypeStruct((4, slabs, 4, depth, units // 4), BF),
        ],
        in_specs=near_specs(1) + any_specs(len(grads)),
        out_specs=near_specs(1) + any_specs(1),
        scratch_shapes=[
            pltpu.VMEM((6, height, width), BF),
            pltpu.VMEM((height, width), BF),
            pltpu.VMEM((height, width), BF),
            pltpu.VMEM((slabs, 4, depth, units), BF),
            pltpu.VMEM((slabs, 4, depth, units), BF),
            dma(6),
            dma(6),
            dma(slabs),
            dma(slabs),
            dma(slabs),
            dma(slabs, 4),
        ],
        compiler_params=pltpu.CompilerParams(
            collective_id=4, has_side_effects=True, vmem_limit_bytes=ROOM
        ),
        name="third_moves",
    )(part, *[grad.reshape(grad.shape[0], 4, 2, depth, units) for grad in grads])


def share_kernel(
    *refs, groups, arrays
):
    count = len(groups)
    grad_refs, refs = refs[:arrays], refs[arrays:]
    rows_ref, gain_ref, cond_ref = refs[:3]
    out_ref, back_ref, gain_out, cond_out = refs[3:7]
    one, got, two, line, gain_got, gain_sum, gain_line = refs[7:14]
    (
        load,
        send_x,
        recv_x,
        send_y,
        recv_y,
        send_z,
        recv_z,
        send_c,
        recv_c,
        send_r,
        recv_r,
        send_g,
        recv_g,
        send_h,
        recv_h,
        send_k,
        recv_k,
        local,
    ) = refs[14:]
    dp, plane, core, z = spot()
    xbit, ybit = plane % 2, plane // 2
    sibling = (flip(dp, 1), z)
    xmate, ymate, _ = plane_mates(dp, z)
    plane_all = [(lax.rem(dp + step, 8), z) for step in range(1, 8)]
    greet(plane_all + column_mates(dp, z)[1:])
    home = z // 2 == core
    above, below = (dp, z + 1), (dp, z - 1)
    width = out_ref.shape[2]
    near = jnp.where(core == 0, jnp.where(z >= 1, 1, 0), jnp.where(z <= 2, 0, 1))
    mates = (xmate, ymate)

    def order(turn):
        return 1 - near if turn == 0 else near

    def columns(which):
        return pl.ds(pl.multiple_of(which * width, width), width)

    def strip(g, turn, bit):
        array, index = groups[g]
        grid = grad_refs[array].at[index]
        if turn == 0:
            return grid.at[:, bit, :, :, columns(order(turn))]
        return grid.at[bit, :, :, :, columns(order(turn))]

    bits = (xbit, ybit)

    def step_one(g, turn):
        return push(
            strip(g, turn, 1 - bits[turn]), got.at[g, turn], send_x.at[g, turn], recv_x.at[g, turn], mates[turn]
        )

    def fetch(g, turn):
        return pltpu.make_async_copy(strip(g, turn, bits[turn]), one.at[g, turn], load.at[g, turn])

    def step_two(g, turn):
        return push(
            one.at[g, turn, 1 - bits[1 - turn]],
            two.at[g, turn],
            send_y.at[g, turn],
            recv_y.at[g, turn],
            mates[1 - turn],
        )

    def after_one(g, turn):
        fetch(g, turn).wait()
        step_one(g, turn).wait_recv()

        def body(i, carry):
            side, part = i // 2, i % 2
            one[g, turn, side, part] = one[g, turn, side, part] + got[g, turn, side, part]
            return carry

        lax.fori_loop(0, 4, body, 0)
        step_two(g, turn).start()

    def z_of(turn):
        return 2 * core + order(turn)

    def add_held(g, turn, source):
        side = bits[1 - turn]

        def body(part, carry):
            one[g, turn, side, part] = one[g, turn, side, part] + source[part]
            return carry

        lax.fori_loop(0, 2, body, 0)

    def line_copy(g, turn, way, target):
        held = one.at[g, turn, bits[1 - turn]]
        which = order(turn)
        return push(held, line.at[g, which, way], send_z.at[g, turn], recv_z.at[g, which, way], target)

    def after_two(g, turn):
        step_two(g, turn).wait_recv()
        add_held(g, turn, two.at[g, turn])
        which, goal = order(turn), z_of(turn)

        @pl.when(jnp.logical_and(z > 0, z <= goal))
        def _():
            line_copy(g, turn, 0, above).wait_recv()
            add_held(g, turn, line.at[g, which, 0])

        @pl.when(jnp.logical_and(z < 3, z >= goal))
        def _():
            line_copy(g, turn, 1, below).wait_recv()
            add_held(g, turn, line.at[g, which, 1])

        @pl.when(z < goal)
        def _():
            line_copy(g, turn, 0, above).start()

        @pl.when(z > goal)
        def _():
            line_copy(g, turn, 1, below).start()

        @pl.when(z == goal)
        def _():
            held = one.at[g, turn, bits[1 - turn]]
            pltpu.make_async_copy(held.at[core], out_ref.at[g], local.at[g]).start()
            push(held.at[1 - core], out_ref.at[g], send_c.at[g], recv_c.at[g], sibling).start()

    for g in range(count):
        for turn in range(2):
            step_one(g, turn).start()
            fetch(g, turn).start()
    many = rows_ref.shape[0]
    for a in range(many):
        for j in range(2):
            stays = jnp.logical_and(home, 2 * core + j == z)

            @pl.when(stays)
            def _(a=a, j=j):
                pltpu.make_async_copy(rows_ref.at[a, j], back_ref.at[a, z % 2], local.at[count + a]).start()

            @pl.when(jnp.logical_not(stays))
            def _(a=a, j=j):
                target = (plane * 2 + z // 2, 2 * core + j)
                push(
                    rows_ref.at[a, j], back_ref.at[a, z % 2], send_r.at[a, j], recv_r.at[a, z % 2], target
                ).start()

    gains = []
    for step in range(1, 8):
        mate = lax.rem(dp + step, 8)
        gains.append(
            push(gain_ref.at[mate], gain_got.at[8 - step], send_g.at[step], recv_g.at[8 - step], (mate, z))
        )
    for copy in gains:
        copy.start()

    @pl.when(home)
    def _():
        pltpu.make_async_copy(cond_ref, cond_out.at[z % 2], local.at[count + many]).start()
        for step in range(1, 4):
            target = (dp, lax.rem(z + step, 4))
            push(cond_ref, cond_out.at[z % 2], send_k.at[step], recv_k.at[z % 2], target).start()

    for copy in gains:
        copy.wait()
    total = gain_ref[dp]
    for step in range(1, 8):
        total = total + gain_got[step]
    gain_sum[...] = total
    sums = []
    for step in range(1, 4):
        target = (dp, lax.rem(z + step, 4))
        sums.append(push(gain_sum, gain_line.at[4 - step], send_h.at[step], recv_h.at[4 - step], target))
    for copy in sums:
        copy.start()

    pieces = [(g, turn) for g in range(count) for turn in range(2)]
    lag = 2
    for i in range(len(pieces) + lag):
        if i < len(pieces):
            after_one(*pieces[i])
        if i >= lag:
            after_two(*pieces[i - lag])

    for copy in sums:
        copy.wait()
    total = gain_sum[...]
    for step in range(1, 4):
        total = total + gain_line[step]
    gain_out[...] = total
    for g in range(count):
        for turn in range(2):
            goal = z_of(turn)
            step_one(g, turn).wait_send()
            step_two(g, turn).wait_send()

            @pl.when(z != goal)
            def _(g=g, turn=turn):
                line_copy(g, turn, 0, above).wait_send()

        @pl.when(home)
        def _(g=g):
            pltpu.make_async_copy(out_ref.at[g], out_ref.at[g], local.at[g]).wait()
            push(out_ref.at[g], out_ref.at[g], send_c.at[g], recv_c.at[g], sibling).wait_send()

        @pl.when(jnp.logical_not(home))
        def _(g=g):
            push(out_ref.at[g], out_ref.at[g], send_c.at[g], recv_c.at[g], sibling).wait_recv()

    for a in range(many):
        for j in range(2):
            stays = jnp.logical_and(home, 2 * core + j == z)

            @pl.when(stays)
            def _(a=a, j=j):
                pltpu.make_async_copy(rows_ref.at[a, j], back_ref.at[a, z % 2], local.at[count + a]).wait()

            @pl.when(jnp.logical_not(stays))
            def _(a=a, j=j):
                push(rows_ref.at[a, j], back_ref.at[a, 0], send_r.at[a, j], recv_r.at[a, 0], sibling).wait_send()

            @pl.when(jnp.logical_not(jnp.logical_and(home, z % 2 == j)))
            def _(a=a, j=j):
                push(rows_ref.at[a, j], back_ref.at[a, j], send_r.at[a, j], recv_r.at[a, j], sibling).wait_recv()

    @pl.when(home)
    def _():
        pltpu.make_async_copy(cond_ref, cond_out.at[z % 2], local.at[count + many]).wait()
        for step in range(1, 4):
            push(cond_ref, cond_out.at[0], send_k.at[step], recv_k.at[0], sibling).wait_send()

    for s in range(2):

        @pl.when(z != 2 * core + s)
        def _(s=s):
            push(cond_ref, cond_out.at[s], send_k.at[1], recv_k.at[s], sibling).wait_recv()


def share_moves(grads, groups, rows, gains, cond):
    count = len(groups)
    depth, width = grads[0].shape[1] // 8, grads[0].shape[2] // 2
    many = rows.shape[0]
    return pl.pallas_call(
        functools.partial(share_kernel, groups=groups, arrays=len(grads)),
        out_shape=[
            jax.ShapeDtypeStruct((count, depth, width), BF),
            jax.ShapeDtypeStruct(rows.shape, BF),
            jax.ShapeDtypeStruct(gains.shape[1:], F32),
            jax.ShapeDtypeStruct((2, *cond.shape), BF),
        ],
        in_specs=any_specs(len(grads)) + near_specs(3),
        out_specs=near_specs(1) + any_specs(1) + near_specs(1) + any_specs(1),
        scratch_shapes=[
            pltpu.VMEM((count, 2, 2, 2, depth, width), BF),
            pltpu.VMEM((count, 2, 2, 2, depth, width), BF),
            pltpu.VMEM((count, 2, 2, depth, width), BF),
            pltpu.VMEM((count, 2, 2, 2, depth, width), BF),
            pltpu.VMEM(gains.shape, F32),
            pltpu.VMEM(gains.shape[1:], F32),
            pltpu.VMEM((4, *gains.shape[1:]), F32),
            dma(count, 2),
            dma(count, 2),
            dma(count, 2),
            dma(count, 2),
            dma(count, 2),
            dma(count, 2),
            dma(count, 2, 2),
            dma(count),
            dma(count),
            dma(many, 2),
            dma(many, 2),
            dma(8),
            dma(8),
            dma(4),
            dma(4),
            dma(4),
            dma(2),
            dma(count + many + 1),
        ],
        compiler_params=pltpu.CompilerParams(
            collective_id=5, has_side_effects=True, vmem_limit_bytes=ROOM
        ),
        name="share_moves",
    )(*[grad.reshape(grad.shape[0], 2, 2, 2, depth, 2 * width) for grad in grads], rows, gains, cond)


def chip_shards(
    inputs,
    context,
    lengths,
    cotangent,
    self_qkv,
    self_out,
    cross_query,
    cross_context,
    cross_out,
    gate_up,
    down_proj,
    norm_gains,
):
    dp, z = lax.axis_index("dp"), lax.axis_index("tensor")
    core, xbit, ybit = dp & 1, (dp >> 1) & 1, (dp >> 2) & 1
    place = (core, xbit, ybit, z)
    model_width = inputs.shape[-1]
    padded = inputs.shape[1] * 4
    half_rows = padded // 2

    def own_half(value):
        return take(value.reshape(2, half_rows, -1), core, 0)

    def both_halves(mine, theirs):
        return ordered(core, mine, theirs, 0).reshape(padded, -1)

    pair_sum = lambda value: value + swap(value.astype(BF), CORE).astype(F32)

    cc_depth = cross_context.shape[1]
    tokens = context.shape[1]
    narrow = jnp.concatenate(
        [
            self_qkv,
            self_out.T[None],
            cross_query[None],
            cross_context.reshape(1, 2 * cc_depth, -1),
            cross_out.T[None],
        ]
    ).astype(BF)
    depth, units = gate_up.shape[1], gate_up.shape[2]
    wide = jnp.concatenate([gate_up, down_proj.T[None]]).astype(BF)
    wide = jnp.moveaxis(wide.reshape(3, depth, 4, units // 4), 2, 1)
    room = -tokens % 16
    cond = jnp.pad(take(context, z % 2, 0), ((0, room), (0, 0)))
    size = jnp.broadcast_to(take(lengths, z % 2, 0), (8, 128))
    sequence, wide, cond, size = first_moves(inputs, wide, cond, size)
    stream = sequence.reshape(padded, model_width).astype(F32)
    length = take(size, z // 2, 0)[0, 0]
    cond = take(cond, z // 2, 0)[:tokens]
    qkv_whole, so_whole, cq_whole, cc_whole, co_whole, gu_whole = weights_moves(
        narrow, wide, ((0, 0), (0, 1), (0, 2), (1, 0), (2, 0), (3, 0), (4, 0)), 2
    )
    wide, qkv_whole = lax.optimization_barrier((wide, qkv_whole))
    quarter = lax.all_gather(wide[2:], "tensor", axis=0)
    so_whole, cq_whole, co_whole = so_whole[0], cq_whole[0], co_whole[0]
    cc_whole = cc_whole[0].reshape(8, 2, cc_depth, -1)
    cc_whole = jnp.moveaxis(cc_whole, 1, 0).reshape(2, 8 * cc_depth, -1)
    cot_half = rows_in(cotangent, z)
    cot = both_halves(cot_half, swap(cot_half, CORE)).astype(F32)

    positions = jnp.arange(padded, dtype=jnp.int32)
    key_valid = positions < length
    row_keep = key_valid.astype(F32)[:, None]
    keep_half = own_half(row_keep)
    context_valid = jnp.ones((cond.shape[0],), dtype=jnp.bool_)

    normed_one, scaled_one, inverse_one = norm_rows(stream, norm_gains[0])
    normed_one = normed_one.astype(BF)
    qkv = jnp.einsum("td,kde->kte", normed_one, qkv_whole, preferred_element_type=F32).astype(BF)
    mixed_one, logsum_one = attend_forward((qkv[0], qkv[1], qkv[2], key_valid))
    branch = jnp.einsum("te,de->td", mixed_one, so_whole, preferred_element_type=F32)
    stream = stream + row_keep * pair_sum(branch)
    normed_two, scaled_two, inverse_two = norm_rows(stream, norm_gains[1])
    normed_two = normed_two.astype(BF)
    cross_rows = jnp.einsum("td,de->te", normed_two, cq_whole, preferred_element_type=F32).astype(BF)
    cond_rows = jnp.einsum("sd,kde->kse", cond, cc_whole, preferred_element_type=F32).astype(BF)
    mixed_two, logsum_two = attend_forward((cross_rows, cond_rows[0], cond_rows[1], context_valid))
    branch = jnp.einsum("te,de->td", mixed_two, co_whole, preferred_element_type=F32)
    stream = stream + row_keep * pair_sum(branch)
    stream_half = own_half(stream)
    normed_three, scaled_three, inverse_three = norm_rows(stream_half, norm_gains[2])
    rows_three, down_whole = second_moves(
        normed_three.astype(BF).reshape(2, -1, model_width), quarter
    )
    rows_three = rows_three.reshape(-1, model_width)
    down_whole = down_whole.reshape(model_width, units)
    gate_rows = jnp.einsum("td,kde->kte", rows_three, gu_whole, preferred_element_type=F32)
    sigmoid_gate = jax.nn.sigmoid(gate_rows[0])
    hidden = (gate_rows[0] * sigmoid_gate * gate_rows[1]).astype(BF)

    grad_stream = row_keep * cot
    grad_branch = plane_rows((keep_half * own_half(grad_stream)).astype(BF))
    grad_hidden = jnp.einsum("td,df->tf", grad_branch, down_whole, preferred_element_type=F32)
    grad_gate = (
        grad_hidden * gate_rows[1] * sigmoid_gate * (1.0 + gate_rows[0] * (1.0 - sigmoid_gate))
    )
    grad_upper = grad_hidden * gate_rows[0] * sigmoid_gate
    grad_expand = jnp.stack([grad_gate, grad_upper]).astype(BF)
    partial_value = jnp.einsum("ktf,kdf->td", grad_expand, gu_whole, preferred_element_type=F32)
    grad_down = jnp.einsum("td,tf->df", grad_branch, hidden, preferred_element_type=F32)
    grad_gates = jnp.einsum("td,ktf->kdf", rows_three, grad_expand, preferred_element_type=F32)
    sums, wide_grads = third_moves(
        partial_value.astype(BF).reshape(4, 2, -1, model_width),
        [grad_gates.astype(BF), grad_down.astype(BF)[None]],
    )
    grad_norm, gain_rows = norm_back(
        sums.reshape(half_rows, model_width), scaled_three, inverse_three, norm_gains[2]
    )
    gain_three = jnp.sum(gain_rows, axis=0)
    wide_grads = lax.psum_scatter(wide_grads, "tensor", scatter_dimension=0, tiled=False)
    branch = jnp.einsum("tf,df->td", hidden, down_whole, preferred_element_type=F32)
    stream_half = stream_half + keep_half * plane_sums(branch)
    output = (keep_half * stream_half).astype(BF)

    grad_stream = grad_stream + both_halves(grad_norm, swap(grad_norm.astype(BF), CORE).astype(F32))
    grad_branch = (row_keep * grad_stream).astype(BF)
    grad_mixed = jnp.einsum("td,de->te", grad_branch, co_whole, preferred_element_type=F32).astype(BF)
    grad_query, grad_key, grad_value = attend_backward(
        (cross_rows, cond_rows[0], cond_rows[1], logsum_two, grad_mixed, context_valid)
    )
    partial_value = jnp.einsum("te,de->td", grad_query, cq_whole, preferred_element_type=F32)
    grad_norm, gain_rows = norm_back(
        pair_sum(partial_value), scaled_two, inverse_two, norm_gains[1]
    )
    gain_two = 0.5 * jnp.sum(gain_rows, axis=0)
    grad_merge = jnp.einsum("td,te->de", grad_branch, mixed_two, preferred_element_type=F32)
    grad_cross = jnp.einsum("td,te->de", normed_two, grad_query, preferred_element_type=F32)
    grad_pairs = jnp.stack([grad_key, grad_value])
    grad_cc = jnp.einsum("sd,kse->kde", cond, grad_pairs, preferred_element_type=F32)
    grad_cc = jnp.moveaxis(grad_cc.reshape(2, 8, cc_depth, -1), 0, 1).reshape(model_width, -1)
    context_part = jnp.einsum("kse,kde->sd", grad_pairs, cc_whole, preferred_element_type=F32)
    context_part = jnp.pad(pair_sum(context_part).astype(BF), ((0, room), (0, 0)))

    grad_stream = grad_stream + grad_norm
    grad_branch = (row_keep * grad_stream).astype(BF)
    grad_mixed = jnp.einsum("td,de->te", grad_branch, so_whole, preferred_element_type=F32).astype(BF)
    grad_after = jnp.einsum("td,te->de", grad_branch, mixed_one, preferred_element_type=F32)
    grad_triple = jnp.stack(
        attend_backward((qkv[0], qkv[1], qkv[2], logsum_one, grad_mixed, key_valid))
    )
    grad_self = jnp.einsum("td,kte->kde", normed_one, grad_triple, preferred_element_type=F32)
    partial_value = jnp.einsum("kte,kde->td", grad_triple, qkv_whole, preferred_element_type=F32)
    grad_norm, gain_rows = norm_back(
        pair_sum(partial_value), scaled_one, inverse_one, norm_gains[0]
    )
    gain_one = 0.5 * jnp.sum(gain_rows, axis=0)
    grad_inputs = own_half(grad_stream + grad_norm).astype(BF)
    back = jnp.stack([output, grad_inputs]).reshape(2, 2, -1, model_width)
    gains = jnp.stack([gain_one, gain_two, gain_three]).reshape(3, 8, -1)
    gains = jnp.pad(jnp.moveaxis(gains, 0, 1), ((0, 0), (0, 5), (0, 0)))
    shares, back, gains, conds = share_moves(
        [
            grad_merge.astype(BF)[None],
            grad_cross.astype(BF)[None],
            grad_cc.astype(BF)[None],
            grad_after.astype(BF)[None],
            grad_self.astype(BF),
        ],
        ((0, 0), (1, 0), (2, 0), (3, 0), (4, 0), (4, 1), (4, 2)),
        back,
        gains,
        context_part,
    )
    shared = lax.all_to_all(wide_grads, "dp", 1, 1, axis_index_groups=[[0, 2, 4, 6], [1, 3, 5, 7]])
    shared = jnp.moveaxis(shared, 1, 2).reshape(3, depth, units).astype(F32)
    shares = shares.astype(F32)
    return (
        back[0],
        back[1].astype(F32),
        conds[:, :tokens].astype(F32),
        shares[4:],
        shares[3].T,
        shares[1],
        shares[2].reshape(2, cc_depth, -1),
        shares[0].T,
        shared[:2],
        shared[2].T,
        gains[:3],
    )


def solution(mesh):
    sizes = (mesh.shape["dp"], mesh.shape["tensor"])
    body = chip_shards if sizes == (8, 4) else shards
    placed = (
        P("dp", "tensor", None),
        P("dp", None, None),
        P("dp"),
        P("dp", "tensor", None),
        P(None, "dp", "tensor"),
        P("tensor", "dp"),
        P("dp", "tensor"),
        P(None, "dp", "tensor"),
        P("tensor", "dp"),
        P(None, "dp", "tensor"),
        P("tensor", "dp"),
        P(),
    )
    return jax.shard_map(
        body,
        mesh=mesh,
        in_specs=placed,
        out_specs=(
            P("dp", "tensor", None),
            P("dp", "tensor", None),
            P("dp", None, None),
            P(None, "dp", "tensor"),
            P("tensor", "dp"),
            P("dp", "tensor"),
            P(None, "dp", "tensor"),
            P("tensor", "dp"),
            P(None, "dp", "tensor"),
            P("tensor", "dp"),
            P(None, "dp"),
        ),
        check_vma=False,
    )
```

```python
import functools

import jax
import jax.numpy as jnp
from jax import lax
from jax.experimental import pallas as pl
from jax.experimental.pallas import tpu as pltpu
from jax.sharding import PartitionSpec as P

HD = 64


EPSILON = 1e-05
NEGATIVE = -1000000000.0


def norm_rows(stream, gain):
    centred = stream - jnp.mean(stream, axis=-1, keepdims=True)
    inverse = lax.rsqrt(jnp.mean(centred * centred, axis=-1, keepdims=True) + EPSILON)
    scaled = centred * inverse
    return (scaled * gain, scaled, inverse)


def norm_back(grad_out, scaled, inverse, gain):
    grad_scaled = grad_out * gain
    centre_part = jnp.mean(grad_scaled, axis=-1, keepdims=True)
    slope_part = jnp.mean(grad_scaled * scaled, axis=-1, keepdims=True)
    grad_in = inverse * (grad_scaled - centre_part - scaled * slope_part)
    return (grad_in, grad_out * scaled)


def split_heads(flat):
    return flat.reshape(flat.shape[0], flat.shape[1] // HD, HD)


def masked_scores(queries, keys_in, key_valid):
    scores = jnp.einsum(
        "qhd,khd->hqk", queries, keys_in, preferred_element_type=jnp.float32
    ) * HD ** (-0.5)
    return jnp.where(key_valid[None, None, :], scores, NEGATIVE)


def attend_forward(item):
    query_rows, key_rows, value_rows, key_valid = item
    scores = masked_scores(split_heads(query_rows), split_heads(key_rows), key_valid)
    peak_score = jnp.max(scores, axis=-1, keepdims=True)
    exponent = jnp.exp(scores - peak_score)
    denominator = jnp.sum(exponent, axis=-1, keepdims=True)
    probs = (exponent / denominator).astype(jnp.bfloat16)
    mixed = jnp.einsum(
        "hqk,khd->qhd", probs, split_heads(value_rows), preferred_element_type=jnp.float32
    )
    return (
        mixed.reshape(query_rows.shape).astype(jnp.bfloat16),
        (peak_score + jnp.log(denominator))[..., 0],
    )


def attend_backward(item):
    query_rows, key_rows, value_rows, logsum, grad_mixed, key_valid = item
    queries = split_heads(query_rows)
    keys_in = split_heads(key_rows)
    values = split_heads(value_rows)
    grads = split_heads(grad_mixed)
    probs = jnp.exp(masked_scores(queries, keys_in, key_valid) - logsum[..., None])
    grad_probs = jnp.einsum("qhd,khd->hqk", grads, values, preferred_element_type=jnp.float32)
    inner_sum = jnp.sum(probs * grad_probs, axis=-1, keepdims=True)
    grad_scores = (probs * (grad_probs - inner_sum)).astype(jnp.bfloat16)
    grad_values = jnp.einsum(
        "hqk,qhd->khd", probs.astype(jnp.bfloat16), grads, preferred_element_type=jnp.float32
    )
    grad_queries = jnp.einsum(
        "hqk,khd->qhd", grad_scores, keys_in, preferred_element_type=jnp.float32
    ) * HD ** (-0.5)
    grad_keys = jnp.einsum(
        "hqk,qhd->khd", grad_scores, queries, preferred_element_type=jnp.float32
    ) * HD ** (-0.5)
    return (
        grad_queries.reshape(query_rows.shape).astype(jnp.bfloat16),
        grad_keys.reshape(key_rows.shape).astype(jnp.bfloat16),
        grad_values.reshape(value_rows.shape).astype(jnp.bfloat16),
    )


def rows_whole(local_rows):
    return lax.all_gather(local_rows, "tensor", axis=1, tiled=True)


def rows_share(partial_value):
    return lax.psum_scatter(partial_value, "tensor", scatter_dimension=1, tiled=True)


def grad_whole(local_rows):
    return lax.all_gather(local_rows, "tensor", axis=1, tiled=True)


def grad_share(partial_value):
    return lax.psum_scatter(
        partial_value.astype(jnp.bfloat16), "tensor", scatter_dimension=1, tiled=True
    ).astype(jnp.float32)


def shards(
    inputs,
    context,
    lengths,
    cotangent,
    self_qkv,
    self_out,
    cross_query,
    cross_context,
    cross_out,
    gate_up,
    down_proj,
    norm_gains,
):
    seq_count, row_count, model_width = inputs.shape
    padded = row_count * lax.axis_size("tensor")
    tokens = seq_count * padded
    local_pos = lax.axis_index("tensor") * row_count + jnp.arange(row_count, dtype=jnp.int32)
    key_valid = jnp.arange(padded, dtype=jnp.int32)[None, :] < lengths[:, None]
    context_valid = jnp.ones((seq_count, context.shape[1]), dtype=jnp.bool_)
    row_keep = (local_pos[None, :] < lengths[:, None]).astype(jnp.float32)[:, :, None]
    (
        full_self_qkv,
        full_self_out,
        full_cross_query,
        full_cross_context,
        full_cross_out,
        full_gate_up,
        full_down,
    ) = (
        lax.all_gather(self_qkv.astype(jnp.bfloat16), "dp", axis=1, tiled=True),
        lax.all_gather(self_out.astype(jnp.bfloat16), "dp", axis=1, tiled=True),
        lax.all_gather(cross_query.astype(jnp.bfloat16), "dp", axis=0, tiled=True),
        lax.all_gather(cross_context.astype(jnp.bfloat16), "dp", axis=1, tiled=True),
        lax.all_gather(cross_out.astype(jnp.bfloat16), "dp", axis=1, tiled=True),
        lax.all_gather(gate_up.astype(jnp.bfloat16), "dp", axis=1, tiled=True),
        lax.all_gather(down_proj.astype(jnp.bfloat16), "dp", axis=1, tiled=True),
    )
    stream = inputs.astype(jnp.float32)
    normed, scaled_one, inverse_one = norm_rows(stream, norm_gains[0])
    whole_one = rows_whole(normed.astype(jnp.bfloat16)).reshape(tokens, model_width)
    qkv_rows = jnp.einsum(
        "td,cde->cte", whole_one, full_self_qkv, preferred_element_type=jnp.float32
    )
    qkv_rows = qkv_rows.astype(jnp.bfloat16).reshape(3, seq_count, padded, -1)
    mixed_one, logsum_one = lax.map(
        attend_forward, (qkv_rows[0], qkv_rows[1], qkv_rows[2], key_valid)
    )
    branch = jnp.dot(
        mixed_one.reshape(tokens, -1), full_self_out, preferred_element_type=jnp.float32
    )
    stream = stream + row_keep * rows_share(branch.reshape(seq_count, padded, model_width))
    normed, scaled_two, inverse_two = norm_rows(stream, norm_gains[1])
    whole_two = rows_whole(normed.astype(jnp.bfloat16)).reshape(tokens, model_width)
    cross_rows = jnp.dot(whole_two, full_cross_query, preferred_element_type=jnp.float32)
    cross_rows = cross_rows.astype(jnp.bfloat16).reshape(seq_count, padded, -1)
    context_rows = jnp.einsum(
        "scd,kde->ksce", context, full_cross_context, preferred_element_type=jnp.float32
    ).astype(jnp.bfloat16)
    mixed_two, logsum_two = lax.map(
        attend_forward, (cross_rows, context_rows[0], context_rows[1], context_valid)
    )
    branch = jnp.dot(
        mixed_two.reshape(tokens, -1), full_cross_out, preferred_element_type=jnp.float32
    )
    stream = stream + row_keep * rows_share(branch.reshape(seq_count, padded, model_width))
    normed, scaled_three, inverse_three = norm_rows(stream, norm_gains[2])
    whole_three = rows_whole(normed.astype(jnp.bfloat16)).reshape(tokens, model_width)
    gate_rows = jnp.einsum(
        "td,kdf->ktf", whole_three, full_gate_up, preferred_element_type=jnp.float32
    )
    sigmoid_gate = jax.nn.sigmoid(gate_rows[0])
    hidden = (gate_rows[0] * sigmoid_gate * gate_rows[1]).astype(jnp.bfloat16)
    branch = jnp.dot(hidden, full_down, preferred_element_type=jnp.float32)
    stream = stream + row_keep * rows_share(branch.reshape(seq_count, padded, model_width))
    output = (row_keep * stream).astype(jnp.bfloat16)
    (
        full_self_qkv,
        full_self_out,
        full_cross_query,
        full_cross_context,
        full_cross_out,
        full_gate_up,
        full_down,
    ) = (
        lax.all_gather(self_qkv.astype(jnp.bfloat16), "dp", axis=1, tiled=True),
        lax.all_gather(self_out.astype(jnp.bfloat16), "dp", axis=1, tiled=True),
        lax.all_gather(cross_query.astype(jnp.bfloat16), "dp", axis=0, tiled=True),
        lax.all_gather(cross_context.astype(jnp.bfloat16), "dp", axis=1, tiled=True),
        lax.all_gather(cross_out.astype(jnp.bfloat16), "dp", axis=1, tiled=True),
        lax.all_gather(gate_up.astype(jnp.bfloat16), "dp", axis=1, tiled=True),
        lax.all_gather(down_proj.astype(jnp.bfloat16), "dp", axis=1, tiled=True),
    )
    grad_stream = row_keep * cotangent.astype(jnp.float32)
    grad_branch = grad_whole((row_keep * grad_stream).astype(jnp.bfloat16)).reshape(
        tokens, model_width
    )
    grad_down = jnp.einsum("tf,td->fd", hidden, grad_branch, preferred_element_type=jnp.float32)
    grad_hidden = jnp.einsum(
        "td,fd->tf", grad_branch, full_down, preferred_element_type=jnp.float32
    )
    grad_gate = (
        grad_hidden * gate_rows[1] * sigmoid_gate * (1.0 + gate_rows[0] * (1.0 - sigmoid_gate))
    )
    grad_upper = grad_hidden * gate_rows[0] * sigmoid_gate
    grad_expand = jnp.stack([grad_gate, grad_upper]).astype(jnp.bfloat16)
    grad_gates = jnp.einsum(
        "td,ktf->kdf", whole_three, grad_expand, preferred_element_type=jnp.float32
    )
    partial_value = jnp.einsum(
        "ktf,kdf->td", grad_expand, full_gate_up, preferred_element_type=jnp.float32
    )
    grad_norm, gain_rows = norm_back(
        grad_share(partial_value.reshape(seq_count, padded, model_width)),
        scaled_three,
        inverse_three,
        norm_gains[2],
    )
    gain_three = jnp.sum(gain_rows, axis=(0, 1))
    grad_stream = grad_stream + grad_norm
    grad_branch = grad_whole((row_keep * grad_stream).astype(jnp.bfloat16)).reshape(
        tokens, model_width
    )
    grad_merge = jnp.einsum(
        "te,td->ed", mixed_two.reshape(tokens, -1), grad_branch, preferred_element_type=jnp.float32
    )
    grad_mixed = jnp.einsum(
        "td,ed->te", grad_branch, full_cross_out, preferred_element_type=jnp.float32
    )
    grad_mixed = grad_mixed.astype(jnp.bfloat16).reshape(seq_count, padded, -1)
    grad_query, grad_key, grad_value = lax.map(
        attend_backward,
        (cross_rows, context_rows[0], context_rows[1], logsum_two, grad_mixed, context_valid),
    )
    grad_cross = jnp.einsum(
        "td,te->de", whole_two, grad_query.reshape(tokens, -1), preferred_element_type=jnp.float32
    )
    grad_pairs = jnp.stack([grad_key, grad_value])
    grad_context_proj = jnp.einsum(
        "scd,ksce->kde", context, grad_pairs, preferred_element_type=jnp.float32
    )
    context_part = jnp.einsum(
        "ksce,kde->scd", grad_pairs, full_cross_context, preferred_element_type=jnp.float32
    )
    partial_value = jnp.einsum(
        "te,de->td",
        grad_query.reshape(tokens, -1),
        full_cross_query,
        preferred_element_type=jnp.float32,
    )
    grad_norm, gain_rows = norm_back(
        grad_share(partial_value.reshape(seq_count, padded, model_width)),
        scaled_two,
        inverse_two,
        norm_gains[1],
    )
    gain_two = jnp.sum(gain_rows, axis=(0, 1))
    grad_stream = grad_stream + grad_norm
    grad_branch = grad_whole((row_keep * grad_stream).astype(jnp.bfloat16)).reshape(
        tokens, model_width
    )
    grad_after = jnp.einsum(
        "te,td->ed", mixed_one.reshape(tokens, -1), grad_branch, preferred_element_type=jnp.float32
    )
    grad_mixed = jnp.einsum(
        "td,ed->te", grad_branch, full_self_out, preferred_element_type=jnp.float32
    )
    grad_mixed = grad_mixed.astype(jnp.bfloat16).reshape(seq_count, padded, -1)
    grad_query, grad_key, grad_value = lax.map(
        attend_backward, (qkv_rows[0], qkv_rows[1], qkv_rows[2], logsum_one, grad_mixed, key_valid)
    )
    grad_triple = jnp.stack([grad_query, grad_key, grad_value]).reshape(3, tokens, -1)
    grad_self = jnp.einsum(
        "td,cte->cde", whole_one, grad_triple, preferred_element_type=jnp.float32
    )
    partial_value = jnp.einsum(
        "cte,cde->td", grad_triple, full_self_qkv, preferred_element_type=jnp.float32
    )
    grad_norm, gain_rows = norm_back(
        grad_share(partial_value.reshape(seq_count, padded, model_width)),
        scaled_one,
        inverse_one,
        norm_gains[0],
    )
    gain_one = jnp.sum(gain_rows, axis=(0, 1))
    grad_inputs = grad_stream + grad_norm
    gain_partial = jnp.stack([gain_one, gain_two, gain_three])
    gain_total, grad_context = (
        lax.psum(gain_partial.astype(jnp.bfloat16), "tensor").astype(jnp.float32),
        lax.psum(context_part.astype(jnp.bfloat16), "tensor").astype(jnp.float32),
    )
    result_grads = (
        lax.psum_scatter(
            grad_self.astype(jnp.bfloat16), "dp", scatter_dimension=1, tiled=True
        ).astype(jnp.float32),
        lax.psum_scatter(
            grad_after.astype(jnp.bfloat16), "dp", scatter_dimension=1, tiled=True
        ).astype(jnp.float32),
        lax.psum_scatter(
            grad_cross.astype(jnp.bfloat16), "dp", scatter_dimension=0, tiled=True
        ).astype(jnp.float32),
        lax.psum_scatter(
            grad_context_proj.astype(jnp.bfloat16), "dp", scatter_dimension=1, tiled=True
        ).astype(jnp.float32),
        lax.psum_scatter(
            grad_merge.astype(jnp.bfloat16), "dp", scatter_dimension=1, tiled=True
        ).astype(jnp.float32),
        lax.psum_scatter(
            grad_gates.astype(jnp.bfloat16), "dp", scatter_dimension=1, tiled=True
        ).astype(jnp.float32),
        lax.psum_scatter(
            grad_down.astype(jnp.bfloat16), "dp", scatter_dimension=1, tiled=True
        ).astype(jnp.float32),
        lax.psum_scatter(
            gain_total.astype(jnp.bfloat16), "dp", scatter_dimension=1, tiled=True
        ).astype(jnp.float32),
    )
    return (
        output,
        grad_inputs,
        grad_context,
        result_grads[0],
        result_grads[1],
        result_grads[2],
        result_grads[3],
        result_grads[4],
        result_grads[5],
        result_grads[6],
        result_grads[7],
    )


CORE, XBIT, YBIT = 1, 2, 4
BF = jnp.bfloat16
F32 = jnp.float32


def swap(value, bit):
    count = lax.axis_size("dp")
    return lax.ppermute(value, "dp", [(i, i ^ bit) for i in range(count)])


def take(value, index, axis):
    return lax.dynamic_index_in_dim(value, index, axis, keepdims=False)


def ordered(place, mine, theirs, axis):
    low = jnp.where(place == 0, mine, theirs)
    high = jnp.where(place == 0, theirs, mine)
    return jnp.stack([low, high], axis)


def added(mine, theirs):
    return mine.astype(F32) + theirs.astype(F32)


def plane_sums(partial_value):
    blocks = partial_value.astype(BF).reshape(4, 2, -1, partial_value.shape[-1])
    upper, lower = blocks[:, 0], blocks[:, 1]
    got = swap(jnp.stack([upper[1], upper[3]]), XBIT)
    upper_near, upper_far = added(upper[0], got[0]), added(upper[2], got[1])
    got = swap(jnp.stack([lower[2], lower[3]]), YBIT)
    lower_near, lower_far = added(lower[0], got[0]), added(lower[1], got[1])
    upper_sum = added(upper_near, swap(upper_far.astype(BF), YBIT))
    lower_sum = added(lower_near, swap(lower_far.astype(BF), XBIT))
    return jnp.concatenate([upper_sum, lower_sum])


MESH = pl.DeviceIdType.MESH


def spot():
    dp, z = lax.axis_index("dp"), lax.axis_index("tensor")
    return dp, dp // 2, dp % 2, z


def greet(devices):
    barrier = pltpu.get_barrier_semaphore()
    for dp, z in devices:
        pl.semaphore_signal(
            barrier, inc=1, device_id={"dp": dp, "tensor": z}, device_id_type=MESH
        )
    pl.semaphore_wait(barrier, len(devices))


def flip(dp, bit):
    bits = {1: dp % 2, 2: dp // 2 % 2, 4: dp // 4 % 2}
    return dp + bit * (1 - 2 * bits[bit])


def plane_mates(dp, z):
    return [(flip(dp, 2), z), (flip(dp, 4), z), (flip(flip(dp, 2), 4), z)]


def column_mates(dp, z):
    mates = [(flip(dp, 1), z)]
    for step in range(1, 4):
        far = lax.rem(z + step, 4)
        mates += [(dp, far), (flip(dp, 1), far)]
    return mates


def push(source, target, send, recv, device):
    dp, z = device
    return pltpu.make_async_remote_copy(
        src_ref=source,
        dst_ref=target,
        send_sem=send,
        recv_sem=recv,
        device_id={"dp": dp, "tensor": z},
        device_id_type=MESH,
    )


def any_specs(count):
    return [pl.BlockSpec(memory_space=pl.ANY)] * count


def near_specs(count):
    return [pl.BlockSpec(memory_space=pltpu.VMEM)] * count


ROOM = 56 << 20


def dma(*shape):
    return pltpu.SemaphoreType.DMA(shape)


def forward_pair(queries, keys_in, values, valid):
    lane = lax.broadcasted_iota(jnp.int32, (1, 2 * HD), 1)
    total = None
    for side in range(2):
        only = jnp.where(lane // HD == side, 1.0, 0.0)
        picked = (queries.astype(F32) * (only * HD ** (-0.5))).astype(BF)
        turned = (values.astype(F32) * only).T.astype(BF)
        scores = lax.dot_general(
            keys_in, picked, (((1,), (1,)), ((), ())), preferred_element_type=F32
        )
        scores = jnp.where(valid, scores, NEGATIVE)
        exponent = jnp.exp(scores - jnp.max(scores, axis=0, keepdims=True))
        share = 1.0 / jnp.sum(exponent, axis=0, keepdims=True)
        mixed = jnp.dot(turned, exponent.astype(BF), preferred_element_type=F32) * share
        total = mixed if total is None else total + mixed
    return total.T.astype(BF)


class RowsIn:
    def __init__(self, source, target, sems):
        self.source, self.target = source, target
        self.send, self.recv, self.send_on, self.recv_on, self.keep = sems
        self.dp, self.plane, self.core, self.z = spot()
        self.sibling = (flip(self.dp, 1), self.z)
        self.home = self.z // 2 == self.core

    def stays(self, s):
        return jnp.logical_and(self.home, self.z % 2 == s)

    def depart(self):
        for s in range(2):

            @pl.when(jnp.logical_not(self.stays(s)))
            def _(s=s):
                goal = (self.plane * 2 + self.z // 2, 2 * self.core + s)
                push(
                    self.source.at[s],
                    self.target.at[self.z],
                    self.send.at[s],
                    self.recv.at[self.z % 2],
                    goal,
                ).start()

            @pl.when(self.stays(s))
            def _(s=s):
                pltpu.make_async_copy(
                    self.source.at[s], self.target.at[self.z], self.keep.at[0]
                ).start()

    def onward(self, j, core):
        place = self.target.at[2 * core + j]
        return push(place, place, self.send_on.at[j], self.recv_on.at[j], self.sibling)

    def forward(self):
        for j in range(2):
            place = self.target.at[2 * self.core + j]
            mine = jnp.logical_and(self.home, 2 * self.core + j == self.z)

            @pl.when(mine)
            def _():
                pltpu.make_async_copy(self.source.at[0], place, self.keep.at[0]).wait()

            @pl.when(jnp.logical_not(mine))
            def _(j=j):
                push(
                    self.source.at[0], place, self.send.at[0], self.recv.at[j], self.sibling
                ).wait_recv()

            self.onward(j, self.core).start()

    def settle(self):
        for j in range(2):
            self.onward(j, 1 - self.core).wait_recv()

    def finish(self):
        for j in range(2):
            self.onward(j, self.core).wait_send()

            @pl.when(jnp.logical_not(self.stays(j)))
            def _(j=j):
                push(
                    self.source.at[j],
                    self.target.at[self.z],
                    self.send.at[j],
                    self.recv.at[0],
                    self.sibling,
                ).wait_send()


class PlaneRows:
    def __init__(self, target, send, recv):
        self.target, self.send, self.recv = target, send, recv
        dp, _, _, z = spot()
        self.xmate, self.ymate, _ = plane_mates(dp, z)

    def copy(self, near, part, chip, slot, mate):
        return push(
            self.target.at[near, part],
            self.target.at[chip, part],
            self.send.at[slot],
            self.recv.at[slot],
            mate,
        )

    def hop(self, slot):
        near, part, chip, mate = [
            (0, 0, 1, self.xmate),
            (0, 1, 2, self.ymate),
            (0, 0, 2, self.ymate),
            (0, 1, 1, self.xmate),
            (1, 0, 3, self.ymate),
            (2, 1, 3, self.xmate),
        ][slot]
        return self.copy(near, part, chip, slot, mate)

    def start(self):
        for slot in range(4):
            self.hop(slot).start()

    def relay(self):
        for slot in range(2):
            self.hop(slot).wait_recv()
            self.hop(4 + slot).start()

    def finish(self):
        for slot in range(2, 6):
            self.hop(slot).wait_recv()
        for slot in range(6):
            self.hop(slot).wait_send()


def weights_kernel(
    shard_ref,
    units_ref,
    rows_ref,
    cot_ref,
    size_ref,
    cond_ref,
    gain_ref,
    *refs,
    groups,
    wides,
    tokens,
):
    count = len(groups)
    arrays = max(which for which, _ in groups) + 1
    whole_refs, refs = refs[:arrays], refs[arrays:]
    wide_refs, refs = refs[:2], refs[1:]
    one_ref, qkv_ref, mixed_ref, stream_ref, two_ref, query_ref, pair_ref, crossed_ref = refs[1:9]
    after_ref, all_ref, seq_ref, grad_ref, grads_ref, keep_ref, conds_ref = refs[9:16]
    held, part_out, part_in, three, block_ref, sizes = refs[16:22]
    send_e, recv_e, send_n, recv_n, held_sem = refs[22:27]
    send_s, recv_s, send_z, recv_z, send_p, recv_p, local = refs[27:34]
    send_w, recv_w, send_v, recv_v, local_w = refs[34:39]
    stream_rows = RowsIn(rows_ref, seq_ref, refs[39:44])
    grad_rows = RowsIn(cot_ref, grad_ref, refs[44:49])
    send_b, recv_b, send_d, recv_d, send_q, recv_q, keep_sem = refs[49:]
    dp, plane, core, z = spot()
    width = shard_ref.shape[2]
    sibling = (flip(dp, 1), z)
    xmate, ymate, far = plane_mates(dp, z)
    greet(plane_mates(dp, z) + column_mates(dp, z))
    home = z // 2 == core
    above, below = (dp, z + 1), (dp, z - 1)
    stream_rows.depart()
    units = [
        push(
            units_ref.at[:, mate[0] // 2],
            block_ref.at[:, plane],
            send_b.at[slot],
            recv_b.at[slot],
            mate,
        )
        for slot, mate in enumerate([xmate, ymate, far])
    ]
    units_own = pltpu.make_async_copy(
        units_ref.at[:, plane], block_ref.at[:, plane], keep_sem.at[0]
    )
    small = [
        push(size_ref, sizes.at[core], send_d.at[0], recv_d.at[0], sibling),
        push(cond_ref, conds_ref.at[core], send_d.at[1], recv_d.at[1], sibling),
    ]
    small_own = [
        pltpu.make_async_copy(size_ref, sizes.at[core], keep_sem.at[1]),
        pltpu.make_async_copy(cond_ref, conds_ref.at[core], keep_sem.at[2]),
    ]

    def columns(which):
        return pl.ds(pl.multiple_of(which * width, width), width)

    def slab(g):
        array, index = groups[g]
        return whole_refs[array].at[index]

    for g in range(count):
        target = slab(g).at[plane, core, :, columns(z % 2)]

        @pl.when(home)
        def _(g=g, target=target):
            pltpu.make_async_copy(shard_ref.at[g], target, local.at[g]).start()

        @pl.when(jnp.logical_not(home))
        def _(g=g, target=target):
            push(shard_ref.at[g], target, send_s.at[g], recv_s.at[g], sibling).start()

    for copy in small + small_own + units + [units_own]:
        copy.start()

    near = jnp.where(core == 0, jnp.where(z >= 1, 1, 0), jnp.where(z <= 2, 0, 1))

    def order(turn):
        return near if turn == 0 else 1 - near

    def area(g, which, chip):
        return slab(g).at[chip, :, :, columns(which)]

    def on_z(g, turn, act):
        which = order(turn)
        source_z = 2 * core + which
        place = area(g, which, plane)
        for way, (wanted, target) in enumerate(
            [
                (jnp.logical_and(z >= source_z, z < 3), above),
                (jnp.logical_and(z <= source_z, z > 0), below),
            ]
        ):

            @pl.when(wanted)
            def _(way=way, target=target):
                act(push(place, place, send_z.at[g, turn, way], recv_z.at[g, which], target))

    def arrive(g, turn):
        which = order(turn)
        source_z = 2 * core + which

        @pl.when(z == source_z)
        def _():
            mine = slab(g).at[plane, core, :, columns(which)]
            other = slab(g).at[plane, 1 - core, :, columns(which)]
            pltpu.make_async_copy(shard_ref.at[g], mine, local.at[g]).wait()
            push(mine, other, send_s.at[g], recv_s.at[g], sibling).wait_recv()

        @pl.when(z != source_z)
        def _():
            place = area(g, which, plane)
            push(place, place, send_z.at[g, turn, 0], recv_z.at[g, which], sibling).wait_recv()

    def hop(g, turn, chip, slot, mate):
        place = area(g, order(turn), chip)
        return push(place, place, send_p.at[g, turn, slot], recv_p.at[g, turn, slot], mate)

    mates = (xmate, ymate)

    def spread(g, turn):
        arrive(g, turn)
        on_z(g, turn, lambda copy: copy.start())
        hop(g, turn, plane, turn, mates[turn]).start()
        hop(g, turn, plane, 1 - turn, mates[1 - turn]).start()

    def relay(g, turn):
        chip = mates[turn][0] // 2
        hop(g, turn, chip, turn, mates[turn]).wait_recv()
        hop(g, turn, chip, 2, mates[1 - turn]).start()

    wide_width = block_ref.shape[3]

    def quarter(k, block, side):
        spots = pl.ds(pl.multiple_of(block * wide_width, wide_width), wide_width)
        return wide_refs[k // 2].at[k % 2, :, side, :, spots]

    def wide_copy(k, block, way, target):
        place = quarter(k, block, core)
        return push(place, place, send_w.at[k, block, way], recv_w.at[k, block], target)

    def to_sibling(k, block, side):
        place = quarter(k, block, side)
        return push(place, place, send_v.at[k, block], recv_v.at[k, block], sibling)

    def wide_own(k):
        pltpu.make_async_copy(block_ref.at[k], quarter(k, z, core), local_w.at[k]).start()
        pltpu.make_async_copy(block_ref.at[k], quarter(k, z, core), local_w.at[k]).wait()
        for way, (wanted, target) in enumerate([(z < 3, above), (z > 0, below)]):

            @pl.when(wanted)
            def _(way=way, target=target):
                wide_copy(k, z, way, target).start()

        to_sibling(k, z, core).start()

    def wide_step(k, step):
        for way, (block, wanted, further, target) in enumerate(
            [
                (z - step, z - step >= 0, z < 3, above),
                (z + step, z + step <= 3, z > 0, below),
            ]
        ):

            @pl.when(wanted)
            def _(block=block, way=way, target=target):
                wide_copy(k, block, way, target).wait_recv()
                to_sibling(k, block, core).start()

            @pl.when(jnp.logical_and(wanted, further))
            def _(block=block, way=way, target=target):
                wide_copy(k, block, way, target).start()


    def both(step, g):
        step(g, 0)
        step(g, 1)

    def settle(g):
        for turn in range(2):
            hop(g, turn, mates[1 - turn][0] // 2, 1 - turn, mates[1 - turn]).wait_recv()
            hop(g, turn, far[0] // 2, 2, mates[1 - turn]).wait_recv()
        copy = pltpu.make_async_copy(slab(g), held.at[g % 2], held_sem.at[g % 2])
        copy.start()
        copy.wait()

    height = seq_ref.shape[0] * seq_ref.shape[1]
    model_width = seq_ref.shape[2]
    half = height // 2
    tile = 256

    def norm(value, which):
        centred = value - jnp.mean(value, axis=1, keepdims=True)
        inverse = lax.rsqrt(jnp.mean(centred * centred, axis=1, keepdims=True) + EPSILON)
        return (centred * inverse * gain_ref[which : which + 1]).astype(BF)

    def project(g, source, put):
        def body(step, carry):
            rows = source.shape[0] // 2
            lines = pl.ds(pl.multiple_of(step // 3 * rows, 16), rows)
            spots = pl.ds(pl.multiple_of(step % 3 * tile, tile), tile)
            weight = held[g % 2, :, :, :, spots].reshape(model_width, tile)
            put(lines, spots, jnp.dot(source[lines, :], weight, preferred_element_type=F32).astype(BF))
            return carry

        lax.fori_loop(0, 6, body, 0)

    def give(g, source, turn):
        def body(step, carry):
            lines = pl.ds(pl.multiple_of(step // 4 * half, 16), half)
            chip = step % 4
            span = model_width // 4
            weight = held[g % 2, chip].reshape(span, -1)
            value = lax.dot_general(
                source[lines, :], weight, (((1,), (1,)), ((), ())), preferred_element_type=F32
            )
            spots = pl.ds(pl.multiple_of(chip * span, 128), span)
            part_out[turn, lines, spots] = value.astype(BF)
            return carry

        lax.fori_loop(0, 8, body, 0)
        exchange(turn).start()

    def exchange(turn):
        return push(part_out.at[turn], part_in.at[turn], send_e.at[turn], recv_e.at[turn], sibling)

    slices = height // 32

    def first_norm():
        for part in range(seq_ref.shape[0]):
            lines = slice(part * seq_ref.shape[1], (part + 1) * seq_ref.shape[1])
            stream_ref[lines, :] = seq_ref[part].astype(F32)

        def body(i, carry):
            lines = pl.ds(pl.multiple_of(i * 32, 32), 32)
            one_ref[lines, :] = norm(stream_ref[lines, :], 0)
            return carry

        lax.fori_loop(0, slices, body, 0)

    def summed(lines, turn):
        both_parts = part_out[turn, lines, :].astype(F32) + part_in[turn, lines, :].astype(F32)
        return stream_ref[lines, :] + keep_ref[lines, :1] * both_parts

    def second_norm():
        exchange(0).wait_recv()

        def body(i, carry):
            lines = pl.ds(pl.multiple_of(i * 32, 32), 32)
            value = summed(lines, 0)
            stream_ref[lines, :] = value
            two_ref[lines, :] = norm(value, 1)
            return carry

        lax.fori_loop(0, slices, body, 0)

    def third_norm():
        count_rows = half // 2
        for j in range(2):

            def body(i, carry, j=j):
                start = pl.multiple_of(i * 8, 8)
                lines = pl.ds(pl.multiple_of(core * half + j * count_rows + i * 8, 8), 8)
                added = three[pl.ds(pl.multiple_of(j * count_rows + i * 8, 8), 8), :]
                value = stream_ref[lines, :] + keep_ref[lines, :1] * added
                after_ref[j, pl.ds(start, 8), :] = value
                return carry

            lax.fori_loop(0, count_rows // 8, body, 0)
            all_ref[0, j] = norm(after_ref[j], 2)

    def unpack():
        def body(i, carry):
            lines = pl.ds(pl.multiple_of(core * half + i * 16, 16), 16)
            value = part_out[1, lines, :].astype(F32) + part_in[1, lines, :].astype(F32)
            three[pl.ds(pl.multiple_of(i * 16, 16), 16), :] = value
            return carry

        lax.fori_loop(0, half // 16, body, 0)

    def own_heads(pair, carry):
        lanes = pl.ds(pl.multiple_of(pair * 128, 128), 128)
        mixed_ref[:, lanes] = forward_pair(
            qkv_ref[0, :, lanes], qkv_ref[1, :, lanes], qkv_ref[2, :, lanes], keep_ref[:, :1] > 0.0
        )
        return carry

    def cross_heads(pair, carry):
        lanes = pl.ds(pl.multiple_of(pair * 128, 128), 128)
        line = lax.broadcasted_iota(jnp.int32, (pair_ref.shape[1], 1), 0)
        crossed_ref[:, lanes] = forward_pair(
            query_ref[:, lanes], pair_ref[0, :, lanes], pair_ref[1, :, lanes], line < tokens
        )
        return carry

    pairs = qkv_ref.shape[2] // 128

    def put_in(target):
        def put(lines, spots, value):
            target[lines, spots] = value

        return put

    def put_cond(which):
        def body(step, carry):
            spots = pl.ds(pl.multiple_of(step * tile, tile), tile)
            weight = held[5 % 2, :, :, :, spots].reshape(model_width, tile)
            value = jnp.dot(conds_ref[z // 2, which], weight, preferred_element_type=F32)
            pair_ref[which, :, spots] = value.astype(BF)
            return carry

        lax.fori_loop(0, 3, body, 0)

    def set_keep():
        for copy in small_own:
            copy.wait()
        for copy in small:
            copy.wait()
        line = lax.broadcasted_iota(jnp.int32, keep_ref.shape, 0)
        keep_ref[...] = jnp.where(line < sizes[z // 2, :1, :], 1.0, 0.0)

    def set_grads():
        for j in range(2):
            lines = pl.ds(pl.multiple_of((2 * core + j) * grad_ref.shape[1], 8), grad_ref.shape[1])
            value = grad_ref[2 * core + j].astype(F32) * keep_ref[lines, :1]
            grads_ref[0, j] = value.astype(BF)

    plane_norms = PlaneRows(all_ref, send_n, recv_n)
    plane_grads = PlaneRows(grads_ref, send_q, recv_q)

    both(spread, 0)
    stream_rows.forward()
    set_keep()
    stream_rows.settle()
    first_norm()
    both(spread, 1)
    both(spread, 2)
    both(relay, 0)
    both(spread, 3)
    both(relay, 1)
    both(spread, 4)
    settle(0)
    project(0, one_ref, put_in(qkv_ref.at[0]))
    both(relay, 2)
    both(spread, 5)
    both(spread, 6)
    grad_rows.depart()
    for copy in units:
        copy.wait()
    units_own.wait()
    wide_own(0)
    settle(1)
    project(1, one_ref, put_in(qkv_ref.at[1]))
    both(relay, 3)
    wide_own(1)
    settle(2)
    project(2, one_ref, put_in(qkv_ref.at[2]))
    both(relay, 4)
    wide_own(2)
    lax.fori_loop(0, pairs, own_heads, 0)
    wide_step(0, 1)
    grad_rows.forward()
    set_grads()
    plane_grads.start()
    both(relay, 5)
    settle(3)
    give(3, mixed_ref, 0)
    wide_step(1, 1)
    both(relay, 6)
    second_norm()
    wide_step(2, 1)
    plane_grads.relay()
    settle(4)
    project(4, two_ref, put_in(query_ref))
    wide_step(0, 2)
    settle(5)
    put_cond(0)
    put_cond(1)
    lax.fori_loop(0, pairs, cross_heads, 0)
    wide_step(1, 2)
    settle(6)
    give(6, crossed_ref, 1)
    wide_step(2, 2)
    exchange(1).wait_recv()
    unpack()
    third_norm()
    plane_norms.start()
    wide_step(0, 3)
    plane_norms.relay()
    wide_step(1, 3)
    wide_step(2, 3)
    grad_rows.settle()
    plane_grads.finish()
    plane_norms.finish()
    grad_rows.finish()
    stream_rows.finish()
    for turn in range(2):
        exchange(turn).wait_send()
    for g in range(count):
        for turn in range(2):
            for slot in range(3):
                hop(g, turn, plane, slot, xmate).wait_send()
            on_z(g, turn, lambda copy: copy.wait_send())

        @pl.when(jnp.logical_not(home))
        def _(g=g):
            push(shard_ref.at[g], shard_ref.at[g], send_s.at[g], recv_s.at[g], sibling).wait_send()

    for k in range(wides):
        for block in range(4):
            to_sibling(k, block, core).wait_send()
            to_sibling(k, block, 1 - core).wait_recv()

            @pl.when(jnp.logical_and(block <= z, z < 3))
            def _(k=k, block=block):
                wide_copy(k, block, 0, above).wait_send()

            @pl.when(jnp.logical_and(block >= z, z > 0))
            def _(k=k, block=block):
                wide_copy(k, block, 1, below).wait_send()


def weights_moves(shard, units, rows, cot, size, cond, gains, groups, tokens):
    count, depth, width = shard.shape
    sizes = [0] * (max(which for which, _ in groups) + 1)
    for which, _ in groups:
        sizes[which] += 1
    wides, chips, _, unit = units.shape
    _, block, model_width = rows.shape
    height, columns = 4 * block, 2 * width
    like = jax.ShapeDtypeStruct
    row_sems = [dma(2), dma(2), dma(2), dma(2), dma(1)]
    out = pl.pallas_call(
        functools.partial(weights_kernel, groups=groups, wides=wides, tokens=tokens),
        out_shape=[like((slabs, 4, 2, depth, columns), BF) for slabs in sizes]
        + [
            like((2, chips, 2, depth, 4 * unit), BF),
            like((wides - 2, chips, 2, depth, 4 * unit), BF),
            like((height, model_width), BF),
            like((3, height, columns), BF),
            like((height, columns), BF),
            like((height, model_width), F32),
            like((height, model_width), BF),
            like((height, columns), BF),
            like((2, cond.shape[1], columns), BF),
            like((height, columns), BF),
            like((2, block, model_width), F32),
            like((4, 2, block, model_width), BF),
            like((4, block, model_width), BF),
            like((4, block, model_width), BF),
            like((4, 2, block, model_width), BF),
            like((height, 128), F32),
            like((2, *cond.shape), BF),
        ],
        in_specs=near_specs(7),
        out_specs=any_specs(len(sizes) + 2) + near_specs(15),
        scratch_shapes=[
            pltpu.VMEM((2, 4, 2, depth, columns), BF),
            pltpu.VMEM((2, height, model_width), BF),
            pltpu.VMEM((2, height, model_width), BF),
            pltpu.VMEM((2 * block, model_width), F32),
            pltpu.VMEM(units.shape, BF),
            pltpu.VMEM((2, *size.shape), size.dtype),
            dma(2),
            dma(2),
            dma(6),
            dma(6),
            dma(2),
            dma(count),
            dma(count),
            dma(count, 2, 2),
            dma(count, 2),
            dma(count, 2, 3),
            dma(count, 2, 3),
            dma(count),
            dma(wides, 4, 2),
            dma(wides, 4),
            dma(wides, 4),
            dma(wides, 4),
            dma(wides),
            *row_sems,
            *row_sems,
            dma(3),
            dma(3),
            dma(2),
            dma(2),
            dma(6),
            dma(6),
            dma(3),
        ],
        compiler_params=pltpu.CompilerParams(
            collective_id=2, has_side_effects=True, vmem_limit_bytes=60 << 20
        ),
        name="weights_moves",
    )(shard, units, rows, cot, size, cond, gains)
    weights = out[: len(sizes) + 2]
    return [
        whole.reshape(whole.shape[0], 8 * depth, whole.shape[-1]) for whole in weights
    ], out[len(sizes) + 2 :]


def third_kernel(
    part_ref, *refs, counts
):
    many = len(counts)
    grad_refs = refs[:many]
    sum_ref, quarter_ref = refs[many : many + 2]
    got, far_x, far_y, own, theirs = refs[many + 2 : many + 7]
    send_r, recv_r, send_w, recv_w, load, store = refs[many + 7 :]
    dp, plane, core, z = spot()
    sibling = (flip(dp, 1), z)
    xmate, ymate, _ = plane_mates(dp, z)
    greet([sibling, xmate, ymate])

    def rows(source, slot, mate):
        return push(source, got.at[slot], send_r.at[slot], recv_r.at[slot], mate)

    first = [
        rows(part_ref.at[3, 0], 0, xmate),
        rows(part_ref.at[3, 1], 1, ymate),
        rows(part_ref.at[1, 0], 2, xmate),
        rows(part_ref.at[2, 1], 3, ymate),
    ]
    for copy in first:
        copy.start()
    wide, loads, base = [], [], 0
    for grad, count in zip(grad_refs, counts, strict=True):
        for k in range(count):
            slot = base + k
            wide.append(
                push(grad.at[k, :, 1 - core], theirs.at[slot], send_w.at[slot], recv_w.at[slot], sibling)
            )
            loads.append(pltpu.make_async_copy(grad.at[k, :, core], own.at[slot], load.at[slot]))
        base += count
    for copy in wide + loads:
        copy.start()
    slabs = base
    chips, depth, width = own.shape[1:]
    unit = width // 4

    def core_sums(slot):
        loads[slot].wait()
        wide[slot].wait_recv()

        def body(chip, carry):
            own[slot, chip] = own[slot, chip] + theirs[slot, chip]
            return carry

        lax.fori_loop(0, chips, body, 0)
        for block in range(4):
            pltpu.make_async_copy(
                own.at[slot, :, :, pl.ds(block * unit, unit)],
                quarter_ref.at[block, slot],
                store.at[slot, block],
            ).start()

    core_sums(0)
    first[0].wait_recv()
    far_x[...] = (part_ref[2, 0].astype(F32) + got[0].astype(F32)).astype(BF)
    upper = rows(far_x, 4, ymate)
    upper.start()
    first[1].wait_recv()
    far_y[...] = (part_ref[1, 1].astype(F32) + got[1].astype(F32)).astype(BF)
    lower = rows(far_y, 5, xmate)
    lower.start()
    for slot in range(1, slabs):
        core_sums(slot)
    first[2].wait_recv()
    first[3].wait_recv()
    upper.wait_recv()
    sum_ref[0] = part_ref[0, 0].astype(F32) + got[2].astype(F32) + got[4].astype(F32)
    lower.wait_recv()
    sum_ref[1] = part_ref[0, 1].astype(F32) + got[3].astype(F32) + got[5].astype(F32)
    for copy in first + wide + [upper, lower]:
        copy.wait_send()
    for slot in range(slabs):
        for block in range(4):
            pltpu.make_async_copy(
                own.at[slot, :, :, pl.ds(block * unit, unit)],
                quarter_ref.at[block, slot],
                store.at[slot, block],
            ).wait()


def third_moves(part, grads):
    _, _, height, width = part.shape
    counts = tuple(grad.shape[0] for grad in grads)
    slabs = sum(counts)
    depth, units = grads[0].shape[1] // 8, grads[0].shape[2]
    return pl.pallas_call(
        functools.partial(third_kernel, counts=counts),
        out_shape=[
            jax.ShapeDtypeStruct((2, height, width), F32),
            jax.ShapeDtypeStruct((4, slabs, 4, depth, units // 4), BF),
        ],
        in_specs=near_specs(1) + any_specs(len(grads)),
        out_specs=near_specs(1) + any_specs(1),
        scratch_shapes=[
            pltpu.VMEM((6, height, width), BF),
            pltpu.VMEM((height, width), BF),
            pltpu.VMEM((height, width), BF),
            pltpu.VMEM((slabs, 4, depth, units), BF),
            pltpu.VMEM((slabs, 4, depth, units), BF),
            dma(6),
            dma(6),
            dma(slabs),
            dma(slabs),
            dma(slabs),
            dma(slabs, 4),
        ],
        compiler_params=pltpu.CompilerParams(
            collective_id=4, has_side_effects=True, vmem_limit_bytes=ROOM
        ),
        name="third_moves",
    )(part, *[grad.reshape(grad.shape[0], 4, 2, depth, units) for grad in grads])


def backward_pair(queries, keys_in, values, grads, valid):
    lane = lax.broadcasted_iota(jnp.int32, (1, 2 * HD), 1)
    totals = [None, None, None]
    for side in range(2):
        only = jnp.where(lane // HD == side, 1.0, 0.0)
        picked = (queries.astype(F32) * (only * HD ** (-0.5))).astype(BF)
        given = (grads.astype(F32) * only).astype(BF)
        turned = (keys_in.astype(F32) * only).T.astype(BF)
        rows_rows = (((1,), (1,)), ((), ()))
        scores = lax.dot_general(keys_in, picked, rows_rows, preferred_element_type=F32)
        scores = jnp.where(valid, scores, NEGATIVE)
        exponent = jnp.exp(scores - jnp.max(scores, axis=0, keepdims=True))
        probs = exponent * (1.0 / jnp.sum(exponent, axis=0, keepdims=True))
        grad_probs = lax.dot_general(values, given, rows_rows, preferred_element_type=F32)
        inner = jnp.sum(probs * grad_probs, axis=0, keepdims=True)
        grad_scores = (probs * (grad_probs - inner)).astype(BF)
        new = (
            jnp.dot(turned, grad_scores, preferred_element_type=F32).T * HD ** (-0.5),
            jnp.dot(grad_scores, picked, preferred_element_type=F32),
            jnp.dot(probs.astype(BF), given, preferred_element_type=F32),
        )
        totals = [b if a is None else a + b for a, b in zip(totals, new, strict=True)]
    return [total.astype(BF) for total in totals]


def share_kernel(*refs, arrays):
    count = arrays + 3
    grad_refs, refs = refs[:arrays], refs[arrays:]
    (
        qkv_ref,
        mixed_ref,
        valid_ref,
        turned_ref,
        whole_ref,
        stream_ref,
        scaled_ref,
        inverse_ref,
        factor_ref,
        first_ref,
        gain_in,
        cond_ref,
    ) = refs[:12]
    out_ref, back_ref, gain_out, cond_out = refs[12:16]
    one, got, two, line, gain_got, gain_ref, gain_sum, gain_line = refs[16:24]
    made, whole, thirds, part_out, part_in, part_own, rows_ref = refs[24:31]
    (
        load,
        send_x,
        recv_x,
        send_y,
        recv_y,
        send_z,
        recv_z,
        send_c,
        recv_c,
        send_r,
        recv_r,
        send_g,
        recv_g,
        send_h,
        recv_h,
        send_k,
        recv_k,
        local,
        extra,
    ) = refs[31:]
    dp, plane, core, z = spot()
    xbit, ybit = plane % 2, plane // 2
    sibling = (flip(dp, 1), z)
    xmate, ymate, _ = plane_mates(dp, z)
    plane_all = [(lax.rem(dp + step, 8), z) for step in range(1, 8)]
    greet(plane_all + column_mates(dp, z)[1:])
    home = z // 2 == core
    above, below = (dp, z + 1), (dp, z - 1)
    width = out_ref.shape[2]
    near = jnp.where(core == 0, jnp.where(z >= 1, 1, 0), jnp.where(z <= 2, 0, 1))
    mates = (xmate, ymate)

    def order(turn):
        return 1 - near if turn == 0 else near

    def columns(which):
        return pl.ds(pl.multiple_of(which * width, width), width)

    def strip(g, turn, bit):
        grid = grad_refs[g].at[0] if g < arrays else made.at[g - arrays]
        if turn == 0:
            return grid.at[:, bit, :, :, columns(order(turn))]
        return grid.at[bit, :, :, :, columns(order(turn))]

    bits = (xbit, ybit)

    def add_to(target, source):
        def body(part, carry):
            target[part] = target[part] + source[part]
            return carry

        lax.fori_loop(0, 2, body, 0)

    def step_one(g, turn):
        return push(
            strip(g, turn, 1 - bits[turn]), got.at[g, turn], send_x.at[g, turn], recv_x.at[g, turn], mates[turn]
        )

    def fetch(g, turn):
        return pltpu.make_async_copy(strip(g, turn, bits[turn]), one.at[g, turn], load.at[g, turn])

    def kept(g, turn, side):
        if g < arrays:
            return one.at[g, turn, side]
        grid = made.at[g - arrays]
        if turn == 0:
            return grid.at[side, xbit, :, :, columns(order(turn))]
        return grid.at[ybit, side, :, :, columns(order(turn))]

    def step_two(g, turn):
        return push(
            kept(g, turn, 1 - bits[1 - turn]),
            two.at[g, turn],
            send_y.at[g, turn],
            recv_y.at[g, turn],
            mates[1 - turn],
        )

    def after_one(g, turn):
        if g < arrays:
            fetch(g, turn).wait()
        step_one(g, turn).wait_recv()
        for side in range(2):
            add_to(kept(g, turn, side), got.at[g, turn, side])
        step_two(g, turn).start()

    def z_of(turn):
        return 2 * core + order(turn)

    def add_held(g, turn, source):
        add_to(kept(g, turn, bits[1 - turn]), source)

    def line_copy(g, turn, way, target):
        held = kept(g, turn, bits[1 - turn])
        which = order(turn)
        return push(held, line.at[g, which, way], send_z.at[g, turn], recv_z.at[g, which, way], target)

    def after_two(g, turn):
        step_two(g, turn).wait_recv()
        add_held(g, turn, two.at[g, turn])
        which, goal = order(turn), z_of(turn)

        @pl.when(jnp.logical_and(z > 0, z <= goal))
        def _():
            line_copy(g, turn, 0, above).wait_recv()
            add_held(g, turn, line.at[g, which, 0])

        @pl.when(jnp.logical_and(z < 3, z >= goal))
        def _():
            line_copy(g, turn, 1, below).wait_recv()
            add_held(g, turn, line.at[g, which, 1])

        @pl.when(z < goal)
        def _():
            line_copy(g, turn, 0, above).start()

        @pl.when(z > goal)
        def _():
            line_copy(g, turn, 1, below).start()

        @pl.when(z == goal)
        def _():
            held = kept(g, turn, bits[1 - turn])
            pltpu.make_async_copy(held.at[core], out_ref.at[g], local.at[g]).start()
            push(held.at[1 - core], out_ref.at[g], send_c.at[g], recv_c.at[g], sibling).start()

    for g in range(arrays):
        for turn in range(2):
            step_one(g, turn).start()
            fetch(g, turn).start()
    many = rows_ref.shape[0]

    def rows_leave(a):
        for j in range(2):
            stays = jnp.logical_and(home, 2 * core + j == z)

            @pl.when(stays)
            def _(j=j):
                pltpu.make_async_copy(
                    rows_ref.at[a, j], back_ref.at[a, z % 2], local.at[count + a]
                ).start()

            @pl.when(jnp.logical_not(stays))
            def _(j=j):
                target = (plane * 2 + z // 2, 2 * core + j)
                push(
                    rows_ref.at[a, j],
                    back_ref.at[a, z % 2],
                    send_r.at[a, j],
                    recv_r.at[a, z % 2],
                    target,
                ).start()

    rows_ref[0] = first_ref[...]
    rows_leave(0)

    @pl.when(home)
    def _():
        pltpu.make_async_copy(cond_ref, cond_out.at[z % 2], local.at[count + many]).start()
        for step in range(1, 4):
            target = (dp, lax.rem(z + step, 4))
            push(cond_ref, cond_out.at[z % 2], send_k.at[step], recv_k.at[z % 2], target).start()

    def heads(pair, carry):
        lanes = pl.ds(pl.multiple_of(pair * 128, 128), 128)
        grads = backward_pair(
            qkv_ref[0, :, lanes],
            qkv_ref[1, :, lanes],
            qkv_ref[2, :, lanes],
            mixed_ref[:, lanes],
            valid_ref[:, :1] > 0.0,
        )
        for i in range(3):
            thirds[i, :, lanes] = grads[i]
        return carry

    lax.fori_loop(0, qkv_ref.shape[2] // 128, heads, 0)

    def weight_grads(i):
        def body(block, carry):
            value = jnp.dot(turned_ref[block], thirds[i], preferred_element_type=F32)
            made[i, block // 4, block // 2 % 2, block % 2] = value.astype(BF)
            return carry

        lax.fori_loop(0, 8, body, 0)
        for turn in range(2):
            step_one(arrays + i, turn).start()

    half = thirds.shape[1] // 2
    tile = 256

    def row_grads(side, put):
        rows = pl.ds(pl.multiple_of(side * half, 16), half)
        blocks = whole_ref.shape[1] // tile

        def fill(block, slot):
            spots = pl.ds(pl.multiple_of(block * tile, tile), tile)
            return pltpu.make_async_copy(whole_ref.at[:, spots, :], whole.at[slot], extra.at[slot])

        fill(0, 0).start()

        def body(block, carry):
            slot = block % 2

            @pl.when(block + 1 < blocks)
            def _():
                fill(block + 1, 1 - slot).start()

            fill(block, slot).wait()
            spots = pl.ds(pl.multiple_of(block * tile, tile), tile)
            total = None
            for i in range(3):
                value = lax.dot_general(
                    thirds[i, rows, :],
                    whole[slot, i],
                    (((1,), (1,)), ((), ())),
                    preferred_element_type=F32,
                )
                total = value if total is None else total + value
            put(spots, total)
            return carry

        lax.fori_loop(0, blocks, body, 0)

    def put_out(spots, value):
        for j in range(2):
            part_out[j, :, spots] = value[j * (half // 2) : (j + 1) * (half // 2)].astype(BF)

    def put_own(spots, value):
        for j in range(2):
            part_own[j, :, spots] = value[j * (half // 2) : (j + 1) * (half // 2)]

    def ones(g):
        after_one(g, 0)
        after_one(g, 1)

    def twos(g):
        after_two(g, 0)
        after_two(g, 1)

    ones(0)
    weight_grads(0)
    ones(1)
    twos(0)
    weight_grads(1)
    weight_grads(2)
    ones(2)
    twos(1)
    row_grads(1 - core, put_out)
    parts = push(part_out, part_in, extra.at[3], extra.at[4], sibling)
    parts.start()
    row_grads(core, put_own)
    parts.wait()
    gain_one = jnp.zeros((1, part_own.shape[2]), F32)
    for j in range(2):
        value = part_own[j] + part_in[j].astype(F32)
        scaled = scaled_ref[j]
        grad_scaled = value * factor_ref[:1]
        centre = jnp.mean(grad_scaled, axis=1, keepdims=True)
        slope = jnp.mean(grad_scaled * scaled, axis=1, keepdims=True)
        moved = inverse_ref[j, :, :1] * (grad_scaled - centre - scaled * slope)
        rows_ref[1, j] = (stream_ref[j] + moved).astype(BF)
        gain_one = gain_one + jnp.sum(value * scaled, axis=0, keepdims=True)
    rows_leave(1)
    line_of = lax.broadcasted_iota(jnp.int32, gain_ref.shape, 0)
    gain_ref[...] = gain_in[...] + jnp.where(line_of == 0, gain_one, 0.0)
    gains = []
    for step in range(1, 8):
        mate = lax.rem(dp + step, 8)
        gains.append(
            push(gain_ref, gain_got.at[8 - step], send_g.at[step], recv_g.at[8 - step], (mate, z))
        )
    for copy in gains:
        copy.start()
    ones(3)
    twos(2)
    ones(4)
    twos(3)
    for copy in gains:
        copy.wait()
    total = gain_ref[...]
    for step in range(1, 8):
        total = total + gain_got[step]
    gain_sum[...] = total
    sums = []
    for step in range(1, 4):
        target = (dp, lax.rem(z + step, 4))
        sums.append(push(gain_sum, gain_line.at[4 - step], send_h.at[step], recv_h.at[4 - step], target))
    for copy in sums:
        copy.start()
    ones(5)
    twos(4)
    ones(6)
    twos(5)
    twos(6)

    for copy in sums:
        copy.wait()
    total = gain_sum[...]
    for step in range(1, 4):
        total = total + gain_line[step]
    gain_out[...] = total
    for g in range(count):
        for turn in range(2):
            goal = z_of(turn)
            step_one(g, turn).wait_send()
            step_two(g, turn).wait_send()

            @pl.when(z != goal)
            def _(g=g, turn=turn):
                line_copy(g, turn, 0, above).wait_send()

        @pl.when(home)
        def _(g=g):
            pltpu.make_async_copy(out_ref.at[g], out_ref.at[g], local.at[g]).wait()
            push(out_ref.at[g], out_ref.at[g], send_c.at[g], recv_c.at[g], sibling).wait_send()

        @pl.when(jnp.logical_not(home))
        def _(g=g):
            push(out_ref.at[g], out_ref.at[g], send_c.at[g], recv_c.at[g], sibling).wait_recv()

    for a in range(many):
        for j in range(2):
            stays = jnp.logical_and(home, 2 * core + j == z)

            @pl.when(stays)
            def _(a=a, j=j):
                pltpu.make_async_copy(rows_ref.at[a, j], back_ref.at[a, z % 2], local.at[count + a]).wait()

            @pl.when(jnp.logical_not(stays))
            def _(a=a, j=j):
                push(rows_ref.at[a, j], back_ref.at[a, 0], send_r.at[a, j], recv_r.at[a, 0], sibling).wait_send()

            @pl.when(jnp.logical_not(jnp.logical_and(home, z % 2 == j)))
            def _(a=a, j=j):
                push(rows_ref.at[a, j], back_ref.at[a, j], send_r.at[a, j], recv_r.at[a, j], sibling).wait_recv()

    @pl.when(home)
    def _():
        pltpu.make_async_copy(cond_ref, cond_out.at[z % 2], local.at[count + many]).wait()
        for step in range(1, 4):
            push(cond_ref, cond_out.at[0], send_k.at[step], recv_k.at[0], sibling).wait_send()

    for s in range(2):

        @pl.when(z != 2 * core + s)
        def _(s=s):
            push(cond_ref, cond_out.at[s], send_k.at[1], recv_k.at[s], sibling).wait_recv()


def share_moves(grads, qkv, mixed, valid, turned, whole, stream, scaled, inverse, factor, output, gains, cond):
    arrays = len(grads)
    count = arrays + 3
    depth, width = grads[0].shape[1] // 8, grads[0].shape[2] // 2
    many, parts, height, model_width = 2, *output.shape
    padded, columns = qkv.shape[1:]
    return pl.pallas_call(
        functools.partial(share_kernel, arrays=arrays),
        out_shape=[
            jax.ShapeDtypeStruct((count, depth, width), BF),
            jax.ShapeDtypeStruct((many, *output.shape), BF),
            jax.ShapeDtypeStruct(gains.shape, F32),
            jax.ShapeDtypeStruct((2, *cond.shape), BF),
        ],
        in_specs=any_specs(arrays) + near_specs(4) + any_specs(1) + near_specs(7),
        out_specs=near_specs(1) + any_specs(1) + near_specs(1) + any_specs(1),
        scratch_shapes=[
            pltpu.VMEM((arrays, 2, 2, 2, depth, width), BF),
            pltpu.VMEM((count, 2, 2, 2, depth, width), BF),
            pltpu.VMEM((count, 2, 2, depth, width), BF),
            pltpu.VMEM((count, 2, 2, 2, depth, width), BF),
            pltpu.VMEM((8, *gains.shape), F32),
            pltpu.VMEM(gains.shape, F32),
            pltpu.VMEM(gains.shape, F32),
            pltpu.VMEM((4, *gains.shape), F32),
            pltpu.VMEM((3, 2, 2, 2, depth, 2 * width), BF),
            pltpu.VMEM((2, 3, 256, 2 * width), BF),
            pltpu.VMEM(qkv.shape, BF),
            pltpu.VMEM(output.shape, BF),
            pltpu.VMEM(output.shape, BF),
            pltpu.VMEM(output.shape, F32),
            pltpu.VMEM((many, *output.shape), BF),
            dma(count, 2),
            dma(count, 2),
            dma(count, 2),
            dma(count, 2),
            dma(count, 2),
            dma(count, 2),
            dma(count, 2, 2),
            dma(count),
            dma(count),
            dma(many, 2),
            dma(many, 2),
            dma(8),
            dma(8),
            dma(4),
            dma(4),
            dma(4),
            dma(2),
            dma(count + many + 1),
            dma(5),
        ],
        compiler_params=pltpu.CompilerParams(
            collective_id=5, has_side_effects=True, vmem_limit_bytes=61 << 20
        ),
        name="share_moves",
    )(
        *[grad.reshape(1, 2, 2, 2, depth, 2 * width) for grad in grads],
        qkv,
        mixed,
        valid,
        turned,
        whole,
        stream,
        scaled,
        inverse,
        factor,
        output,
        gains,
        cond,
    )


def chip_shards(
    inputs,
    context,
    lengths,
    cotangent,
    self_qkv,
    self_out,
    cross_query,
    cross_context,
    cross_out,
    gate_up,
    down_proj,
    norm_gains,
):
    dp, z = lax.axis_index("dp"), lax.axis_index("tensor")
    core, xbit, ybit = dp & 1, (dp >> 1) & 1, (dp >> 2) & 1
    place = (core, xbit, ybit, z)
    model_width = inputs.shape[-1]
    padded = inputs.shape[1] * 4
    half_rows = padded // 2

    def own_half(value):
        return take(value.reshape(2, half_rows, -1), core, 0)

    def both_halves(mine, theirs):
        return ordered(core, mine, theirs, 0).reshape(padded, -1)

    pair_sum = lambda value: value + swap(value.astype(BF), CORE).astype(F32)

    cc_depth = cross_context.shape[1]
    tokens = context.shape[1]
    narrow = jnp.concatenate(
        [
            self_qkv,
            self_out.T[None],
            cross_query[None],
            cross_context.reshape(1, 2 * cc_depth, -1),
            cross_out.T[None],
        ]
    ).astype(BF)
    depth, units = gate_up.shape[1], gate_up.shape[2]
    wide = jnp.concatenate([gate_up, down_proj.T[None]]).astype(BF)
    wide = jnp.moveaxis(wide.reshape(3, depth, 4, units // 4), 2, 1)
    room = -tokens % 16
    cond = jnp.pad(take(context, z % 2, 0), ((0, room), (0, 0)))
    apart = cond.reshape(-1, 8, 1, cc_depth)
    none = jnp.zeros_like(apart)
    spread_cond = jnp.stack(
        [jnp.concatenate([apart, none], 2), jnp.concatenate([none, apart], 2)]
    ).reshape(2, -1, model_width)
    weights, kept = weights_moves(
        narrow,
        wide,
        inputs,
        cotangent,
        jnp.broadcast_to(take(lengths, z % 2, 0), (8, 128)),
        spread_cond,
        jnp.pad(norm_gains, ((0, 5), (0, 0))),
        ((0, 0), (0, 1), (0, 2), (1, 0), (2, 0), (3, 0), (4, 0)),
        tokens,
    )
    qkv_whole, so_whole, cq_whole, cc_whole, co_whole, gu_whole, down_whole = weights
    so_whole, cq_whole, co_whole = so_whole[0], cq_whole[0], co_whole[0]
    down_whole = down_whole[0]
    cc_whole = cc_whole[0].reshape(8, 2, cc_depth, -1)
    cc_whole = jnp.moveaxis(cc_whole, 1, 0).reshape(2, 8 * cc_depth, -1)
    normed_one, qkv, mixed_one, stream, normed_two, cross_rows, cond_rows = kept[:7]
    mixed_two, stream_half, rows_three, sequence, cot, grad_branch, row_keep, conds = kept[7:]
    row_keep = row_keep[:, :1]
    keep_half = own_half(row_keep)
    context_valid = jnp.ones((tokens,), dtype=jnp.bool_)
    cond = take(conds, z // 2, 0)[0].reshape(-1, 8, 2, cc_depth)[:tokens, :, 0]
    cond = cond.reshape(tokens, -1)
    cond_rows = cond_rows[:, :tokens]
    stream_half = stream_half.reshape(half_rows, model_width)
    rows_three = rows_three.reshape(-1, model_width)
    grad_branch = grad_branch.reshape(-1, model_width)
    cot = cot.reshape(padded, model_width).astype(F32)
    _, scaled_one, inverse_one = norm_rows(
        sequence.reshape(padded, model_width).astype(F32), norm_gains[0]
    )
    _, scaled_two, inverse_two = norm_rows(stream, norm_gains[1])
    _, scaled_three, inverse_three = norm_rows(stream_half, norm_gains[2])
    gate_rows = jnp.einsum("td,kde->kte", rows_three, gu_whole, preferred_element_type=F32)
    sigmoid_gate = jax.nn.sigmoid(gate_rows[0])
    hidden = (gate_rows[0] * sigmoid_gate * gate_rows[1]).astype(BF)

    grad_stream = row_keep * cot
    grad_hidden = jnp.einsum("td,df->tf", grad_branch, down_whole, preferred_element_type=F32)
    grad_gate = (
        grad_hidden * gate_rows[1] * sigmoid_gate * (1.0 + gate_rows[0] * (1.0 - sigmoid_gate))
    )
    grad_upper = grad_hidden * gate_rows[0] * sigmoid_gate
    grad_expand = jnp.stack([grad_gate, grad_upper]).astype(BF)
    partial_value = jnp.einsum("ktf,kdf->td", grad_expand, gu_whole, preferred_element_type=F32)
    grad_down = jnp.einsum("td,tf->df", grad_branch, hidden, preferred_element_type=F32)
    grad_gates = jnp.einsum("td,ktf->kdf", rows_three, grad_expand, preferred_element_type=F32)
    sums, wide_grads = third_moves(
        partial_value.astype(BF).reshape(4, 2, -1, model_width),
        [grad_gates.astype(BF), grad_down.astype(BF)[None]],
    )
    grad_norm, gain_rows = norm_back(
        sums.reshape(half_rows, model_width), scaled_three, inverse_three, norm_gains[2]
    )
    gain_three = jnp.sum(gain_rows, axis=0)
    wide_grads = lax.psum_scatter(wide_grads, "tensor", scatter_dimension=0, tiled=False)
    branch = jnp.einsum("tf,df->td", hidden, down_whole, preferred_element_type=F32)
    stream_half = stream_half + keep_half * plane_sums(branch)
    output = (keep_half * stream_half).astype(BF)

    grad_stream = grad_stream + both_halves(grad_norm, swap(grad_norm.astype(BF), CORE).astype(F32))
    grad_branch = (row_keep * grad_stream).astype(BF)
    grad_mixed = jnp.einsum("td,de->te", grad_branch, co_whole, preferred_element_type=F32).astype(BF)
    scores = masked_scores(split_heads(cross_rows), split_heads(cond_rows[0]), context_valid)
    log_sums = jax.nn.logsumexp(scores, axis=-1)
    grad_query, grad_key, grad_value = attend_backward(
        (cross_rows, cond_rows[0], cond_rows[1], log_sums, grad_mixed, context_valid)
    )
    partial_value = jnp.einsum("te,de->td", grad_query, cq_whole, preferred_element_type=F32)
    grad_norm, gain_rows = norm_back(
        pair_sum(partial_value), scaled_two, inverse_two, norm_gains[1]
    )
    gain_two = 0.5 * jnp.sum(gain_rows, axis=0)
    grad_merge = jnp.einsum("td,te->de", grad_branch, mixed_two, preferred_element_type=F32)
    grad_cross = jnp.einsum("td,te->de", normed_two, grad_query, preferred_element_type=F32)
    grad_pairs = jnp.stack([grad_key, grad_value])
    grad_cc = jnp.einsum("sd,kse->kde", cond, grad_pairs, preferred_element_type=F32)
    grad_cc = jnp.moveaxis(grad_cc.reshape(2, 8, cc_depth, -1), 0, 1).reshape(model_width, -1)
    context_part = jnp.einsum("kse,kde->sd", grad_pairs, cc_whole, preferred_element_type=F32)
    context_part = jnp.pad(pair_sum(context_part).astype(BF), ((0, room), (0, 0)))

    grad_stream = grad_stream + grad_norm
    grad_branch = (row_keep * grad_stream).astype(BF)
    grad_mixed = jnp.einsum("td,de->te", grad_branch, so_whole, preferred_element_type=F32).astype(BF)
    grad_after = jnp.einsum("td,te->de", grad_branch, mixed_one, preferred_element_type=F32)
    gains = jnp.stack([jnp.zeros_like(gain_two), gain_two, gain_three])
    shares, back, gains, conds = share_moves(
        [
            grad_merge.astype(BF)[None],
            grad_cross.astype(BF)[None],
            grad_cc.astype(BF)[None],
            grad_after.astype(BF)[None],
        ],
        qkv,
        grad_mixed,
        jnp.broadcast_to(row_keep, (padded, 128)),
        normed_one.T.reshape(8, -1, padded),
        qkv_whole,
        own_half(grad_stream).reshape(2, -1, model_width),
        own_half(scaled_one).reshape(2, -1, model_width),
        jnp.broadcast_to(own_half(inverse_one), (half_rows, 128)).reshape(2, -1, 128),
        jnp.broadcast_to(norm_gains[0], (8, model_width)),
        output.reshape(2, -1, model_width),
        jnp.pad(gains, ((0, 5), (0, 0))),
        context_part,
    )
    gains = lax.dynamic_slice_in_dim(gains[:3], dp * depth, depth, 1)
    shares = shares.astype(F32)
    wide_grads, back = lax.optimization_barrier((wide_grads, back))
    shared = lax.all_to_all(wide_grads, "dp", 1, 1, axis_index_groups=[[0, 2, 4, 6], [1, 3, 5, 7]])
    shared = jnp.moveaxis(shared, 1, 2).reshape(3, depth, units).astype(F32)
    return (
        back[0],
        back[1].astype(F32),
        conds[:, :tokens].astype(F32),
        shares[4:],
        shares[3].T,
        shares[1],
        shares[2].reshape(2, cc_depth, -1),
        shares[0].T,
        shared[:2],
        shared[2].T,
        gains,
    )


def solution(mesh):
    sizes = (mesh.shape["dp"], mesh.shape["tensor"])
    body = chip_shards if sizes == (8, 4) else shards
    placed = (
        P("dp", "tensor", None),
        P("dp", None, None),
        P("dp"),
        P("dp", "tensor", None),
        P(None, "dp", "tensor"),
        P("tensor", "dp"),
        P("dp", "tensor"),
        P(None, "dp", "tensor"),
        P("tensor", "dp"),
        P(None, "dp", "tensor"),
        P("tensor", "dp"),
        P(),
    )
    return jax.shard_map(
        body,
        mesh=mesh,
        in_specs=placed,
        out_specs=(
            P("dp", "tensor", None),
            P("dp", "tensor", None),
            P("dp", None, None),
            P(None, "dp", "tensor"),
            P("tensor", "dp"),
            P("dp", "tensor"),
            P(None, "dp", "tensor"),
            P("tensor", "dp"),
            P(None, "dp", "tensor"),
            P("tensor", "dp"),
            P(None, "dp"),
        ),
        check_vma=False,
    )
```

```python
import functools

import jax
import jax.numpy as jnp
from jax import lax
from jax.experimental import pallas as pl
from jax.experimental.pallas import tpu as pltpu
from jax.sharding import PartitionSpec as P

HD = 64


EPSILON = 1e-05
NEGATIVE = -1000000000.0


def norm_rows(stream, gain):
    centred = stream - jnp.mean(stream, axis=-1, keepdims=True)
    inverse = lax.rsqrt(jnp.mean(centred * centred, axis=-1, keepdims=True) + EPSILON)
    scaled = centred * inverse
    return (scaled * gain, scaled, inverse)


def norm_back(grad_out, scaled, inverse, gain):
    grad_scaled = grad_out * gain
    centre_part = jnp.mean(grad_scaled, axis=-1, keepdims=True)
    slope_part = jnp.mean(grad_scaled * scaled, axis=-1, keepdims=True)
    grad_in = inverse * (grad_scaled - centre_part - scaled * slope_part)
    return (grad_in, grad_out * scaled)


def split_heads(flat):
    return flat.reshape(flat.shape[0], flat.shape[1] // HD, HD)


def masked_scores(queries, keys_in, key_valid):
    scores = jnp.einsum(
        "qhd,khd->hqk", queries, keys_in, preferred_element_type=jnp.float32
    ) * HD ** (-0.5)
    return jnp.where(key_valid[None, None, :], scores, NEGATIVE)


def attend_forward(item):
    query_rows, key_rows, value_rows, key_valid = item
    scores = masked_scores(split_heads(query_rows), split_heads(key_rows), key_valid)
    peak_score = jnp.max(scores, axis=-1, keepdims=True)
    exponent = jnp.exp(scores - peak_score)
    denominator = jnp.sum(exponent, axis=-1, keepdims=True)
    probs = (exponent / denominator).astype(jnp.bfloat16)
    mixed = jnp.einsum(
        "hqk,khd->qhd", probs, split_heads(value_rows), preferred_element_type=jnp.float32
    )
    return (
        mixed.reshape(query_rows.shape).astype(jnp.bfloat16),
        (peak_score + jnp.log(denominator))[..., 0],
    )


def attend_backward(item):
    query_rows, key_rows, value_rows, logsum, grad_mixed, key_valid = item
    queries = split_heads(query_rows)
    keys_in = split_heads(key_rows)
    values = split_heads(value_rows)
    grads = split_heads(grad_mixed)
    probs = jnp.exp(masked_scores(queries, keys_in, key_valid) - logsum[..., None])
    grad_probs = jnp.einsum("qhd,khd->hqk", grads, values, preferred_element_type=jnp.float32)
    inner_sum = jnp.sum(probs * grad_probs, axis=-1, keepdims=True)
    grad_scores = (probs * (grad_probs - inner_sum)).astype(jnp.bfloat16)
    grad_values = jnp.einsum(
        "hqk,qhd->khd", probs.astype(jnp.bfloat16), grads, preferred_element_type=jnp.float32
    )
    grad_queries = jnp.einsum(
        "hqk,khd->qhd", grad_scores, keys_in, preferred_element_type=jnp.float32
    ) * HD ** (-0.5)
    grad_keys = jnp.einsum(
        "hqk,qhd->khd", grad_scores, queries, preferred_element_type=jnp.float32
    ) * HD ** (-0.5)
    return (
        grad_queries.reshape(query_rows.shape).astype(jnp.bfloat16),
        grad_keys.reshape(key_rows.shape).astype(jnp.bfloat16),
        grad_values.reshape(value_rows.shape).astype(jnp.bfloat16),
    )


def rows_whole(local_rows):
    return lax.all_gather(local_rows, "tensor", axis=1, tiled=True)


def rows_share(partial_value):
    return lax.psum_scatter(partial_value, "tensor", scatter_dimension=1, tiled=True)


def grad_whole(local_rows):
    return lax.all_gather(local_rows, "tensor", axis=1, tiled=True)


def grad_share(partial_value):
    return lax.psum_scatter(
        partial_value.astype(jnp.bfloat16), "tensor", scatter_dimension=1, tiled=True
    ).astype(jnp.float32)


def shards(
    inputs,
    context,
    lengths,
    cotangent,
    self_qkv,
    self_out,
    cross_query,
    cross_context,
    cross_out,
    gate_up,
    down_proj,
    norm_gains,
):
    seq_count, row_count, model_width = inputs.shape
    padded = row_count * lax.axis_size("tensor")
    tokens = seq_count * padded
    local_pos = lax.axis_index("tensor") * row_count + jnp.arange(row_count, dtype=jnp.int32)
    key_valid = jnp.arange(padded, dtype=jnp.int32)[None, :] < lengths[:, None]
    context_valid = jnp.ones((seq_count, context.shape[1]), dtype=jnp.bool_)
    row_keep = (local_pos[None, :] < lengths[:, None]).astype(jnp.float32)[:, :, None]
    (
        full_self_qkv,
        full_self_out,
        full_cross_query,
        full_cross_context,
        full_cross_out,
        full_gate_up,
        full_down,
    ) = (
        lax.all_gather(self_qkv.astype(jnp.bfloat16), "dp", axis=1, tiled=True),
        lax.all_gather(self_out.astype(jnp.bfloat16), "dp", axis=1, tiled=True),
        lax.all_gather(cross_query.astype(jnp.bfloat16), "dp", axis=0, tiled=True),
        lax.all_gather(cross_context.astype(jnp.bfloat16), "dp", axis=1, tiled=True),
        lax.all_gather(cross_out.astype(jnp.bfloat16), "dp", axis=1, tiled=True),
        lax.all_gather(gate_up.astype(jnp.bfloat16), "dp", axis=1, tiled=True),
        lax.all_gather(down_proj.astype(jnp.bfloat16), "dp", axis=1, tiled=True),
    )
    stream = inputs.astype(jnp.float32)
    normed, scaled_one, inverse_one = norm_rows(stream, norm_gains[0])
    whole_one = rows_whole(normed.astype(jnp.bfloat16)).reshape(tokens, model_width)
    qkv_rows = jnp.einsum(
        "td,cde->cte", whole_one, full_self_qkv, preferred_element_type=jnp.float32
    )
    qkv_rows = qkv_rows.astype(jnp.bfloat16).reshape(3, seq_count, padded, -1)
    mixed_one, logsum_one = lax.map(
        attend_forward, (qkv_rows[0], qkv_rows[1], qkv_rows[2], key_valid)
    )
    branch = jnp.dot(
        mixed_one.reshape(tokens, -1), full_self_out, preferred_element_type=jnp.float32
    )
    stream = stream + row_keep * rows_share(branch.reshape(seq_count, padded, model_width))
    normed, scaled_two, inverse_two = norm_rows(stream, norm_gains[1])
    whole_two = rows_whole(normed.astype(jnp.bfloat16)).reshape(tokens, model_width)
    cross_rows = jnp.dot(whole_two, full_cross_query, preferred_element_type=jnp.float32)
    cross_rows = cross_rows.astype(jnp.bfloat16).reshape(seq_count, padded, -1)
    context_rows = jnp.einsum(
        "scd,kde->ksce", context, full_cross_context, preferred_element_type=jnp.float32
    ).astype(jnp.bfloat16)
    mixed_two, logsum_two = lax.map(
        attend_forward, (cross_rows, context_rows[0], context_rows[1], context_valid)
    )
    branch = jnp.dot(
        mixed_two.reshape(tokens, -1), full_cross_out, preferred_element_type=jnp.float32
    )
    stream = stream + row_keep * rows_share(branch.reshape(seq_count, padded, model_width))
    normed, scaled_three, inverse_three = norm_rows(stream, norm_gains[2])
    whole_three = rows_whole(normed.astype(jnp.bfloat16)).reshape(tokens, model_width)
    gate_rows = jnp.einsum(
        "td,kdf->ktf", whole_three, full_gate_up, preferred_element_type=jnp.float32
    )
    sigmoid_gate = jax.nn.sigmoid(gate_rows[0])
    hidden = (gate_rows[0] * sigmoid_gate * gate_rows[1]).astype(jnp.bfloat16)
    branch = jnp.dot(hidden, full_down, preferred_element_type=jnp.float32)
    stream = stream + row_keep * rows_share(branch.reshape(seq_count, padded, model_width))
    output = (row_keep * stream).astype(jnp.bfloat16)
    (
        full_self_qkv,
        full_self_out,
        full_cross_query,
        full_cross_context,
        full_cross_out,
        full_gate_up,
        full_down,
    ) = (
        lax.all_gather(self_qkv.astype(jnp.bfloat16), "dp", axis=1, tiled=True),
        lax.all_gather(self_out.astype(jnp.bfloat16), "dp", axis=1, tiled=True),
        lax.all_gather(cross_query.astype(jnp.bfloat16), "dp", axis=0, tiled=True),
        lax.all_gather(cross_context.astype(jnp.bfloat16), "dp", axis=1, tiled=True),
        lax.all_gather(cross_out.astype(jnp.bfloat16), "dp", axis=1, tiled=True),
        lax.all_gather(gate_up.astype(jnp.bfloat16), "dp", axis=1, tiled=True),
        lax.all_gather(down_proj.astype(jnp.bfloat16), "dp", axis=1, tiled=True),
    )
    grad_stream = row_keep * cotangent.astype(jnp.float32)
    grad_branch = grad_whole((row_keep * grad_stream).astype(jnp.bfloat16)).reshape(
        tokens, model_width
    )
    grad_down = jnp.einsum("tf,td->fd", hidden, grad_branch, preferred_element_type=jnp.float32)
    grad_hidden = jnp.einsum(
        "td,fd->tf", grad_branch, full_down, preferred_element_type=jnp.float32
    )
    grad_gate = (
        grad_hidden * gate_rows[1] * sigmoid_gate * (1.0 + gate_rows[0] * (1.0 - sigmoid_gate))
    )
    grad_upper = grad_hidden * gate_rows[0] * sigmoid_gate
    grad_expand = jnp.stack([grad_gate, grad_upper]).astype(jnp.bfloat16)
    grad_gates = jnp.einsum(
        "td,ktf->kdf", whole_three, grad_expand, preferred_element_type=jnp.float32
    )
    partial_value = jnp.einsum(
        "ktf,kdf->td", grad_expand, full_gate_up, preferred_element_type=jnp.float32
    )
    grad_norm, gain_rows = norm_back(
        grad_share(partial_value.reshape(seq_count, padded, model_width)),
        scaled_three,
        inverse_three,
        norm_gains[2],
    )
    gain_three = jnp.sum(gain_rows, axis=(0, 1))
    grad_stream = grad_stream + grad_norm
    grad_branch = grad_whole((row_keep * grad_stream).astype(jnp.bfloat16)).reshape(
        tokens, model_width
    )
    grad_merge = jnp.einsum(
        "te,td->ed", mixed_two.reshape(tokens, -1), grad_branch, preferred_element_type=jnp.float32
    )
    grad_mixed = jnp.einsum(
        "td,ed->te", grad_branch, full_cross_out, preferred_element_type=jnp.float32
    )
    grad_mixed = grad_mixed.astype(jnp.bfloat16).reshape(seq_count, padded, -1)
    grad_query, grad_key, grad_value = lax.map(
        attend_backward,
        (cross_rows, context_rows[0], context_rows[1], logsum_two, grad_mixed, context_valid),
    )
    grad_cross = jnp.einsum(
        "td,te->de", whole_two, grad_query.reshape(tokens, -1), preferred_element_type=jnp.float32
    )
    grad_pairs = jnp.stack([grad_key, grad_value])
    grad_context_proj = jnp.einsum(
        "scd,ksce->kde", context, grad_pairs, preferred_element_type=jnp.float32
    )
    context_part = jnp.einsum(
        "ksce,kde->scd", grad_pairs, full_cross_context, preferred_element_type=jnp.float32
    )
    partial_value = jnp.einsum(
        "te,de->td",
        grad_query.reshape(tokens, -1),
        full_cross_query,
        preferred_element_type=jnp.float32,
    )
    grad_norm, gain_rows = norm_back(
        grad_share(partial_value.reshape(seq_count, padded, model_width)),
        scaled_two,
        inverse_two,
        norm_gains[1],
    )
    gain_two = jnp.sum(gain_rows, axis=(0, 1))
    grad_stream = grad_stream + grad_norm
    grad_branch = grad_whole((row_keep * grad_stream).astype(jnp.bfloat16)).reshape(
        tokens, model_width
    )
    grad_after = jnp.einsum(
        "te,td->ed", mixed_one.reshape(tokens, -1), grad_branch, preferred_element_type=jnp.float32
    )
    grad_mixed = jnp.einsum(
        "td,ed->te", grad_branch, full_self_out, preferred_element_type=jnp.float32
    )
    grad_mixed = grad_mixed.astype(jnp.bfloat16).reshape(seq_count, padded, -1)
    grad_query, grad_key, grad_value = lax.map(
        attend_backward, (qkv_rows[0], qkv_rows[1], qkv_rows[2], logsum_one, grad_mixed, key_valid)
    )
    grad_triple = jnp.stack([grad_query, grad_key, grad_value]).reshape(3, tokens, -1)
    grad_self = jnp.einsum(
        "td,cte->cde", whole_one, grad_triple, preferred_element_type=jnp.float32
    )
    partial_value = jnp.einsum(
        "cte,cde->td", grad_triple, full_self_qkv, preferred_element_type=jnp.float32
    )
    grad_norm, gain_rows = norm_back(
        grad_share(partial_value.reshape(seq_count, padded, model_width)),
        scaled_one,
        inverse_one,
        norm_gains[0],
    )
    gain_one = jnp.sum(gain_rows, axis=(0, 1))
    grad_inputs = grad_stream + grad_norm
    gain_partial = jnp.stack([gain_one, gain_two, gain_three])
    gain_total, grad_context = (
        lax.psum(gain_partial.astype(jnp.bfloat16), "tensor").astype(jnp.float32),
        lax.psum(context_part.astype(jnp.bfloat16), "tensor").astype(jnp.float32),
    )
    result_grads = (
        lax.psum_scatter(
            grad_self.astype(jnp.bfloat16), "dp", scatter_dimension=1, tiled=True
        ).astype(jnp.float32),
        lax.psum_scatter(
            grad_after.astype(jnp.bfloat16), "dp", scatter_dimension=1, tiled=True
        ).astype(jnp.float32),
        lax.psum_scatter(
            grad_cross.astype(jnp.bfloat16), "dp", scatter_dimension=0, tiled=True
        ).astype(jnp.float32),
        lax.psum_scatter(
            grad_context_proj.astype(jnp.bfloat16), "dp", scatter_dimension=1, tiled=True
        ).astype(jnp.float32),
        lax.psum_scatter(
            grad_merge.astype(jnp.bfloat16), "dp", scatter_dimension=1, tiled=True
        ).astype(jnp.float32),
        lax.psum_scatter(
            grad_gates.astype(jnp.bfloat16), "dp", scatter_dimension=1, tiled=True
        ).astype(jnp.float32),
        lax.psum_scatter(
            grad_down.astype(jnp.bfloat16), "dp", scatter_dimension=1, tiled=True
        ).astype(jnp.float32),
        lax.psum_scatter(
            gain_total.astype(jnp.bfloat16), "dp", scatter_dimension=1, tiled=True
        ).astype(jnp.float32),
    )
    return (
        output,
        grad_inputs,
        grad_context,
        result_grads[0],
        result_grads[1],
        result_grads[2],
        result_grads[3],
        result_grads[4],
        result_grads[5],
        result_grads[6],
        result_grads[7],
    )


BF = jnp.bfloat16
F32 = jnp.float32


def take(value, index, axis):
    return lax.dynamic_index_in_dim(value, index, axis, keepdims=False)


MESH = pl.DeviceIdType.MESH


def spot():
    dp, z = lax.axis_index("dp"), lax.axis_index("tensor")
    return dp, dp // 2, dp % 2, z


def greet(devices):
    barrier = pltpu.get_barrier_semaphore()
    for dp, z in devices:
        pl.semaphore_signal(
            barrier, inc=1, device_id={"dp": dp, "tensor": z}, device_id_type=MESH
        )
    pl.semaphore_wait(barrier, len(devices))


def flip(dp, bit):
    bits = {1: dp % 2, 2: dp // 2 % 2, 4: dp // 4 % 2}
    return dp + bit * (1 - 2 * bits[bit])


def plane_mates(dp, z):
    return [(flip(dp, 2), z), (flip(dp, 4), z), (flip(flip(dp, 2), 4), z)]


def column_mates(dp, z):
    mates = [(flip(dp, 1), z)]
    for step in range(1, 4):
        far = lax.rem(z + step, 4)
        mates += [(dp, far), (flip(dp, 1), far)]
    return mates


def push(source, target, send, recv, device):
    dp, z = device
    return pltpu.make_async_remote_copy(
        src_ref=source,
        dst_ref=target,
        send_sem=send,
        recv_sem=recv,
        device_id={"dp": dp, "tensor": z},
        device_id_type=MESH,
    )


def any_specs(count):
    return [pl.BlockSpec(memory_space=pl.ANY)] * count


def near_specs(count):
    return [pl.BlockSpec(memory_space=pltpu.VMEM)] * count


ROOM = 56 << 20


def dma(*shape):
    return pltpu.SemaphoreType.DMA(shape)


def forward_pair(queries, keys_in, values, valid):
    lane = lax.broadcasted_iota(jnp.int32, (1, 2 * HD), 1)
    total = None
    for side in range(2):
        only = jnp.where(lane // HD == side, 1.0, 0.0)
        picked = (queries.astype(F32) * (only * HD ** (-0.5))).astype(BF)
        turned = (values.astype(F32) * only).T.astype(BF)
        scores = lax.dot_general(
            keys_in, picked, (((1,), (1,)), ((), ())), preferred_element_type=F32
        )
        scores = jnp.where(valid, scores, NEGATIVE)
        exponent = jnp.exp(scores - jnp.max(scores, axis=0, keepdims=True))
        share = 1.0 / jnp.sum(exponent, axis=0, keepdims=True)
        mixed = jnp.dot(turned, exponent.astype(BF), preferred_element_type=F32) * share
        total = mixed if total is None else total + mixed
    return total.T.astype(BF)


class RowsIn:
    def __init__(self, source, target, sems):
        self.source, self.target = source, target
        self.send, self.recv, self.send_on, self.recv_on, self.keep = sems
        self.dp, self.plane, self.core, self.z = spot()
        self.sibling = (flip(self.dp, 1), self.z)
        self.home = self.z // 2 == self.core

    def stays(self, s):
        return jnp.logical_and(self.home, self.z % 2 == s)

    def depart(self):
        for s in range(2):

            @pl.when(jnp.logical_not(self.stays(s)))
            def _(s=s):
                goal = (self.plane * 2 + self.z // 2, 2 * self.core + s)
                push(
                    self.source.at[s],
                    self.target.at[self.z],
                    self.send.at[s],
                    self.recv.at[self.z % 2],
                    goal,
                ).start()

            @pl.when(self.stays(s))
            def _(s=s):
                pltpu.make_async_copy(
                    self.source.at[s], self.target.at[self.z], self.keep.at[0]
                ).start()

    def onward(self, j, core):
        place = self.target.at[2 * core + j]
        return push(place, place, self.send_on.at[j], self.recv_on.at[j], self.sibling)

    def forward(self):
        for j in range(2):
            place = self.target.at[2 * self.core + j]
            mine = jnp.logical_and(self.home, 2 * self.core + j == self.z)

            @pl.when(mine)
            def _():
                pltpu.make_async_copy(self.source.at[0], place, self.keep.at[0]).wait()

            @pl.when(jnp.logical_not(mine))
            def _(j=j):
                push(
                    self.source.at[0], place, self.send.at[0], self.recv.at[j], self.sibling
                ).wait_recv()

            self.onward(j, self.core).start()

    def settle(self):
        for j in range(2):
            self.onward(j, 1 - self.core).wait_recv()

    def finish(self):
        for j in range(2):
            self.onward(j, self.core).wait_send()

            @pl.when(jnp.logical_not(self.stays(j)))
            def _(j=j):
                push(
                    self.source.at[j],
                    self.target.at[self.z],
                    self.send.at[j],
                    self.recv.at[0],
                    self.sibling,
                ).wait_send()


class PlaneRows:
    def __init__(self, target, send, recv):
        self.target, self.send, self.recv = target, send, recv
        dp, _, _, z = spot()
        self.xmate, self.ymate, _ = plane_mates(dp, z)

    def copy(self, near, part, chip, slot, mate):
        return push(
            self.target.at[near, part],
            self.target.at[chip, part],
            self.send.at[slot],
            self.recv.at[slot],
            mate,
        )

    def hop(self, slot):
        near, part, chip, mate = [
            (0, 0, 1, self.xmate),
            (0, 1, 2, self.ymate),
            (0, 0, 2, self.ymate),
            (0, 1, 1, self.xmate),
            (1, 0, 3, self.ymate),
            (2, 1, 3, self.xmate),
        ][slot]
        return self.copy(near, part, chip, slot, mate)

    def start(self):
        for slot in range(4):
            self.hop(slot).start()

    def relay(self):
        for slot in range(2):
            self.hop(slot).wait_recv()
            self.hop(4 + slot).start()

    def finish(self):
        for slot in range(2, 6):
            self.hop(slot).wait_recv()
        for slot in range(6):
            self.hop(slot).wait_send()


def weights_kernel(
    shard_ref,
    units_ref,
    rows_ref,
    cot_ref,
    size_ref,
    cond_ref,
    gain_ref,
    *refs,
    groups,
    wides,
    tokens,
):
    count = len(groups)
    arrays = max(which for which, _ in groups) + 1
    whole_refs, refs = refs[:arrays], refs[arrays:]
    wide_refs, refs = refs[:2], refs[1:]
    one_ref, qkv_ref, mixed_ref, stream_ref, two_ref, query_ref, pair_ref, crossed_ref = refs[1:9]
    after_ref, all_ref, seq_ref, grad_ref, grads_ref, keep_ref, conds_ref = refs[9:16]
    held, part_out, part_in, three, block_ref, sizes = refs[16:22]
    send_e, recv_e, send_n, recv_n, held_sem = refs[22:27]
    send_s, recv_s, send_z, recv_z, send_p, recv_p, local = refs[27:34]
    send_w, recv_w, send_v, recv_v, local_w = refs[34:39]
    stream_rows = RowsIn(rows_ref, seq_ref, refs[39:44])
    grad_rows = RowsIn(cot_ref, grad_ref, refs[44:49])
    send_b, recv_b, send_d, recv_d, send_q, recv_q, keep_sem = refs[49:]
    dp, plane, core, z = spot()
    width = shard_ref.shape[2]
    sibling = (flip(dp, 1), z)
    xmate, ymate, far = plane_mates(dp, z)
    greet(plane_mates(dp, z) + column_mates(dp, z))
    home = z // 2 == core
    above, below = (dp, z + 1), (dp, z - 1)
    stream_rows.depart()
    units = [
        push(
            units_ref.at[:, mate[0] // 2],
            block_ref.at[:, plane],
            send_b.at[slot],
            recv_b.at[slot],
            mate,
        )
        for slot, mate in enumerate([xmate, ymate, far])
    ]
    units_own = pltpu.make_async_copy(
        units_ref.at[:, plane], block_ref.at[:, plane], keep_sem.at[0]
    )
    small = [
        push(size_ref, sizes.at[core], send_d.at[0], recv_d.at[0], sibling),
        push(cond_ref, conds_ref.at[core], send_d.at[1], recv_d.at[1], sibling),
    ]
    small_own = [
        pltpu.make_async_copy(size_ref, sizes.at[core], keep_sem.at[1]),
        pltpu.make_async_copy(cond_ref, conds_ref.at[core], keep_sem.at[2]),
    ]

    def columns(which):
        return pl.ds(pl.multiple_of(which * width, width), width)

    def slab(g):
        array, index = groups[g]
        return whole_refs[array].at[index]

    for g in range(count):
        target = slab(g).at[plane, core, :, columns(z % 2)]

        @pl.when(home)
        def _(g=g, target=target):
            pltpu.make_async_copy(shard_ref.at[g], target, local.at[g]).start()

        @pl.when(jnp.logical_not(home))
        def _(g=g, target=target):
            push(shard_ref.at[g], target, send_s.at[g], recv_s.at[g], sibling).start()

    for copy in small + small_own + units + [units_own]:
        copy.start()

    near = jnp.where(core == 0, jnp.where(z >= 1, 1, 0), jnp.where(z <= 2, 0, 1))

    def order(turn):
        return near if turn == 0 else 1 - near

    def area(g, which, chip):
        return slab(g).at[chip, :, :, columns(which)]

    def on_z(g, turn, act):
        which = order(turn)
        source_z = 2 * core + which
        place = area(g, which, plane)
        for way, (wanted, target) in enumerate(
            [
                (jnp.logical_and(z >= source_z, z < 3), above),
                (jnp.logical_and(z <= source_z, z > 0), below),
            ]
        ):

            @pl.when(wanted)
            def _(way=way, target=target):
                act(push(place, place, send_z.at[g, turn, way], recv_z.at[g, which], target))

    def arrive(g, turn):
        which = order(turn)
        source_z = 2 * core + which

        @pl.when(z == source_z)
        def _():
            mine = slab(g).at[plane, core, :, columns(which)]
            other = slab(g).at[plane, 1 - core, :, columns(which)]
            pltpu.make_async_copy(shard_ref.at[g], mine, local.at[g]).wait()
            push(mine, other, send_s.at[g], recv_s.at[g], sibling).wait_recv()

        @pl.when(z != source_z)
        def _():
            place = area(g, which, plane)
            push(place, place, send_z.at[g, turn, 0], recv_z.at[g, which], sibling).wait_recv()

    def hop(g, turn, chip, slot, mate):
        place = area(g, order(turn), chip)
        return push(place, place, send_p.at[g, turn, slot], recv_p.at[g, turn, slot], mate)

    mates = (xmate, ymate)

    def spread(g, turn):
        arrive(g, turn)
        on_z(g, turn, lambda copy: copy.start())
        hop(g, turn, plane, turn, mates[turn]).start()
        hop(g, turn, plane, 1 - turn, mates[1 - turn]).start()

    def relay(g, turn):
        chip = mates[turn][0] // 2
        hop(g, turn, chip, turn, mates[turn]).wait_recv()
        hop(g, turn, chip, 2, mates[1 - turn]).start()

    wide_width = block_ref.shape[3]

    def quarter(k, block, side):
        spots = pl.ds(pl.multiple_of(block * wide_width, wide_width), wide_width)
        return wide_refs[k // 2].at[k % 2, :, side, :, spots]

    def wide_copy(k, block, way, target):
        place = quarter(k, block, core)
        return push(place, place, send_w.at[k, block, way], recv_w.at[k, block], target)

    def to_sibling(k, block, side):
        place = quarter(k, block, side)
        return push(place, place, send_v.at[k, block], recv_v.at[k, block], sibling)

    def wide_own(k):
        pltpu.make_async_copy(block_ref.at[k], quarter(k, z, core), local_w.at[k]).start()
        pltpu.make_async_copy(block_ref.at[k], quarter(k, z, core), local_w.at[k]).wait()
        for way, (wanted, target) in enumerate([(z < 3, above), (z > 0, below)]):

            @pl.when(wanted)
            def _(way=way, target=target):
                wide_copy(k, z, way, target).start()

        to_sibling(k, z, core).start()

    def wide_step(k, step):
        for way, (block, wanted, further, target) in enumerate(
            [
                (z - step, z - step >= 0, z < 3, above),
                (z + step, z + step <= 3, z > 0, below),
            ]
        ):

            @pl.when(wanted)
            def _(block=block, way=way, target=target):
                wide_copy(k, block, way, target).wait_recv()
                to_sibling(k, block, core).start()

            @pl.when(jnp.logical_and(wanted, further))
            def _(block=block, way=way, target=target):
                wide_copy(k, block, way, target).start()


    def both(step, g):
        step(g, 0)
        step(g, 1)

    def settle(g):
        for turn in range(2):
            hop(g, turn, mates[1 - turn][0] // 2, 1 - turn, mates[1 - turn]).wait_recv()
            hop(g, turn, far[0] // 2, 2, mates[1 - turn]).wait_recv()
        copy = pltpu.make_async_copy(slab(g), held.at[g % 2], held_sem.at[g % 2])
        copy.start()
        copy.wait()

    height = seq_ref.shape[0] * seq_ref.shape[1]
    model_width = seq_ref.shape[2]
    depth = shard_ref.shape[1]
    half = height // 2
    tile = 256

    def norm(value, which):
        centred = value - jnp.mean(value, axis=1, keepdims=True)
        inverse = lax.rsqrt(jnp.mean(centred * centred, axis=1, keepdims=True) + EPSILON)
        return (centred * inverse * gain_ref[which : which + 1]).astype(BF)

    def project(g, source, put):
        def body(step, carry):
            rows = source.shape[0] // 2
            lines = pl.ds(pl.multiple_of(step // 3 * rows, 16), rows)
            spots = pl.ds(pl.multiple_of(step % 3 * tile, tile), tile)
            weight = held[g % 2, :, :, :, spots].reshape(model_width, tile)
            put(lines, spots, jnp.dot(source[lines, :], weight, preferred_element_type=F32).astype(BF))
            return carry

        lax.fori_loop(0, 6, body, 0)

    def give(g, source, turn):
        def body(step, carry):
            lines = pl.ds(pl.multiple_of(step // 4 * half, 16), half)
            chip = step % 4
            span = model_width // 4
            weight = held[g % 2, chip].reshape(span, -1)
            value = lax.dot_general(
                source[lines, :], weight, (((1,), (1,)), ((), ())), preferred_element_type=F32
            )
            spots = pl.ds(pl.multiple_of(chip * span, 128), span)
            part_out[turn, lines, spots] = value.astype(BF)
            return carry

        lax.fori_loop(0, 8, body, 0)
        exchange(turn).start()

    def exchange(turn):
        return push(part_out.at[turn], part_in.at[turn], send_e.at[turn], recv_e.at[turn], sibling)

    slices = height // 32

    def first_norm():
        for part in range(seq_ref.shape[0]):
            lines = slice(part * seq_ref.shape[1], (part + 1) * seq_ref.shape[1])
            stream_ref[lines, :] = seq_ref[part].astype(F32)

        def body(i, carry):
            lines = pl.ds(pl.multiple_of(i * 32, 32), 32)
            one_ref[lines, :] = norm(stream_ref[lines, :], 0)
            return carry

        lax.fori_loop(0, slices, body, 0)

    def summed(lines, turn):
        both_parts = part_out[turn, lines, :].astype(F32) + part_in[turn, lines, :].astype(F32)
        return stream_ref[lines, :] + keep_ref[lines, :1] * both_parts

    def second_norm():
        exchange(0).wait_recv()

        def body(i, carry):
            lines = pl.ds(pl.multiple_of(i * 32, 32), 32)
            value = summed(lines, 0)
            stream_ref[lines, :] = value
            two_ref[lines, :] = norm(value, 1)
            return carry

        lax.fori_loop(0, slices, body, 0)

    def third_norm():
        count_rows = half // 2
        for j in range(2):

            def body(i, carry, j=j):
                start = pl.multiple_of(i * 8, 8)
                lines = pl.ds(pl.multiple_of(core * half + j * count_rows + i * 8, 8), 8)
                added = three[pl.ds(pl.multiple_of(j * count_rows + i * 8, 8), 8), :]
                value = stream_ref[lines, :] + keep_ref[lines, :1] * added
                after_ref[j, pl.ds(start, 8), :] = value
                return carry

            lax.fori_loop(0, count_rows // 8, body, 0)
            all_ref[0, j] = norm(after_ref[j], 2)

    def unpack():
        def body(i, carry):
            lines = pl.ds(pl.multiple_of(core * half + i * 16, 16), 16)
            value = part_out[1, lines, :].astype(F32) + part_in[1, lines, :].astype(F32)
            three[pl.ds(pl.multiple_of(i * 16, 16), 16), :] = value
            return carry

        lax.fori_loop(0, half // 16, body, 0)

    def own_heads(pair, carry):
        lanes = pl.ds(pl.multiple_of(pair * 128, 128), 128)
        mixed_ref[:, lanes] = forward_pair(
            qkv_ref[0, :, lanes], qkv_ref[1, :, lanes], qkv_ref[2, :, lanes], keep_ref[:, :1] > 0.0
        )
        return carry

    def cross_heads(pair, carry):
        lanes = pl.ds(pl.multiple_of(pair * 128, 128), 128)
        line = lax.broadcasted_iota(jnp.int32, (pair_ref.shape[1], 1), 0)
        crossed_ref[:, lanes] = forward_pair(
            query_ref[:, lanes], pair_ref[0, :, lanes], pair_ref[1, :, lanes], line < tokens
        )
        return carry

    pairs = qkv_ref.shape[2] // 128

    def put_in(target):
        def put(lines, spots, value):
            target[lines, spots] = value

        return put

    def put_cond(which):
        def body(step, carry):
            spots = pl.ds(pl.multiple_of(step * tile, tile), tile)
            lines = slice(which * (depth // 2), (which + 1) * (depth // 2))
            weight = held[5 % 2, :, :, lines, spots].reshape(model_width // 2, tile)
            value = jnp.dot(conds_ref[z // 2], weight, preferred_element_type=F32)
            pair_ref[which, :, spots] = value.astype(BF)
            return carry

        lax.fori_loop(0, 3, body, 0)

    def set_keep():
        for copy in small_own:
            copy.wait()
        for copy in small:
            copy.wait()
        line = lax.broadcasted_iota(jnp.int32, keep_ref.shape, 0)
        keep_ref[...] = jnp.where(line < sizes[z // 2, :1, :], 1.0, 0.0)

    def set_grads():
        for j in range(2):
            lines = pl.ds(pl.multiple_of((2 * core + j) * grad_ref.shape[1], 8), grad_ref.shape[1])
            value = grad_ref[2 * core + j].astype(F32) * keep_ref[lines, :1]
            grads_ref[0, j] = value.astype(BF)

    plane_norms = PlaneRows(all_ref, send_n, recv_n)
    plane_grads = PlaneRows(grads_ref, send_q, recv_q)

    both(spread, 0)
    stream_rows.forward()
    set_keep()
    stream_rows.settle()
    first_norm()
    both(spread, 1)
    both(spread, 2)
    both(relay, 0)
    both(spread, 3)
    both(relay, 1)
    both(spread, 4)
    settle(0)
    project(0, one_ref, put_in(qkv_ref.at[0]))
    both(relay, 2)
    both(spread, 5)
    both(spread, 6)
    grad_rows.depart()
    for copy in units:
        copy.wait()
    units_own.wait()
    wide_own(0)
    settle(1)
    project(1, one_ref, put_in(qkv_ref.at[1]))
    both(relay, 3)
    wide_own(1)
    settle(2)
    project(2, one_ref, put_in(qkv_ref.at[2]))
    both(relay, 4)
    wide_own(2)
    lax.fori_loop(0, pairs, own_heads, 0)
    wide_step(0, 1)
    grad_rows.forward()
    set_grads()
    plane_grads.start()
    both(relay, 5)
    settle(3)
    give(3, mixed_ref, 0)
    wide_step(1, 1)
    both(relay, 6)
    second_norm()
    wide_step(2, 1)
    plane_grads.relay()
    settle(4)
    project(4, two_ref, put_in(query_ref))
    wide_step(0, 2)
    settle(5)
    put_cond(0)
    put_cond(1)
    lax.fori_loop(0, pairs, cross_heads, 0)
    wide_step(1, 2)
    settle(6)
    give(6, crossed_ref, 1)
    wide_step(2, 2)
    exchange(1).wait_recv()
    unpack()
    third_norm()
    plane_norms.start()
    wide_step(0, 3)
    plane_norms.relay()
    wide_step(1, 3)
    wide_step(2, 3)
    grad_rows.settle()
    plane_grads.finish()
    plane_norms.finish()
    grad_rows.finish()
    stream_rows.finish()
    for turn in range(2):
        exchange(turn).wait_send()
    for g in range(count):
        for turn in range(2):
            for slot in range(3):
                hop(g, turn, plane, slot, xmate).wait_send()
            on_z(g, turn, lambda copy: copy.wait_send())

        @pl.when(jnp.logical_not(home))
        def _(g=g):
            push(shard_ref.at[g], shard_ref.at[g], send_s.at[g], recv_s.at[g], sibling).wait_send()

    for k in range(wides):
        for block in range(4):
            to_sibling(k, block, core).wait_send()
            to_sibling(k, block, 1 - core).wait_recv()

            @pl.when(jnp.logical_and(block <= z, z < 3))
            def _(k=k, block=block):
                wide_copy(k, block, 0, above).wait_send()

            @pl.when(jnp.logical_and(block >= z, z > 0))
            def _(k=k, block=block):
                wide_copy(k, block, 1, below).wait_send()


def weights_moves(shard, units, rows, cot, size, cond, gains, groups, tokens):
    count, depth, width = shard.shape
    sizes = [0] * (max(which for which, _ in groups) + 1)
    for which, _ in groups:
        sizes[which] += 1
    wides, chips, _, unit = units.shape
    _, block, model_width = rows.shape
    height, columns = 4 * block, 2 * width
    like = jax.ShapeDtypeStruct
    row_sems = [dma(2), dma(2), dma(2), dma(2), dma(1)]
    out = pl.pallas_call(
        functools.partial(weights_kernel, groups=groups, wides=wides, tokens=tokens),
        out_shape=[like((slabs, 4, 2, depth, columns), BF) for slabs in sizes]
        + [
            like((2, chips, 2, depth, 4 * unit), BF),
            like((wides - 2, chips, 2, depth, 4 * unit), BF),
            like((height, model_width), BF),
            like((3, height, columns), BF),
            like((height, columns), BF),
            like((height, model_width), F32),
            like((height, model_width), BF),
            like((height, columns), BF),
            like((2, cond.shape[0], columns), BF),
            like((height, columns), BF),
            like((2, block, model_width), F32),
            like((4, 2, block, model_width), BF),
            like((4, block, model_width), BF),
            like((4, block, model_width), BF),
            like((4, 2, block, model_width), BF),
            like((height, 128), F32),
            like((2, *cond.shape), BF),
        ],
        in_specs=near_specs(7),
        out_specs=any_specs(len(sizes) + 2) + near_specs(15),
        scratch_shapes=[
            pltpu.VMEM((2, 4, 2, depth, columns), BF),
            pltpu.VMEM((2, height, model_width), BF),
            pltpu.VMEM((2, height, model_width), BF),
            pltpu.VMEM((2 * block, model_width), F32),
            pltpu.VMEM(units.shape, BF),
            pltpu.VMEM((2, *size.shape), size.dtype),
            dma(2),
            dma(2),
            dma(6),
            dma(6),
            dma(2),
            dma(count),
            dma(count),
            dma(count, 2, 2),
            dma(count, 2),
            dma(count, 2, 3),
            dma(count, 2, 3),
            dma(count),
            dma(wides, 4, 2),
            dma(wides, 4),
            dma(wides, 4),
            dma(wides, 4),
            dma(wides),
            *row_sems,
            *row_sems,
            dma(3),
            dma(3),
            dma(2),
            dma(2),
            dma(6),
            dma(6),
            dma(3),
        ],
        compiler_params=pltpu.CompilerParams(
            collective_id=2, has_side_effects=True, vmem_limit_bytes=60 << 20
        ),
        name="weights_moves",
    )(shard, units, rows, cot, size, cond, gains)
    weights = out[: len(sizes) + 2]
    return [
        whole.reshape(whole.shape[0], 8 * depth, whole.shape[-1]) for whole in weights
    ], out[len(sizes) + 2 :]


def third_kernel(
    part_ref,
    left_ref,
    right_ref,
    other_ref,
    last_ref,
    sum_ref,
    quarter_ref,
    got,
    far_x,
    far_y,
    made,
    theirs,
    turned,
    send_r,
    recv_r,
    send_w,
    recv_w,
    store,
):
    dp, plane, core, z = spot()
    sibling = (flip(dp, 1), z)
    xmate, ymate, _ = plane_mates(dp, z)
    greet([sibling, xmate, ymate])

    def rows(source, slot, mate):
        return push(source, got.at[slot], send_r.at[slot], recv_r.at[slot], mate)

    first = [
        rows(part_ref.at[3, 0], 0, xmate),
        rows(part_ref.at[3, 1], 1, ymate),
        rows(part_ref.at[1, 0], 2, xmate),
        rows(part_ref.at[2, 1], 3, ymate),
    ]
    for copy in first:
        copy.start()
    slabs, chips, _, depth, units = made.shape
    span = 2 * depth
    unit = units // 4
    tile = units // 3

    def products(source, pairs):
        def body(chip, carry):
            spots = pl.ds(pl.multiple_of(chip * span, 128), span)
            turned[...] = source[:, spots].T
            for slot, value in pairs:
                for step in range(3):
                    columns = slice(step * tile, (step + 1) * tile)
                    result = jnp.dot(turned[...], value[:, columns], preferred_element_type=F32)
                    made[slot, chip, :, :, columns] = result.astype(BF).reshape(2, depth, tile)
            return carry

        lax.fori_loop(0, chips, body, 0)

    def cross(slot):
        return push(
            made.at[slot, :, 1 - core],
            theirs.at[slot],
            send_w.at[slot],
            recv_w.at[slot],
            sibling,
        )

    def leave(slot, block):
        return pltpu.make_async_copy(
            made.at[slot, :, core, :, pl.ds(block * unit, unit)],
            quarter_ref.at[block, slot],
            store.at[slot, block],
        )

    def core_sums(slot):
        cross(slot).wait_recv()

        def body(chip, carry):
            made[slot, chip, core] = made[slot, chip, core] + theirs[slot, chip]
            return carry

        lax.fori_loop(0, chips, body, 0)
        for block in range(4):
            leave(slot, block).start()

    products(left_ref, [(0, right_ref.at[0]), (1, right_ref.at[1])])
    cross(0).start()
    cross(1).start()
    first[0].wait_recv()
    far_x[...] = (part_ref[2, 0].astype(F32) + got[0].astype(F32)).astype(BF)
    upper = rows(far_x, 4, ymate)
    upper.start()
    first[1].wait_recv()
    far_y[...] = (part_ref[1, 1].astype(F32) + got[1].astype(F32)).astype(BF)
    lower = rows(far_y, 5, xmate)
    lower.start()
    products(other_ref, [(2, last_ref)])
    cross(2).start()
    core_sums(0)
    core_sums(1)
    first[2].wait_recv()
    first[3].wait_recv()
    upper.wait_recv()
    sum_ref[0] = part_ref[0, 0].astype(F32) + got[2].astype(F32) + got[4].astype(F32)
    lower.wait_recv()
    sum_ref[1] = part_ref[0, 1].astype(F32) + got[3].astype(F32) + got[5].astype(F32)
    core_sums(2)
    for copy in first + [upper, lower]:
        copy.wait_send()
    for slot in range(slabs):
        cross(slot).wait_send()
        for block in range(4):
            leave(slot, block).wait()


def third_moves(part, left, right, other, last):
    _, _, height, width = part.shape
    tokens, units = last.shape
    depth, slabs = width // 8, right.shape[0] + 1
    return pl.pallas_call(
        third_kernel,
        out_shape=[
            jax.ShapeDtypeStruct((2, height, width), F32),
            jax.ShapeDtypeStruct((4, slabs, 4, depth, units // 4), BF),
        ],
        in_specs=near_specs(5),
        out_specs=near_specs(1) + any_specs(1),
        scratch_shapes=[
            pltpu.VMEM((6, height, width), BF),
            pltpu.VMEM((height, width), BF),
            pltpu.VMEM((height, width), BF),
            pltpu.VMEM((slabs, 4, 2, depth, units), BF),
            pltpu.VMEM((slabs, 4, depth, units), BF),
            pltpu.VMEM((2 * depth, tokens), BF),
            dma(6),
            dma(6),
            dma(slabs),
            dma(slabs),
            dma(slabs, 4),
        ],
        compiler_params=pltpu.CompilerParams(
            collective_id=4, has_side_effects=True, vmem_limit_bytes=60 << 20
        ),
        name="third_moves",
    )(part, left, right, other, last)


def turned_dot(source, chip, value):
    span = source.shape[1] // 4
    spots = pl.ds(pl.multiple_of(chip * span, 128), span)
    product = lax.dot_general(
        source[:, spots], value, (((0,), (0,)), ((), ())), preferred_element_type=F32
    )
    return product.astype(BF).reshape(2, span // 2, -1)


def norm_parts(value):
    centred = value - jnp.mean(value, axis=1, keepdims=True)
    inverse = lax.rsqrt(jnp.mean(centred * centred, axis=1, keepdims=True) + EPSILON)
    return centred * inverse, inverse


def norm_grad(grad_out, scaled, inverse, gain):
    grad_scaled = grad_out * gain
    centre = jnp.mean(grad_scaled, axis=1, keepdims=True)
    slope = jnp.mean(grad_scaled * scaled, axis=1, keepdims=True)
    return inverse * (grad_scaled - centre - scaled * slope)


def cross_kernel(*refs, tokens):
    (
        sums_ref,
        part_ref,
        after_ref,
        stream_ref,
        cot_ref,
        keep_ref,
        gain_ref,
        two_ref,
        query_ref,
        pair_ref,
        crossed_ref,
        mixed_ref,
        seq_ref,
        conds_ref,
        co_ref,
        cq_ref,
        cc_ref,
        so_ref,
    ) = refs[:18]
    slabs_ref, grad_mixed, moved_ref, scaled_ref, inverse_ref, out_ref, gain_out, cond_out = refs[18:26]
    held, grad, rounded, given, dquery, dpair, cond_mine, cond_got = refs[26:34]
    got, far_x, far_y, half_mine, half_got, part_out, part_in = refs[34:41]
    send_r, recv_r, send_e, recv_e, held_sem = refs[41:]
    dp, plane, core, z = spot()
    sibling = (flip(dp, 1), z)
    xmate, ymate, _ = plane_mates(dp, z)
    greet([sibling, xmate, ymate])
    _, block, model_width = after_ref.shape
    height = 4 * block
    half = height // 2
    tile = 256
    wide = query_ref.shape[1]

    def rows(source, slot, mate):
        return push(source, got.at[slot], send_r.at[slot], recv_r.at[slot], mate)

    first = [
        rows(part_ref.at[3, 0], 0, xmate),
        rows(part_ref.at[3, 1], 1, ymate),
        rows(part_ref.at[1, 0], 2, xmate),
        rows(part_ref.at[2, 1], 3, ymate),
    ]
    for copy in first:
        copy.start()

    def fetch(source, slot):
        return pltpu.make_async_copy(source, held.at[slot], held_sem.at[slot])

    fetch(co_ref, 0).start()
    fetch(cq_ref, 1).start()

    def exchange(slot, source, target):
        return push(source, target, send_e.at[slot], recv_e.at[slot], sibling)

    gain_three = jnp.zeros((1, model_width), F32)
    for j in range(2):
        scaled, inverse = norm_parts(after_ref[j])
        value = norm_grad(sums_ref[j], scaled, inverse, gain_ref[2:3])
        gain_three = gain_three + jnp.sum(sums_ref[j] * scaled, axis=0, keepdims=True)
        half_mine[j] = value.astype(BF)
        lines = pl.ds(pl.multiple_of((2 * core + j) * block, 8), block)
        grad[lines, :] = keep_ref[lines, :1] * cot_ref[2 * core + j].astype(F32) + value
    halves = exchange(0, half_mine, half_got)
    halves.start()
    for j in range(2):
        scaled, inverse = norm_parts(seq_ref[2 * core + j].astype(F32))
        scaled_ref[j] = scaled
        inverse_ref[j] = jnp.broadcast_to(inverse, inverse_ref.shape[1:])
    halves.wait()
    for j in range(2):
        lines = pl.ds(pl.multiple_of((2 * (1 - core) + j) * block, 8), block)
        value = keep_ref[lines, :1] * cot_ref[2 * (1 - core) + j].astype(F32)
        grad[lines, :] = value + half_got[j].astype(F32)

    def round_rows(i, carry):
        lines = pl.ds(pl.multiple_of(i * 32, 32), 32)
        rounded[lines, :] = (keep_ref[lines, :1] * grad[lines, :]).astype(BF)
        return carry

    def project(slot, target):
        def body(step, carry):
            lines = pl.ds(pl.multiple_of(step // 3 * half, 16), half)
            spots = pl.ds(pl.multiple_of(step % 3 * tile, tile), tile)
            weight = held[slot, :, :, :, spots].reshape(model_width, tile)
            value = jnp.dot(rounded[lines, :], weight, preferred_element_type=F32)
            target[lines, spots] = value.astype(BF)
            return carry

        lax.fori_loop(0, 6, body, 0)

    def slab_grad(index, source, value):
        def body(chip, carry):
            slabs_ref[index, chip // 2, chip % 2] = turned_dot(source, chip, value[...])
            return carry

        lax.fori_loop(0, 4, body, 0)

    fetch(co_ref, 0).wait()
    lax.fori_loop(0, height // 32, round_rows, 0)
    project(0, given)
    fetch(cc_ref, 0).start()

    def heads(pair, carry):
        lanes = pl.ds(pl.multiple_of(pair * 128, 128), 128)
        line = lax.broadcasted_iota(jnp.int32, (pair_ref.shape[1], 1), 0)
        grads = backward_pair(
            query_ref[:, lanes],
            pair_ref[0, :, lanes],
            pair_ref[1, :, lanes],
            given[:, lanes],
            line < tokens,
        )
        dquery[:, lanes] = grads[0]
        dpair[0, :, lanes] = grads[1]
        dpair[1, :, lanes] = grads[2]
        return carry

    lax.fori_loop(0, wide // 128, heads, 0)
    fetch(cq_ref, 1).wait()

    def back(step, carry):
        lines = pl.ds(pl.multiple_of(step // 4 * half, 16), half)
        chip = step % 4
        span = model_width // 4
        value = lax.dot_general(
            dquery[lines, :],
            held[1, chip].reshape(span, wide),
            (((1,), (1,)), ((), ())),
            preferred_element_type=F32,
        )
        part_out[lines, pl.ds(pl.multiple_of(chip * span, 128), span)] = value.astype(BF)
        return carry

    lax.fori_loop(0, 8, back, 0)
    parts = exchange(1, part_out, part_in)
    parts.start()
    fetch(so_ref, 1).start()
    fetch(cc_ref, 0).wait()

    part = held.shape[3] // 2
    total = None
    for which in range(2):
        lines = slice(which * part, (which + 1) * part)
        weight = held[0, :, :, lines, :].reshape(model_width // 2, wide)
        value = lax.dot_general(
            dpair[which], weight, (((1,), (1,)), ((), ())), preferred_element_type=F32
        )
        total = value if total is None else total + value
        product = lax.dot_general(
            conds_ref[z // 2], dpair[which], (((0,), (0,)), ((), ())), preferred_element_type=F32
        )
        slabs_ref[2, :, :, :, lines, :] = product.astype(BF).reshape(2, 2, 2, part, wide)
    cond_mine[...] = total.astype(BF)
    conds = exchange(2, cond_mine, cond_got)
    conds.start()
    slab_grad(0, rounded, crossed_ref)
    first[0].wait_recv()
    far_x[...] = (part_ref[2, 0].astype(F32) + got[0].astype(F32)).astype(BF)
    upper = rows(far_x, 4, ymate)
    upper.start()
    first[1].wait_recv()
    far_y[...] = (part_ref[1, 1].astype(F32) + got[1].astype(F32)).astype(BF)
    lower = rows(far_y, 5, xmate)
    lower.start()
    parts.wait()
    gain_row = lax.broadcasted_iota(jnp.int32, gain_out.shape, 0)
    gain_out[...] = jnp.where(gain_row == 2, gain_three, 0.0)

    def second_norm(i, carry):
        lines = pl.ds(pl.multiple_of(i * 32, 32), 32)
        scaled, inverse = norm_parts(stream_ref[lines, :])
        value = part_out[lines, :].astype(F32) + part_in[lines, :].astype(F32)
        total = grad[lines, :] + norm_grad(value, scaled, inverse, gain_ref[1:2])
        grad[lines, :] = total
        rounded[lines, :] = (keep_ref[lines, :1] * total).astype(BF)
        return carry + jnp.sum(value * scaled, axis=0, keepdims=True)

    gain_two = lax.fori_loop(0, height // 32, second_norm, jnp.zeros((1, model_width), F32))
    gain_out[...] = jnp.where(gain_row == 1, 0.5 * gain_two, gain_out[...])
    fetch(so_ref, 1).wait()
    project(1, grad_mixed)
    slab_grad(1, two_ref, dquery)
    slab_grad(3, rounded, mixed_ref)
    for j in range(2):
        lines = pl.ds(pl.multiple_of((2 * core + j) * block, 8), block)
        moved_ref[j] = grad[lines, :]
    conds.wait()
    cond_out[...] = (cond_mine[...].astype(F32) + cond_got[...].astype(F32)).astype(BF)
    first[2].wait_recv()
    first[3].wait_recv()
    for j, copy in enumerate([upper, lower]):
        copy.wait_recv()
        value = part_ref[0, j].astype(F32) + got[2 + j].astype(F32) + got[4 + j].astype(F32)
        lines = pl.ds(pl.multiple_of((2 * core + j) * block, 8), block)
        keep = keep_ref[lines, :1]
        out_ref[j] = (keep * (after_ref[j] + keep * value)).astype(BF)
    for copy in first + [upper, lower]:
        copy.wait_send()


def cross_moves(sums, part, after, stream, cot, keep, gains, two, query, pair, crossed, mixed, seq, conds, weights, tokens):
    _, block, model_width = after.shape
    height, wide = query.shape
    depth = model_width // 8
    like = jax.ShapeDtypeStruct
    slab = (4, 2, depth, wide)
    return pl.pallas_call(
        functools.partial(cross_kernel, tokens=tokens),
        out_shape=[
            like((4, 2, 2, 2, depth, wide), BF),
            like(query.shape, BF),
            like(after.shape, F32),
            like(after.shape, F32),
            like((2, block, 128), F32),
            like(after.shape, BF),
            like(gains.shape, F32),
            like((pair.shape[1], model_width // 2), BF),
        ],
        in_specs=near_specs(14) + any_specs(4),
        out_specs=near_specs(8),
        scratch_shapes=[
            pltpu.VMEM((2, *slab), BF),
            pltpu.VMEM((height, model_width), F32),
            pltpu.VMEM((height, model_width), BF),
            pltpu.VMEM(query.shape, BF),
            pltpu.VMEM(query.shape, BF),
            pltpu.VMEM(pair.shape, BF),
            pltpu.VMEM((pair.shape[1], model_width // 2), BF),
            pltpu.VMEM((pair.shape[1], model_width // 2), BF),
            pltpu.VMEM((6, block, model_width), BF),
            pltpu.VMEM((block, model_width), BF),
            pltpu.VMEM((block, model_width), BF),
            pltpu.VMEM(after.shape, BF),
            pltpu.VMEM(after.shape, BF),
            pltpu.VMEM((height, model_width), BF),
            pltpu.VMEM((height, model_width), BF),
            dma(6),
            dma(6),
            dma(3),
            dma(3),
            dma(2),
        ],
        compiler_params=pltpu.CompilerParams(
            collective_id=6, has_side_effects=True, vmem_limit_bytes=62 << 20
        ),
        name="cross_moves",
    )(
        sums,
        part,
        after,
        stream,
        cot,
        keep,
        gains,
        two,
        query,
        pair,
        crossed,
        mixed,
        seq,
        conds,
        *[weight.reshape(slab) for weight in weights],
    )


def backward_pair(queries, keys_in, values, grads, valid):
    lane = lax.broadcasted_iota(jnp.int32, (1, 2 * HD), 1)
    totals = [None, None, None]
    for side in range(2):
        only = jnp.where(lane // HD == side, 1.0, 0.0)
        picked = (queries.astype(F32) * (only * HD ** (-0.5))).astype(BF)
        given = (grads.astype(F32) * only).astype(BF)
        turned = (keys_in.astype(F32) * only).T.astype(BF)
        rows_rows = (((1,), (1,)), ((), ()))
        scores = lax.dot_general(keys_in, picked, rows_rows, preferred_element_type=F32)
        scores = jnp.where(valid, scores, NEGATIVE)
        exponent = jnp.exp(scores - jnp.max(scores, axis=0, keepdims=True))
        probs = exponent * (1.0 / jnp.sum(exponent, axis=0, keepdims=True))
        grad_probs = lax.dot_general(values, given, rows_rows, preferred_element_type=F32)
        inner = jnp.sum(probs * grad_probs, axis=0, keepdims=True)
        grad_scores = (probs * (grad_probs - inner)).astype(BF)
        new = (
            jnp.dot(turned, grad_scores, preferred_element_type=F32).T * HD ** (-0.5),
            jnp.dot(grad_scores, picked, preferred_element_type=F32),
            jnp.dot(probs.astype(BF), given, preferred_element_type=F32),
        )
        totals = [b if a is None else a + b for a, b in zip(totals, new, strict=True)]
    return [total.astype(BF) for total in totals]


def share_kernel(*refs, arrays):
    count = arrays + 3
    grads_ref, refs = refs[0], refs[1:]
    (
        qkv_ref,
        mixed_ref,
        valid_ref,
        turned_ref,
        whole_ref,
        stream_ref,
        scaled_ref,
        inverse_ref,
        factor_ref,
        first_ref,
        gain_in,
        cond_ref,
    ) = refs[:12]
    out_ref, back_ref, gain_out, cond_out = refs[12:16]
    one, got, two, line, gain_got, gain_ref, gain_sum, gain_line = refs[16:24]
    made, whole, thirds, part_out, part_in, part_own, rows_ref = refs[24:31]
    (
        load,
        send_x,
        recv_x,
        send_y,
        recv_y,
        send_z,
        recv_z,
        send_c,
        recv_c,
        send_r,
        recv_r,
        send_g,
        recv_g,
        send_h,
        recv_h,
        send_k,
        recv_k,
        local,
        extra,
    ) = refs[31:]
    dp, plane, core, z = spot()
    xbit, ybit = plane % 2, plane // 2
    sibling = (flip(dp, 1), z)
    xmate, ymate, _ = plane_mates(dp, z)
    plane_all = [(lax.rem(dp + step, 8), z) for step in range(1, 8)]
    greet(plane_all + column_mates(dp, z)[1:])
    home = z // 2 == core
    above, below = (dp, z + 1), (dp, z - 1)
    width = out_ref.shape[2]
    near = jnp.where(core == 0, jnp.where(z >= 1, 1, 0), jnp.where(z <= 2, 0, 1))
    mates = (xmate, ymate)

    def order(turn):
        return 1 - near if turn == 0 else near

    def columns(which):
        return pl.ds(pl.multiple_of(which * width, width), width)

    def strip(g, turn, bit):
        grid = grads_ref.at[g] if g < arrays else made.at[g - arrays]
        if turn == 0:
            return grid.at[:, bit, :, :, columns(order(turn))]
        return grid.at[bit, :, :, :, columns(order(turn))]

    bits = (xbit, ybit)

    def add_to(target, source):
        def body(part, carry):
            target[part] = target[part] + source[part]
            return carry

        lax.fori_loop(0, 2, body, 0)

    def step_one(g, turn):
        return push(
            strip(g, turn, 1 - bits[turn]), got.at[g, turn], send_x.at[g, turn], recv_x.at[g, turn], mates[turn]
        )

    def fetch(g, turn):
        return pltpu.make_async_copy(strip(g, turn, bits[turn]), one.at[g, turn], load.at[g, turn])

    def kept(g, turn, side):
        if g < arrays:
            return one.at[g, turn, side]
        grid = made.at[g - arrays]
        if turn == 0:
            return grid.at[side, xbit, :, :, columns(order(turn))]
        return grid.at[ybit, side, :, :, columns(order(turn))]

    def step_two(g, turn):
        return push(
            kept(g, turn, 1 - bits[1 - turn]),
            two.at[g, turn],
            send_y.at[g, turn],
            recv_y.at[g, turn],
            mates[1 - turn],
        )

    def after_one(g, turn):
        if g < arrays:
            fetch(g, turn).wait()
        step_one(g, turn).wait_recv()
        for side in range(2):
            add_to(kept(g, turn, side), got.at[g, turn, side])
        step_two(g, turn).start()

    def z_of(turn):
        return 2 * core + order(turn)

    def add_held(g, turn, source):
        add_to(kept(g, turn, bits[1 - turn]), source)

    def line_copy(g, turn, way, target):
        held = kept(g, turn, bits[1 - turn])
        which = order(turn)
        return push(held, line.at[g, which, way], send_z.at[g, turn], recv_z.at[g, which, way], target)

    def after_two(g, turn):
        step_two(g, turn).wait_recv()
        add_held(g, turn, two.at[g, turn])
        which, goal = order(turn), z_of(turn)

        @pl.when(jnp.logical_and(z > 0, z <= goal))
        def _():
            line_copy(g, turn, 0, above).wait_recv()
            add_held(g, turn, line.at[g, which, 0])

        @pl.when(jnp.logical_and(z < 3, z >= goal))
        def _():
            line_copy(g, turn, 1, below).wait_recv()
            add_held(g, turn, line.at[g, which, 1])

        @pl.when(z < goal)
        def _():
            line_copy(g, turn, 0, above).start()

        @pl.when(z > goal)
        def _():
            line_copy(g, turn, 1, below).start()

        @pl.when(z == goal)
        def _():
            held = kept(g, turn, bits[1 - turn])
            pltpu.make_async_copy(held.at[core], out_ref.at[g], local.at[g]).start()
            push(held.at[1 - core], out_ref.at[g], send_c.at[g], recv_c.at[g], sibling).start()

    for g in range(arrays):
        for turn in range(2):
            step_one(g, turn).start()
            fetch(g, turn).start()
    many = rows_ref.shape[0]

    def rows_leave(a):
        for j in range(2):
            stays = jnp.logical_and(home, 2 * core + j == z)

            @pl.when(stays)
            def _(j=j):
                pltpu.make_async_copy(
                    rows_ref.at[a, j], back_ref.at[a, z % 2], local.at[count + a]
                ).start()

            @pl.when(jnp.logical_not(stays))
            def _(j=j):
                target = (plane * 2 + z // 2, 2 * core + j)
                push(
                    rows_ref.at[a, j],
                    back_ref.at[a, z % 2],
                    send_r.at[a, j],
                    recv_r.at[a, z % 2],
                    target,
                ).start()

    rows_ref[0] = first_ref[...]
    rows_leave(0)

    @pl.when(home)
    def _():
        pltpu.make_async_copy(cond_ref, cond_out.at[z % 2], local.at[count + many]).start()
        for step in range(1, 4):
            target = (dp, lax.rem(z + step, 4))
            push(cond_ref, cond_out.at[z % 2], send_k.at[step], recv_k.at[z % 2], target).start()

    def heads(pair, carry):
        lanes = pl.ds(pl.multiple_of(pair * 128, 128), 128)
        grads = backward_pair(
            qkv_ref[0, :, lanes],
            qkv_ref[1, :, lanes],
            qkv_ref[2, :, lanes],
            mixed_ref[:, lanes],
            valid_ref[:, :1] > 0.0,
        )
        for i in range(3):
            thirds[i, :, lanes] = grads[i]
        return carry

    lax.fori_loop(0, qkv_ref.shape[2] // 128, heads, 0)

    def weight_grads(i):
        def body(chip, carry):
            made[i, chip // 2, chip % 2] = turned_dot(turned_ref, chip, thirds[i])
            return carry

        lax.fori_loop(0, 4, body, 0)
        for turn in range(2):
            step_one(arrays + i, turn).start()

    half = thirds.shape[1] // 2
    tile = 256

    def row_grads(side, put):
        rows = pl.ds(pl.multiple_of(side * half, 16), half)
        blocks = whole_ref.shape[1] // tile

        def fill(block, slot):
            spots = pl.ds(pl.multiple_of(block * tile, tile), tile)
            return pltpu.make_async_copy(whole_ref.at[:, spots, :], whole.at[slot], extra.at[slot])

        fill(0, 0).start()

        def body(block, carry):
            slot = block % 2

            @pl.when(block + 1 < blocks)
            def _():
                fill(block + 1, 1 - slot).start()

            fill(block, slot).wait()
            spots = pl.ds(pl.multiple_of(block * tile, tile), tile)
            total = None
            for i in range(3):
                value = lax.dot_general(
                    thirds[i, rows, :],
                    whole[slot, i],
                    (((1,), (1,)), ((), ())),
                    preferred_element_type=F32,
                )
                total = value if total is None else total + value
            put(spots, total)
            return carry

        lax.fori_loop(0, blocks, body, 0)

    def put_out(spots, value):
        for j in range(2):
            part_out[j, :, spots] = value[j * (half // 2) : (j + 1) * (half // 2)].astype(BF)

    def put_own(spots, value):
        for j in range(2):
            part_own[j, :, spots] = value[j * (half // 2) : (j + 1) * (half // 2)]

    def ones(g):
        after_one(g, 0)
        after_one(g, 1)

    def twos(g):
        after_two(g, 0)
        after_two(g, 1)

    ones(0)
    weight_grads(0)
    ones(1)
    twos(0)
    weight_grads(1)
    weight_grads(2)
    ones(2)
    twos(1)
    row_grads(1 - core, put_out)
    parts = push(part_out, part_in, extra.at[3], extra.at[4], sibling)
    parts.start()
    row_grads(core, put_own)
    parts.wait()
    gain_one = jnp.zeros((1, part_own.shape[2]), F32)
    for j in range(2):
        value = part_own[j] + part_in[j].astype(F32)
        scaled = scaled_ref[j]
        grad_scaled = value * factor_ref[:1]
        centre = jnp.mean(grad_scaled, axis=1, keepdims=True)
        slope = jnp.mean(grad_scaled * scaled, axis=1, keepdims=True)
        moved = inverse_ref[j, :, :1] * (grad_scaled - centre - scaled * slope)
        rows_ref[1, j] = (stream_ref[j] + moved).astype(BF)
        gain_one = gain_one + jnp.sum(value * scaled, axis=0, keepdims=True)
    rows_leave(1)
    line_of = lax.broadcasted_iota(jnp.int32, gain_ref.shape, 0)
    gain_ref[...] = gain_in[...] + jnp.where(line_of == 0, gain_one, 0.0)
    gains = []
    for step in range(1, 8):
        mate = lax.rem(dp + step, 8)
        gains.append(
            push(gain_ref, gain_got.at[8 - step], send_g.at[step], recv_g.at[8 - step], (mate, z))
        )
    for copy in gains:
        copy.start()
    ones(3)
    twos(2)
    ones(4)
    twos(3)
    for copy in gains:
        copy.wait()
    total = gain_ref[...]
    for step in range(1, 8):
        total = total + gain_got[step]
    gain_sum[...] = total
    sums = []
    for step in range(1, 4):
        target = (dp, lax.rem(z + step, 4))
        sums.append(push(gain_sum, gain_line.at[4 - step], send_h.at[step], recv_h.at[4 - step], target))
    for copy in sums:
        copy.start()
    ones(5)
    twos(4)
    ones(6)
    twos(5)
    twos(6)

    for copy in sums:
        copy.wait()
    total = gain_sum[...]
    for step in range(1, 4):
        total = total + gain_line[step]
    gain_out[...] = total
    for g in range(count):
        for turn in range(2):
            goal = z_of(turn)
            step_one(g, turn).wait_send()
            step_two(g, turn).wait_send()

            @pl.when(z != goal)
            def _(g=g, turn=turn):
                line_copy(g, turn, 0, above).wait_send()

        @pl.when(home)
        def _(g=g):
            pltpu.make_async_copy(out_ref.at[g], out_ref.at[g], local.at[g]).wait()
            push(out_ref.at[g], out_ref.at[g], send_c.at[g], recv_c.at[g], sibling).wait_send()

        @pl.when(jnp.logical_not(home))
        def _(g=g):
            push(out_ref.at[g], out_ref.at[g], send_c.at[g], recv_c.at[g], sibling).wait_recv()

    for a in range(many):
        for j in range(2):
            stays = jnp.logical_and(home, 2 * core + j == z)

            @pl.when(stays)
            def _(a=a, j=j):
                pltpu.make_async_copy(rows_ref.at[a, j], back_ref.at[a, z % 2], local.at[count + a]).wait()

            @pl.when(jnp.logical_not(stays))
            def _(a=a, j=j):
                push(rows_ref.at[a, j], back_ref.at[a, 0], send_r.at[a, j], recv_r.at[a, 0], sibling).wait_send()

            @pl.when(jnp.logical_not(jnp.logical_and(home, z % 2 == j)))
            def _(a=a, j=j):
                push(rows_ref.at[a, j], back_ref.at[a, j], send_r.at[a, j], recv_r.at[a, j], sibling).wait_recv()

    @pl.when(home)
    def _():
        pltpu.make_async_copy(cond_ref, cond_out.at[z % 2], local.at[count + many]).wait()
        for step in range(1, 4):
            push(cond_ref, cond_out.at[0], send_k.at[step], recv_k.at[0], sibling).wait_send()

    for s in range(2):

        @pl.when(z != 2 * core + s)
        def _(s=s):
            push(cond_ref, cond_out.at[s], send_k.at[1], recv_k.at[s], sibling).wait_recv()


def share_moves(grads, qkv, mixed, valid, turned, whole, stream, scaled, inverse, factor, output, gains, cond):
    arrays, depth, width = grads.shape[0], grads.shape[4], grads.shape[5] // 2
    count = arrays + 3
    many, parts, height, model_width = 2, *output.shape
    padded, columns = qkv.shape[1:]
    return pl.pallas_call(
        functools.partial(share_kernel, arrays=arrays),
        out_shape=[
            jax.ShapeDtypeStruct((count, depth, width), BF),
            jax.ShapeDtypeStruct((many, *output.shape), BF),
            jax.ShapeDtypeStruct(gains.shape, F32),
            jax.ShapeDtypeStruct((2, *cond.shape), BF),
        ],
        in_specs=any_specs(1) + near_specs(4) + any_specs(1) + near_specs(7),
        out_specs=near_specs(1) + any_specs(1) + near_specs(1) + any_specs(1),
        scratch_shapes=[
            pltpu.VMEM((arrays, 2, 2, 2, depth, width), BF),
            pltpu.VMEM((count, 2, 2, 2, depth, width), BF),
            pltpu.VMEM((count, 2, 2, depth, width), BF),
            pltpu.VMEM((count, 2, 2, 2, depth, width), BF),
            pltpu.VMEM((8, *gains.shape), F32),
            pltpu.VMEM(gains.shape, F32),
            pltpu.VMEM(gains.shape, F32),
            pltpu.VMEM((4, *gains.shape), F32),
            pltpu.VMEM((3, 2, 2, 2, depth, 2 * width), BF),
            pltpu.VMEM((2, 3, 256, 2 * width), BF),
            pltpu.VMEM(qkv.shape, BF),
            pltpu.VMEM(output.shape, BF),
            pltpu.VMEM(output.shape, BF),
            pltpu.VMEM(output.shape, F32),
            pltpu.VMEM((many, *output.shape), BF),
            dma(count, 2),
            dma(count, 2),
            dma(count, 2),
            dma(count, 2),
            dma(count, 2),
            dma(count, 2),
            dma(count, 2, 2),
            dma(count),
            dma(count),
            dma(many, 2),
            dma(many, 2),
            dma(8),
            dma(8),
            dma(4),
            dma(4),
            dma(4),
            dma(2),
            dma(count + many + 1),
            dma(5),
        ],
        compiler_params=pltpu.CompilerParams(
            collective_id=5, has_side_effects=True, vmem_limit_bytes=61 << 20
        ),
        name="share_moves",
    )(
        grads,
        qkv,
        mixed,
        valid,
        turned,
        whole,
        stream,
        scaled,
        inverse,
        factor,
        output,
        gains,
        cond,
    )


def chip_shards(
    inputs,
    context,
    lengths,
    cotangent,
    self_qkv,
    self_out,
    cross_query,
    cross_context,
    cross_out,
    gate_up,
    down_proj,
    norm_gains,
):
    dp, z = lax.axis_index("dp"), lax.axis_index("tensor")
    model_width = inputs.shape[-1]

    cc_depth = cross_context.shape[1]
    tokens = context.shape[1]
    narrow = jnp.concatenate(
        [
            self_qkv,
            self_out.T[None],
            cross_query[None],
            cross_context.reshape(1, 2 * cc_depth, -1),
            cross_out.T[None],
        ]
    ).astype(BF)
    depth, units = gate_up.shape[1], gate_up.shape[2]
    wide = jnp.concatenate([gate_up, down_proj.T[None]]).astype(BF)
    wide = jnp.moveaxis(wide.reshape(3, depth, 4, units // 4), 2, 1)
    room = -tokens % 16
    cond = jnp.pad(take(context, z % 2, 0), ((0, room), (0, 0)))
    weights, kept = weights_moves(
        narrow,
        wide,
        inputs,
        cotangent,
        jnp.broadcast_to(take(lengths, z % 2, 0), (8, 128)),
        cond,
        jnp.pad(norm_gains, ((0, 5), (0, 0))),
        ((0, 0), (0, 1), (0, 2), (1, 0), (2, 0), (3, 0), (4, 0)),
        tokens,
    )
    qkv_whole, so_whole, cq_whole, cc_whole, co_whole, gu_whole, down_whole = weights
    down_whole = down_whole[0]
    normed_one, qkv, mixed_one, stream, normed_two, cross_rows, cond_rows = kept[:7]
    mixed_two, after, rows_three, sequence, cot, grad_branch, row_keep, conds = kept[7:]
    rows_three = rows_three.reshape(-1, model_width)
    grad_branch = grad_branch.reshape(-1, model_width)
    gate_rows = jnp.einsum("td,kde->kte", rows_three, gu_whole, preferred_element_type=F32)
    sigmoid_gate = jax.nn.sigmoid(gate_rows[0])
    hidden = (gate_rows[0] * sigmoid_gate * gate_rows[1]).astype(BF)

    grad_hidden = jnp.einsum("td,df->tf", grad_branch, down_whole, preferred_element_type=F32)
    grad_gate = (
        grad_hidden * gate_rows[1] * sigmoid_gate * (1.0 + gate_rows[0] * (1.0 - sigmoid_gate))
    )
    grad_upper = grad_hidden * gate_rows[0] * sigmoid_gate
    grad_expand = jnp.stack([grad_gate, grad_upper]).astype(BF)
    partial_value = jnp.einsum("ktf,kdf->td", grad_expand, gu_whole, preferred_element_type=F32)
    sums, wide_grads = third_moves(
        partial_value.astype(BF).reshape(4, 2, -1, model_width),
        rows_three,
        grad_expand,
        grad_branch,
        hidden,
    )
    wide_grads = lax.psum_scatter(wide_grads, "tensor", scatter_dimension=0, tiled=False)
    branch = jnp.einsum("tf,df->td", hidden, down_whole, preferred_element_type=F32).astype(BF)

    grads, grad_mixed, moved, scaled_one, inverse_one, output, gains, conds_grad = cross_moves(
        sums,
        branch.reshape(4, 2, -1, model_width),
        after,
        stream,
        cot,
        row_keep,
        jnp.pad(norm_gains, ((0, 5), (0, 0))),
        normed_two,
        cross_rows,
        cond_rows,
        mixed_two,
        mixed_one,
        sequence,
        conds,
        [co_whole, cq_whole, cc_whole, so_whole],
        tokens,
    )
    shares, back, gains, conds = share_moves(
        grads,
        qkv,
        grad_mixed,
        row_keep,
        normed_one,
        qkv_whole,
        moved,
        scaled_one,
        inverse_one,
        jnp.broadcast_to(norm_gains[0], (8, model_width)),
        output,
        gains,
        conds_grad,
    )
    gains = lax.dynamic_slice_in_dim(gains[:3], dp * depth, depth, 1)
    shares = shares.astype(F32)
    wide_grads, back = lax.optimization_barrier((wide_grads, back))
    shared = lax.all_to_all(wide_grads, "dp", 1, 1, axis_index_groups=[[0, 2, 4, 6], [1, 3, 5, 7]])
    shared = jnp.moveaxis(shared, 1, 2).reshape(3, depth, units).astype(F32)
    return (
        back[0],
        back[1].astype(F32),
        conds[:, :tokens].astype(F32),
        shares[4:],
        shares[3].T,
        shares[1],
        shares[2].reshape(2, cc_depth, -1),
        shares[0].T,
        shared[:2],
        shared[2].T,
        gains,
    )


def solution(mesh):
    sizes = (mesh.shape["dp"], mesh.shape["tensor"])
    body = chip_shards if sizes == (8, 4) else shards
    placed = (
        P("dp", "tensor", None),
        P("dp", None, None),
        P("dp"),
        P("dp", "tensor", None),
        P(None, "dp", "tensor"),
        P("tensor", "dp"),
        P("dp", "tensor"),
        P(None, "dp", "tensor"),
        P("tensor", "dp"),
        P(None, "dp", "tensor"),
        P("tensor", "dp"),
        P(),
    )
    return jax.shard_map(
        body,
        mesh=mesh,
        in_specs=placed,
        out_specs=(
            P("dp", "tensor", None),
            P("dp", "tensor", None),
            P("dp", None, None),
            P(None, "dp", "tensor"),
            P("tensor", "dp"),
            P("dp", "tensor"),
            P(None, "dp", "tensor"),
            P("tensor", "dp"),
            P(None, "dp", "tensor"),
            P("tensor", "dp"),
            P(None, "dp"),
        ),
        check_vma=False,
    )
```
